32 devices in a mesh: gx: 4 (over z), gy: 8 (over y, x, core).
Axes of the slice: x: 2, y: 2, z: 4, core: 2. Of those that a mesh axis runs over, the one named last changes fastest.
Arguments:
- populations_in: float32 [19, 4, 128, 3072], P(None, None, 'gx', 'gy'), may hold values from 0.02 to 0.1
- marker_force: float32 [2, 3, 16384], P(None, None, ('gx', 'gy')), may hold values from -1.2 to 1.2
- marker_frac: float32 [2, 3, 16384], P(None, None, ('gx', 'gy')), may hold values from 0 to 1
- marker_cell: int32 [2, 3, 16384], P(None, None, ('gx', 'gy')), may hold values from 0 to 382, as said below
- marker_tile: int32 [2, 16384, 1], P(None, ('gx', 'gy')), may hold values from 0 to 31; in each aligned block of 512 rows (0 to 511, 512 to 1023, ..., all dimensions but the last counted through in order) at most 32 rows name the same one
Outputs:
- populations_out: float32 [19, 4, 128, 3072], P(None, None, 'gx', 'gy')
- marker_velocity: float32 [2, 3, 16384], P(None, None, ('gx', 'gy'))
The draws below stay inside these ranges and needn't reach their ends.
Inputs may be any that keep to these rules, and one draw needn't show every extreme that they name: `marker_cell`: row 0 lies below 31, row 1 below 383, row 2 below 3, so that a marker's 2 x 2 x 2 kernel stays inside the tile that marker_tile names. `marker_tile`: in each step, of the 512 markers that one device holds at most 32 name the same tile.
All inputs are finite; a program needn't handle non-finite values.
Results may differ from the reference program's by a relative error of at most 0.0003.
Values sent between devices are 32-bit elements; how exact they have to be, the bound alone decides.
No kernel may reach another device: no remote copies, remote signals or barrier semaphores. Data moves between devices by JAX's collectives and lax.ppermute only.
A program may use at most 128 MiB of HBM per device.

```python
import math
import jax
import jax.numpy as jnp
import numpy as np

VELOCITIES = 19
PLANES = 4
STEPS = 2
CX = 32
CY = 384
MK_DEV = 512
MARKERS = 16384
CAP = 32
NX = 128
NY = 3072
N_GY = 8
DEVICES = 32


def draw_marker_cell(key, part):
    upper = jnp.array([CX - 1, CY - 1, PLANES - 1], jnp.int32)
    return jax.random.randint(key, (STEPS, 3, MARKERS), 0, upper[None, :, None]).astype(jnp.int32)


def block_scale(rng, dims, shards, least, high):
    factor_of, own = 1.0, jax.random.fold_in(rng, 6)
    for position, blocks in shards:
        draws = jnp.exp(jax.random.uniform(jax.random.fold_in(own, position), (blocks,), jnp.float32, least / len(shards), high / len(shards)))
        factor_of = factor_of * jnp.repeat(draws, dims[position] // blocks).reshape([-1 if axis == position else 1 for axis in range(len(dims))])
    return factor_of


def assign_block(rng, own, number, rows, count, top, most, skew):
    sequence = jax.random.permutation(rng, count)
    crowded, ordinary = shares(count, rows * top, most, skew, True), shares(count, rows * top, most, skew, False)
    places = jnp.arange(count)

    def named(sizes, offset_by):
        used = int((sizes > 0).sum())
        fixed = max(1, used // 4)
        passed = fixed + (places - fixed + offset_by * (used - fixed)) % max(1, count - fixed)
        return jnp.zeros((count,), jnp.int32).at[sequence[jnp.where(places < fixed, places, passed)]].set(jnp.asarray(sizes, jnp.int32))

    sizes = jnp.where(number % 4 == 0, named(crowded, number // 4), named(ordinary, number - number // 4 - 1))
    mixed = jax.random.permutation(jax.random.fold_in(own, 3), count)
    source_of, sink = mixed[0:count // 2 * 2:2], mixed[1:count // 2 * 2:2]
    margin = jnp.minimum(sizes[source_of] - 1, most - sizes[sink]) // 2
    margin = jnp.where((source_of == sequence[0]) | (sink == sequence[0]) | (sizes[sink] == 0), 0, jnp.maximum(margin, 0))
    passed = jax.random.randint(jax.random.fold_in(own, 4), (count // 2,), 0, 1 << 20) % (margin + 1)
    sizes = sizes.at[source_of].add(-passed).at[sink].add(passed)
    members = jnp.searchsorted(jnp.cumsum(sizes), jnp.arange(rows * top), side="right").astype(jnp.int32)
    table = members.reshape(top, rows).T
    table = table[jax.random.permutation(jax.random.fold_in(own, 1), rows)]
    offset_by = jax.random.randint(jax.random.fold_in(own, 2), (rows, 1), 0, top)
    return jnp.take_along_axis(table, (jnp.arange(top)[None, :] + offset_by) % top, axis=1)


def shares(number_of, total, reach, slope, full):
    weights = [(1 << 20) // math.isqrt(rank ** slope) + 1 for rank in range(1, number_of + 1)]
    largest = reach if full else min(reach, max(-(-total // number_of), total * weights[0] // sum(weights)))
    least = 1 if total - largest >= number_of - 1 else 0
    holding, surplus = [largest] + [least] * (number_of - 1), total - largest - least * (number_of - 1)
    while surplus > 0:
        candidates = [i for i in range(1, number_of) if holding[i] < largest] or [i for i in range(1, number_of) if holding[i] < reach]
        pool, budget = sum([weights[i] for i in candidates]), surplus
        for i in candidates:
            more = min(reach - holding[i], max(1, budget * weights[i] // pool), surplus)
            holding[i] = holding[i] + more
            surplus = surplus - more
    return np.array(holding)


def bell_draw(stream_key, shape, deviation, bound, cuts=(), kind=jnp.bfloat16):
    values = jax.random.normal(stream_key, shape, jnp.float32) * deviation
    if len(cuts) > 0:
        values = block_scale(stream_key, shape, cuts, -0.22, 0.18) * values
    return jnp.clip(values, min=-bound, max=bound).astype(kind)


def setup_inputs(seed: int = 0) -> dict:
    streams_of = jax.random.split(jax.random.key(seed), 6)
    populations_in = jnp.clip(0.02 + 0.08 * jax.random.uniform(streams_of[0], (VELOCITIES, PLANES, NX, NY), jnp.float32) ** block_scale(streams_of[0], (VELOCITIES, PLANES, NX, NY), ((2, 4), (3, 8)), -0.2, 0.2), 0.02, 0.1)
    marker_force = bell_draw(streams_of[1], (STEPS, 3, MARKERS), 0.2, 1.2, ((2, 32),), jnp.float32)
    marker_frac = jnp.clip(1.0 * jax.random.uniform(streams_of[2], (STEPS, 3, MARKERS), jnp.float32) ** block_scale(streams_of[2], (STEPS, 3, MARKERS), ((2, 32),), -0.2, 0.2), 0.0, 1.0)
    marker_cell = draw_marker_cell(jax.random.fold_in(streams_of[5], 71), 0)
    marker_tile_keys = jax.random.split(jax.random.fold_in(streams_of[4], 1), STEPS * MARKERS // MK_DEV)
    marker_tile_turns = jax.random.permutation(jax.random.fold_in(streams_of[4], 3), STEPS * MARKERS // MK_DEV)
    marker_tile = jax.vmap(lambda own, number: assign_block(jax.random.fold_in(streams_of[4], 2), own, number, MK_DEV, DEVICES, 1, CAP, 2))(marker_tile_keys, marker_tile_turns).reshape((STEPS, MARKERS, 1))
    return {"populations_in": populations_in, "marker_force": marker_force, "marker_frac": marker_frac, "marker_cell": marker_cell, "marker_tile": marker_tile}


LATTICE = [(0, 0, 0), (1, 0, 0), (-1, 0, 0), (0, 1, 0), (0, -1, 0), (0, 0, 1), (0, 0, -1),
           (1, 1, 0), (-1, -1, 0), (1, -1, 0), (-1, 1, 0), (1, 0, 1), (-1, 0, -1),
           (1, 0, -1), (-1, 0, 1), (0, 1, 1), (0, -1, -1), (0, 1, -1), (0, -1, 1)]
WEIGHTS = [1.0 / 3.0] + [1.0 / 18.0] * 6 + [1.0 / 36.0] * 12
relax_time = 0.8


def lattice_dot(vector, comps, like):
    total = jnp.zeros_like(like)
    for number in range(3):
        if vector[number] == 1:
            total = total + comps[number]
        elif vector[number] == -1:
            total = total - comps[number]
    return total


def moments(fields):
    density = fields[0]
    for member in range(1, 19):
        density = density + fields[member]
    momenta = []
    for number in range(3):
        total = jnp.zeros_like(density)
        for member in range(19):
            if LATTICE[member][number] == 1:
                total = total + fields[member]
            elif LATTICE[member][number] == -1:
                total = total - fields[member]
        momenta.append(total)
    return density, momenta


def velocity_of(fields, force):
    density, momenta = moments(fields)
    return [(momenta[number] + 0.5 * force[number]) / density for number in range(3)]


def collide(fields, force):
    density, momenta = moments(fields)
    speed = [(momenta[number] + 0.5 * force[number]) / density for number in range(3)]
    speed_sq = speed[0] * speed[0] + speed[1] * speed[1] + speed[2] * speed[2]
    along_force = speed[0] * force[0] + speed[1] * force[1] + speed[2] * force[2]
    posts = []
    for member in range(19):
        vector = LATTICE[member]
        project = lattice_dot(vector, speed, density)
        cforce = lattice_dot(vector, force, density)
        equilib = WEIGHTS[member] * density * (1.0 + 3.0 * project + 4.5 * project * project - 1.5 * speed_sq)
        source = (1.0 - 0.5 / relax_time) * WEIGHTS[member] * (3.0 * (cforce - along_force) + 9.0 * project * cforce)
        posts.append(fields[member] - (fields[member] - equilib) / relax_time + source)
    return posts


def reference(populations_in, marker_force, marker_frac, marker_cell, marker_tile):
    fields = [populations_in[member] for member in range(19)]
    outputs = []
    for step in range(STEPS):
        tiles = marker_tile[step, :, 0]
        base_x = (tiles // N_GY) * CX + marker_cell[step, 0]
        base_y = (tiles % N_GY) * CY + marker_cell[step, 1]
        base_z = marker_cell[step, 2]
        frac = marker_frac[step]
        force = marker_force[step]
        corners = []
        for shift_z in range(2):
            weight_z = frac[2] if shift_z else 1.0 - frac[2]
            for shift_x in range(2):
                weight_x = frac[0] if shift_x else 1.0 - frac[0]
                for shift_y in range(2):
                    weight_y = frac[1] if shift_y else 1.0 - frac[1]
                    flat = ((base_z + shift_z) * NX + base_x + shift_x) * NY + base_y + shift_y
                    corners.append((flat.astype(jnp.int32), weight_z * weight_x * weight_y))
        field = jnp.zeros((3, PLANES * NX * NY), jnp.float32)
        for flat, weight in corners:
            field = field.at[:, flat].add(weight[None, :] * force)
        force_field = field.reshape(3, PLANES, NX, NY)
        posts = collide(fields, force_field)
        fields = [jnp.roll(posts[member], (LATTICE[member][2], LATTICE[member][0], LATTICE[member][1]), axis=(0, 1, 2))
                  for member in range(19)]
        probe = jnp.stack(velocity_of(fields, force_field)).reshape(3, -1)
        sampled = jnp.zeros((3, MARKERS), jnp.float32)
        for flat, weight in corners:
            sampled = sampled + weight[None, :] * probe[:, flat]
        outputs.append(sampled)
    return jnp.stack(fields), jnp.stack(outputs)
```

```python
import jax
import jax.numpy as jnp
from jax import lax
from jax.experimental import pallas as pl
from jax.experimental.pallas import tpu as pltpu
from jax.sharding import PartitionSpec as P

LATTICE = [
    (0, 0, 0),
    (1, 0, 0),
    (-1, 0, 0),
    (0, 1, 0),
    (0, -1, 0),
    (0, 0, 1),
    (0, 0, -1),
    (1, 1, 0),
    (-1, -1, 0),
    (1, -1, 0),
    (-1, 1, 0),
    (1, 0, 1),
    (-1, 0, -1),
    (1, 0, -1),
    (-1, 0, 1),
    (0, 1, 1),
    (0, -1, -1),
    (0, 1, -1),
    (0, -1, 1),
]
WEIGHTS = [1.0 / 3.0] + [1.0 / 18.0] * 6 + [1.0 / 36.0] * 12
relax_time = 0.8
OMEGA = 1.0 / relax_time
SOURCE = 1.0 - 0.5 / relax_time
LANES = 128

X_UP = [i for i in range(19) if LATTICE[i][0] == 1]
X_DOWN = [i for i in range(19) if LATTICE[i][0] == -1]
Y_UP = [i for i in range(19) if LATTICE[i][1] == 1]
Y_DOWN = [i for i in range(19) if LATTICE[i][1] == -1]

BF = jnp.bfloat16
F32 = jnp.float32


def split2(x):
    high = x.astype(BF)
    low = (x - high.astype(F32)).astype(BF)
    return high, low


def split3(x):
    high = x.astype(BF)
    rest = x - high.astype(F32)
    middle = rest.astype(BF)
    low = (rest - middle.astype(F32)).astype(BF)
    return high, middle, low


def nt(a, b):
    return lax.dot_general(a, b, (((1,), (1,)), ((), ())), preferred_element_type=F32)


def nn(a, b):
    return lax.dot_general(a, b, (((1,), (0,)), ((), ())), preferred_element_type=F32)


def iota(shape, dim):
    return lax.broadcasted_iota(jnp.int32, shape, dim)


def slot_table(slot, slots):
    owned = slot.shape[1]
    return jnp.where(iota((slots, owned), 0) == slot, 1.0, 0.0).astype(BF)


def pack_kernel(devices, cap, steps, tile_ref, cell_ref, frac_ref, force_ref, out_ref, slot_ref, rows):
    owned = cell_ref.shape[2]
    slots = devices * cap
    lines = owned // LANES
    earlier = jnp.where(iota((owned, owned), 0) < iota((owned, owned), 1), 1.0, 0.0).astype(BF)
    octets = []
    for step in range(steps):
        tiles = jnp.concatenate(
            [tile_ref[step * lines + r : step * lines + r + 1, :] for r in range(lines)], axis=1
        )
        member = jnp.where(iota((devices, owned), 0) == tiles, 1.0, 0.0)
        rank = jnp.sum(nn(member.astype(BF), earlier) * member, axis=0, keepdims=True)
        slot = tiles * cap + rank.astype(jnp.int32)
        slot_ref[step : step + 1, :] = slot
        rows[...] = jnp.zeros_like(rows)
        for number in range(3):
            rows[number : number + 1, :] = cell_ref[number, step : step + 1, :].astype(F32)
            rows[3 + number : 4 + number, :] = frac_ref[number, step : step + 1, :]
            rows[6 + number : 7 + number, :] = force_ref[number, step : step + 1, :]
        parts = jnp.concatenate(split3(rows[...]), axis=0)
        packed = nt(parts, slot_table(slot, slots))
        packed = packed[0:16] + packed[16:32] + packed[32:48]
        octets += [packed[0:8], packed[8:16]]
    group = iota((8, LANES), 1) // cap
    per = LANES // cap
    for device in range(devices):
        line, place = device // per, device % per
        block = jnp.zeros((8, LANES), F32)
        for number, octet in enumerate(octets):
            piece = octet[:, line * LANES : (line + 1) * LANES]
            shift = (number - place) * cap % LANES
            if shift:
                piece = pltpu.roll(piece, shift, 1)
            block = jnp.where(group == number, piece, block)
        out_ref[device] = block


def gather_octet(recv_ref, cap, number):
    devices = recv_ref.shape[0]
    per = LANES // cap
    group = iota((8, LANES), 1) // cap
    pieces = []
    for line in range(devices // per):
        total = jnp.zeros((8, LANES), F32)
        for place in range(per):
            piece = recv_ref[line * per + place]
            shift = (place - number) * cap % LANES
            if shift:
                piece = pltpu.roll(piece, shift, 1)
            total = jnp.where(group == place, piece, total)
        pieces.append(total)
    return jnp.concatenate(pieces, axis=1)


def unpack_kernel(cap, steps, recv_ref, slot_ref, out_ref):
    rows = gather_octet(recv_ref, cap, 0)
    slots = rows.shape[1]
    parts = jnp.concatenate(split3(jnp.concatenate([rows, rows], axis=0)), axis=0)
    for step in range(steps):
        found = nn(parts, slot_table(slot_ref[step : step + 1, :], slots))
        found = found[0:8] + found[16:24] + found[32:40]
        for number in range(3):
            out_ref[number, step : step + 1, :] = found[step * 3 + number : step * 3 + number + 1]


def line_weights(cell, frac, extent):
    grid = iota((extent, cell.shape[1]), 0).astype(F32)
    return jnp.where(grid == cell, 1.0 - frac, jnp.where(grid == cell + 1.0, frac, 0.0))


def y_table(cell, frac, extent):
    grid = iota((extent, cell.shape[1]), 0).astype(F32)
    lower, upper = grid == cell, grid == cell + 1.0
    tables = []
    for low, high in zip(split2(1.0 - frac), split2(frac)):
        low, high = low.astype(F32), high.astype(F32)
        tables.append(jnp.where(lower, low, jnp.where(upper, high, 0.0)).astype(BF))
    return tables


def plane_table(rows, planes, width_x):
    kernel_x = line_weights(rows[0:1], rows[3:4], width_x)
    kernel_z = line_weights(rows[2:3], rows[5:6], 8)
    return [kernel_z[z : z + 1] * kernel_x for z in range(planes)]


def spread(first, second, planes, width_x, width_y, force_ref):
    table = jnp.concatenate(plane_table(first, planes, width_x), axis=0)
    along_y = y_table(first[1:2], first[4:5], width_y)
    size = planes * width_x
    for number, strength in enumerate((first[6:7], first[7:8], second[0:1])):
        high, low = split2(table * strength)
        force_ref[number * size : (number + 1) * size, :] = (
            nt(high, along_y[0]) + nt(high, along_y[1]) + nt(low, along_y[0])
        )


def sample(first, planes, width_x, width_y, probe_ref):
    table = jnp.concatenate(plane_table(first, planes, width_x), axis=0)
    along_y = y_table(first[1:2], first[4:5], width_y)
    size = planes * width_x
    rows = []
    for number in range(3):
        high, low = split2(probe_ref[number * size : (number + 1) * size, :])
        found = nn(high, along_y[0]) + nn(high, along_y[1]) + nn(low, along_y[0])
        rows.append(jnp.sum(found * table, axis=0, keepdims=True))
    return rows


def moments(f):
    density = f[0]
    diff = {}
    for member in range(1, 19, 2):
        density = density + (f[member] + f[member + 1])
        diff[member] = f[member] - f[member + 1]
    momenta = []
    for number in range(3):
        total = None
        for member in range(1, 19, 2):
            sign = LATTICE[member][number]
            if sign == 0:
                continue
            if total is None:
                total = diff[member] if sign == 1 else -diff[member]
            else:
                total = total + diff[member] if sign == 1 else total - diff[member]
        momenta.append(total)
    return density, momenta


def dot_c(vector, comps):
    total = None
    for number in range(3):
        if vector[number] == 0:
            continue
        if total is None:
            total = comps[number] if vector[number] == 1 else -comps[number]
        else:
            total = total + comps[number] if vector[number] == 1 else total - comps[number]
    return total


def collide(f, density, momenta, force):
    inverse = 1.0 / density
    speed = [(momenta[n] + 0.5 * force[n]) * inverse for n in range(3)]
    scaled = OMEGA * density
    speed_sq = speed[0] * speed[0] + speed[1] * speed[1] + speed[2] * speed[2]
    along = speed[0] * force[0] + speed[1] * force[1] + speed[2] * force[2]
    base = scaled * (1.0 - 1.5 * speed_sq) - (3.0 * SOURCE) * along
    flow = [scaled * speed[n] for n in range(3)]
    pull = [(3.0 * SOURCE) * force[n] for n in range(3)]
    linear = [3.0 * flow[n] + pull[n] for n in range(3)]
    square = [4.5 * flow[n] + 3.0 * pull[n] for n in range(3)]
    posts = [(1.0 - OMEGA) * f[0] + WEIGHTS[0] * base]
    for member in range(1, 19, 2):
        vector = LATTICE[member]
        even = WEIGHTS[member] * (base + dot_c(vector, speed) * dot_c(vector, square))
        odd = WEIGHTS[member] * dot_c(vector, linear)
        posts.append((1.0 - OMEGA) * f[member] + (even + odd))
        posts.append((1.0 - OMEGA) * f[member + 1] + (even - odd))
    return posts


def send_faces(post_ref, x_up, x_down, y_up, y_down):
    planes, width_x, width_y = post_ref.shape[1], post_ref.shape[2], post_ref.shape[3]
    for out, members, row in ((x_up, X_UP, width_x - 1), (x_down, X_DOWN, 0)):
        out[...] = jnp.zeros_like(out)
        for place, member in enumerate(members):
            for z in range(planes):
                number = place * planes + z
                out[number : number + 1, :] = post_ref[member, z, row : row + 1, :]
    lane = iota((width_x, LANES), 1)
    count = 5 * planes
    for out, members, start, at in ((y_up, Y_UP, width_y - LANES, LANES - 1), (y_down, Y_DOWN, 0, 0)):
        total = jnp.zeros((width_x, LANES), F32)
        for place, member in enumerate(members):
            for z in range(planes):
                number = place * planes + z
                block = post_ref[member, z, :, start : start + LANES]
                if LATTICE[member][0]:
                    block = pltpu.roll(block, LATTICE[member][0] % width_x, 0)
                if (number - at) % LANES:
                    block = pltpu.roll(block, (number - at) % LANES, 1)
                total = jnp.where(lane == number, block, total)
        packed = jnp.zeros((8, LANES), F32)
        group = iota((8, LANES), 1) // count
        for number in range(width_x // 8):
            piece = total[number * 8 : number * 8 + 8]
            if number:
                piece = pltpu.roll(piece, number * count, 1)
            packed = jnp.where(group == number, piece, packed)
        out[...] = packed


def corner_kernel(planes, width_x, y_up, y_down, x_low, x_high, out_up, out_down):
    count = 5 * planes
    width_y = x_low.shape[1]
    lane, row = iota((8, LANES), 1), iota((8, LANES), 0)
    for source, out, members, start, at in (
        (y_up, out_up, Y_UP, width_y - LANES, LANES - 1),
        (y_down, out_down, Y_DOWN, 0, 0),
    ):
        block = source[...]
        for place, member in enumerate(members):
            along = LATTICE[member][0]
            if along == 0:
                continue
            halo, order = (x_low, X_UP) if along == 1 else (x_high, X_DOWN)
            group, sub = (0, 0) if along == 1 else (width_x // 8 - 1, 7)
            for z in range(planes):
                number = order.index(member) * planes + z
                target = group * count + place * planes + z
                piece = jnp.broadcast_to(halo[number : number + 1, start : start + LANES], (8, LANES))
                if (target - at) % LANES:
                    piece = pltpu.roll(piece, (target - at) % LANES, 1)
                block = jnp.where((lane == target) & (row == sub), piece, block)
        out[...] = block


def stream(post_ref, x_low, x_high, y_low, y_high, out_ref):
    planes, width_x, width_y = post_ref.shape[1], post_ref.shape[2], post_ref.shape[3]
    count = 5 * planes
    rows = iota((width_x, width_y), 0)
    lane = iota((width_x, LANES), 1)
    low, high = y_low[...], y_high[...]
    for member in range(19):
        along_x, along_y, along_z = LATTICE[member]
        for z in range(planes):
            block = post_ref[member, z]
            if along_x == 1:
                number = X_UP.index(member) * planes + z
                block = jnp.where(rows == 0, x_low[number : number + 1, :], pltpu.roll(block, 1, 0))
            elif along_x == -1:
                number = X_DOWN.index(member) * planes + z
                block = jnp.where(
                    rows == width_x - 1,
                    x_high[number : number + 1, :],
                    pltpu.roll(block, width_x - 1, 0),
                )
            to = (z + along_z) % planes
            if along_y == 0:
                out_ref[member, to] = block
                continue
            halo, order, at = (low, Y_UP, 0) if along_y == 1 else (high, Y_DOWN, LANES - 1)
            number = order.index(member) * planes + z
            edge = []
            for group in range(width_x // 8):
                shift = (at - group * count - number) % LANES
                edge.append(pltpu.roll(halo, shift, 1) if shift else halo)
            edge = jnp.concatenate(edge, axis=0)
            block = pltpu.roll(block, along_y % width_y, 1)
            start = 0 if along_y == 1 else width_y - LANES
            first = jnp.where(lane == at, edge, block[:, start : start + LANES])
            if along_y == 1:
                block = jnp.concatenate([first, block[:, LANES:]], axis=1)
            else:
                block = jnp.concatenate([block[:, :start], first], axis=1)
            out_ref[member, to] = block


def blocks(planes, width_x, width_y, body):
    per = width_x // 8

    @pl.loop(0, planes * per)
    def _(index):
        z = index // per
        row = pl.multiple_of((index % per) * 8, 8)
        flat = pl.multiple_of(index * 8, 8)
        for start in range(0, width_y, LANES):
            body(z, pl.ds(row, 8), flat, pl.ds(start, LANES))


def spread_kernel(cap, step, planes, width_x, recv_ref, force_ref):
    first = gather_octet(recv_ref, cap, 2 * step)
    second = gather_octet(recv_ref, cap, 2 * step + 1)
    spread(first, second, planes, width_x, force_ref.shape[1], force_ref)


def first_kernel(cap, recv_ref, f_ref, force_ref, post_ref, x_up, x_down, y_up, y_down):
    planes, width_x, width_y = f_ref.shape[1], f_ref.shape[2], f_ref.shape[3]
    spread_kernel(cap, 0, planes, width_x, recv_ref, force_ref)
    size = planes * width_x

    def body(z, row, flat, lanes):
        f = [f_ref[member, z, row, lanes] for member in range(19)]
        force = [force_ref[pl.ds(number * size + flat, 8), lanes] for number in range(3)]
        density, momenta = moments(f)
        for member, value in enumerate(collide(f, density, momenta, force)):
            post_ref[member, z, row, lanes] = value

    blocks(planes, width_x, width_y, body)
    send_faces(post_ref, x_up, x_down, y_up, y_down)


def middle_kernel(
    post_in, x_low, x_high, y_low, y_high, force_ref, next_ref, probe_ref, post_ref, x_up, x_down, y_up, y_down, f_ref
):
    planes, width_x, width_y = post_in.shape[1], post_in.shape[2], post_in.shape[3]
    size = planes * width_x
    stream(post_in, x_low, x_high, y_low, y_high, f_ref)

    def body(z, row, flat, lanes):
        f = [f_ref[member, z, row, lanes] for member in range(19)]
        density, momenta = moments(f)
        inverse = 1.0 / density
        force = []
        for number in range(3):
            at = pl.ds(number * size + flat, 8)
            probe_ref[at, lanes] = (momenta[number] + 0.5 * force_ref[at, lanes]) * inverse
            force.append(next_ref[at, lanes])
        for member, value in enumerate(collide(f, density, momenta, force)):
            post_ref[member, z, row, lanes] = value

    blocks(planes, width_x, width_y, body)
    send_faces(post_ref, x_up, x_down, y_up, y_down)


def sample_kernel(cap, step, planes, width_x, recv_ref, probe_ref, out_ref):
    first = gather_octet(recv_ref, cap, 2 * step)
    out_ref[...] = jnp.zeros_like(out_ref)
    for number, row in enumerate(sample(first, planes, width_x, probe_ref.shape[1], probe_ref)):
        out_ref[number : number + 1, :] = row


def last_kernel(
    cap, step, post_in, x_low, x_high, y_low, y_high, force_ref, recv_ref, sampled_ref, f_ref, out_ref, probe_ref, rows
):
    planes, width_x, width_y = post_in.shape[1], post_in.shape[2], post_in.shape[3]
    size = planes * width_x
    stream(post_in, x_low, x_high, y_low, y_high, f_ref)

    def body(z, row, flat, lanes):
        f = [f_ref[member, z, row, lanes] for member in range(19)]
        density, momenta = moments(f)
        inverse = 1.0 / density
        for number in range(3):
            at = pl.ds(number * size + flat, 8)
            probe_ref[at, lanes] = (momenta[number] + 0.5 * force_ref[at, lanes]) * inverse

    blocks(planes, width_x, width_y, body)
    first = gather_octet(recv_ref, cap, 2 * step)
    rows[...] = sampled_ref[...]
    for number, row in enumerate(sample(first, planes, width_x, width_y, probe_ref)):
        rows[3 * step + number : 3 * step + number + 1, :] = row
    per = LANES // cap
    for device in range(out_ref.shape[0]):
        line, place = device // per, device % per
        piece = rows[:, line * LANES : (line + 1) * LANES]
        if place:
            piece = pltpu.roll(piece, LANES - place * cap, 1)
        out_ref[device] = piece


def call(kernel, outs, scratch=(), flops=0, moved=0, limit=40):
    shapes = [jax.ShapeDtypeStruct(shape, kind) for shape, kind in outs]
    return pl.pallas_call(
        kernel,
        out_shape=shapes,
        scratch_shapes=list(scratch),
        cost_estimate=pl.CostEstimate(flops=flops, bytes_accessed=moved, transcendentals=0),
        compiler_params=pltpu.CompilerParams(vmem_limit_bytes=limit * 1024 * 1024),
    )


def pair(up, down, axis):
    count = lax.axis_size(axis)
    forward = [(i, (i + 1) % count) for i in range(count)]
    backward = [(target, source) for source, target in forward]
    return lax.ppermute(up, axis, forward), lax.ppermute(down, axis, backward)


def exchange(faces, planes, width_x):
    x_up, x_down, y_up, y_down = faces
    x_low, x_high = pair(x_up, x_down, "gx")

    def kernel(*refs):
        corner_kernel(planes, width_x, *refs)

    y_up, y_down = call(kernel, [((8, LANES), F32)] * 2, moved=300000)(y_up, y_down, x_low, x_high)
    y_low, y_high = pair(y_up, y_down, "gy")
    return x_low, x_high, y_low, y_high


def local(populations_in, marker_force, marker_frac, marker_cell, marker_tile):
    devices = lax.axis_size("gx") * lax.axis_size("gy")
    steps, owned = marker_force.shape[0], marker_force.shape[2]
    cap = max(2, 2 * owned // devices)
    slots = devices * cap
    planes, width_x, width_y = populations_in.shape[1:]
    size = planes * width_x
    by_comp = lambda x: jnp.transpose(x, (1, 0, 2))

    def pack(*refs):
        pack_kernel(devices, cap, steps, *refs)

    outgoing, slot = call(
        pack,
        [((devices, 8, LANES), F32), ((steps, owned), jnp.int32)],
        [pltpu.VMEM((16, owned), F32)],
    )(
        marker_tile.reshape(steps * owned // LANES, LANES),
        by_comp(marker_cell),
        by_comp(marker_frac),
        by_comp(marker_force),
    )
    arrived = lax.all_to_all(outgoing, ("gx", "gy"), split_axis=0, concat_axis=0, tiled=True)

    field = ((3 * size, width_y), F32)
    pops = (populations_in.shape, F32)
    rows_x = -(-5 * planes // 8) * 8
    faces = [((rows_x, width_y), F32)] * 2 + [((8, LANES), F32)] * 2

    def first(*refs):
        first_kernel(cap, *refs)

    force_0, post, *sent = call(first, [field, pops] + faces)(arrived, populations_in)
    halos = exchange(sent, planes, width_x)

    def second_spread(*refs):
        spread_kernel(cap, 1, planes, width_x, *refs)

    (force_1,) = call(second_spread, [field], flops=10**9, moved=10**6)(arrived)

    probe, post, *sent = call(middle_kernel, [field, pops] + faces, [pltpu.VMEM(pops[0], F32)])(
        post, *halos, force_0, force_1
    )
    halos = exchange(sent, planes, width_x)

    def first_sample(*refs):
        sample_kernel(cap, 0, planes, width_x, *refs)

    (sampled,) = call(first_sample, [((8, slots), F32)], flops=10**9, moved=10**6)(arrived, probe)

    def last(*refs):
        last_kernel(cap, 1, *refs)

    fields, back = call(
        last,
        [pops, ((devices, 8, LANES), F32)],
        [pltpu.VMEM(field[0], F32), pltpu.VMEM((8, slots), F32)],
    )(post, *halos, force_1, arrived, sampled)
    returned = lax.all_to_all(back, ("gx", "gy"), split_axis=0, concat_axis=0, tiled=True)

    def unpack(*refs):
        unpack_kernel(cap, steps, *refs)

    (velocity,) = call(unpack, [((3, steps, owned), F32)])(returned, slot)
    return fields, by_comp(velocity)


def solution(mesh):
    return jax.shard_map(
        local,
        mesh=mesh,
        in_specs=(
            P(None, None, "gx", "gy"),
            P(None, None, ("gx", "gy")),
            P(None, None, ("gx", "gy")),
            P(None, None, ("gx", "gy")),
            P(None, ("gx", "gy"), None),
        ),
        out_specs=(P(None, None, "gx", "gy"), P(None, None, ("gx", "gy"))),
        check_vma=False,
    )
```

```python
import jax
import jax.numpy as jnp
from jax import lax
from jax.experimental import pallas as pl
from jax.experimental.pallas import tpu as pltpu
from jax.sharding import PartitionSpec as P

LATTICE = [
    (0, 0, 0),
    (1, 0, 0),
    (-1, 0, 0),
    (0, 1, 0),
    (0, -1, 0),
    (0, 0, 1),
    (0, 0, -1),
    (1, 1, 0),
    (-1, -1, 0),
    (1, -1, 0),
    (-1, 1, 0),
    (1, 0, 1),
    (-1, 0, -1),
    (1, 0, -1),
    (-1, 0, 1),
    (0, 1, 1),
    (0, -1, -1),
    (0, 1, -1),
    (0, -1, 1),
]
WEIGHTS = [1.0 / 3.0] + [1.0 / 18.0] * 6 + [1.0 / 36.0] * 12
relax_time = 0.8
OMEGA = 1.0 / relax_time
SOURCE = 1.0 - 0.5 / relax_time
LANES = 128

X_UP = [i for i in range(19) if LATTICE[i][0] == 1]
X_DOWN = [i for i in range(19) if LATTICE[i][0] == -1]
Y_UP = [i for i in range(19) if LATTICE[i][1] == 1]
Y_DOWN = [i for i in range(19) if LATTICE[i][1] == -1]

BF = jnp.bfloat16
F32 = jnp.float32


def split2(x):
    high = x.astype(BF)
    low = (x - high.astype(F32)).astype(BF)
    return high, low


def split3(x):
    high = x.astype(BF)
    rest = x - high.astype(F32)
    middle = rest.astype(BF)
    low = (rest - middle.astype(F32)).astype(BF)
    return high, middle, low


def nt(a, b):
    return lax.dot_general(a, b, (((1,), (1,)), ((), ())), preferred_element_type=F32)


def nn(a, b):
    return lax.dot_general(a, b, (((1,), (0,)), ((), ())), preferred_element_type=F32)


def iota(shape, dim):
    return lax.broadcasted_iota(jnp.int32, shape, dim)


def slot_table(slot, slots):
    owned = slot.shape[1]
    return jnp.where(iota((slots, owned), 0) == slot, 1.0, 0.0).astype(BF)


def fetch(pairs, sems):
    copies = [pltpu.make_async_copy(source, target, sems.at[n]) for n, (source, target) in enumerate(pairs)]
    for copy in copies:
        copy.start()
    return copies


def pack_kernel(
    devices, cap, steps, tile_in, cell_in, frac_in, force_in, out_ref, slot_ref, rows, tile_ref, cell_ref, frac_ref, force_ref, sems
):
    copies = fetch([(tile_in, tile_ref), (cell_in, cell_ref), (frac_in, frac_ref), (force_in, force_ref)], sems)
    owned = cell_ref.shape[2]
    slots = devices * cap
    lines = owned // LANES
    earlier = jnp.where(iota((owned, owned), 0) < iota((owned, owned), 1), 1.0, 0.0).astype(BF)
    octets = []
    for copy in copies:
        copy.wait()
    for step in range(steps):
        tiles = jnp.concatenate(
            [tile_ref[step * lines + r : step * lines + r + 1, :] for r in range(lines)], axis=1
        )
        member = jnp.where(iota((devices, owned), 0) == tiles, 1.0, 0.0)
        rank = jnp.sum(nn(member.astype(BF), earlier) * member, axis=0, keepdims=True)
        slot = tiles * cap + rank.astype(jnp.int32)
        slot_ref[step : step + 1, :] = slot
        rows[...] = jnp.zeros_like(rows)
        for number in range(3):
            rows[number : number + 1, :] = cell_ref[number, step : step + 1, :].astype(F32)
            rows[3 + number : 4 + number, :] = frac_ref[number, step : step + 1, :]
            rows[6 + number : 7 + number, :] = force_ref[number, step : step + 1, :]
        parts = jnp.concatenate(split3(rows[...]), axis=0)
        packed = nt(parts, slot_table(slot, slots))
        packed = packed[0:16] + packed[16:32] + packed[32:48]
        octets += [packed[0:8], packed[8:16]]
    group = iota((8, LANES), 1) // cap
    per = LANES // cap
    for device in range(devices):
        line, place = device // per, device % per
        block = jnp.zeros((8, LANES), F32)
        for number, octet in enumerate(octets):
            piece = octet[:, line * LANES : (line + 1) * LANES]
            shift = (number - place) * cap % LANES
            if shift:
                piece = pltpu.roll(piece, shift, 1)
            block = jnp.where(group == number, piece, block)
        out_ref[device] = block


def gather_octet(recv_ref, cap, number):
    devices = recv_ref.shape[0]
    per = LANES // cap
    group = iota((8, LANES), 1) // cap
    pieces = []
    for line in range(devices // per):
        total = jnp.zeros((8, LANES), F32)
        for place in range(per):
            piece = recv_ref[line * per + place]
            shift = (place - number) * cap % LANES
            if shift:
                piece = pltpu.roll(piece, shift, 1)
            total = jnp.where(group == place, piece, total)
        pieces.append(total)
    return jnp.concatenate(pieces, axis=1)


def unpack_kernel(cap, steps, recv_ref, slot_ref, out_ref):
    devices = recv_ref.shape[0]
    per = LANES // cap
    group = iota((steps, LANES), 1) // cap
    comps = []
    for number in range(3):
        pieces = []
        for line in range(devices // per):
            total = jnp.zeros((steps, LANES), F32)
            for place in range(per):
                piece = recv_ref[line * per + place]
                shift = (place - number) * cap % LANES
                if shift:
                    piece = pltpu.roll(piece, shift, 1)
                total = jnp.where(group == place, piece, total)
            pieces.append(total)
        comps.append(jnp.concatenate(pieces, axis=1))
    slots = devices * cap
    for step in range(steps):
        rows = jnp.concatenate([comp[step : step + 1] for comp in comps] + [jnp.zeros((13, slots), F32)], axis=0)
        found = nn(jnp.concatenate(split3(rows), axis=0), slot_table(slot_ref[step : step + 1, :], slots))
        found = found[0:8] + found[16:24] + found[32:40]
        for number in range(3):
            out_ref[number, step : step + 1, :] = found[number : number + 1]


def line_weights(cell, frac, extent):
    grid = iota((extent, cell.shape[1]), 0).astype(F32)
    return jnp.where(grid == cell, 1.0 - frac, jnp.where(grid == cell + 1.0, frac, 0.0))


def y_table(cell, frac, extent):
    grid = iota((extent, cell.shape[1]), 0).astype(F32)
    lower, upper = grid == cell, grid == cell + 1.0
    tables = []
    for low, high in zip(split2(1.0 - frac), split2(frac)):
        low, high = low.astype(F32), high.astype(F32)
        tables.append(jnp.where(lower, low, jnp.where(upper, high, 0.0)).astype(BF))
    return tables


def plane_table(rows, planes, width_x):
    kernel_x = line_weights(rows[0:1], rows[3:4], width_x)
    kernel_z = line_weights(rows[2:3], rows[5:6], 8)
    return [kernel_z[z : z + 1] * kernel_x for z in range(planes)]


def spread(first, second, planes, width_x, width_y, force_ref):
    table = jnp.concatenate(plane_table(first, planes, width_x), axis=0)
    along_y = y_table(first[1:2], first[4:5], width_y)
    size = planes * width_x
    for number, strength in enumerate((first[6:7], first[7:8], second[0:1])):
        high, low = split2(table * strength)
        force_ref[number * size : (number + 1) * size, :] = (
            nt(high, along_y[0]) + nt(high, along_y[1]) + nt(low, along_y[0])
        )


def sample(first, planes, width_x, width_y, probe_ref):
    table = jnp.concatenate(plane_table(first, planes, width_x), axis=0)
    along_y = y_table(first[1:2], first[4:5], width_y)
    size = planes * width_x
    rows = []
    for number in range(3):
        high, low = split2(probe_ref[number * size : (number + 1) * size, :])
        found = nn(high, along_y[0]) + nn(high, along_y[1]) + nn(low, along_y[0])
        rows.append(jnp.sum(found * table, axis=0, keepdims=True))
    return rows


def moments(f):
    density = f[0]
    diff = {}
    for member in range(1, 19, 2):
        density = density + (f[member] + f[member + 1])
        diff[member] = f[member] - f[member + 1]
    momenta = []
    for number in range(3):
        total = None
        for member in range(1, 19, 2):
            sign = LATTICE[member][number]
            if sign == 0:
                continue
            if total is None:
                total = diff[member] if sign == 1 else -diff[member]
            else:
                total = total + diff[member] if sign == 1 else total - diff[member]
        momenta.append(total)
    return density, momenta


def dot_c(vector, comps):
    total = None
    for number in range(3):
        if vector[number] == 0:
            continue
        if total is None:
            total = comps[number] if vector[number] == 1 else -comps[number]
        else:
            total = total + comps[number] if vector[number] == 1 else total - comps[number]
    return total


def collide(f, density, momenta, force):
    inverse = 1.0 / density
    speed = [(momenta[n] + 0.5 * force[n]) * inverse for n in range(3)]
    scaled = OMEGA * density
    speed_sq = speed[0] * speed[0] + speed[1] * speed[1] + speed[2] * speed[2]
    along = speed[0] * force[0] + speed[1] * force[1] + speed[2] * force[2]
    base = scaled * (1.0 - 1.5 * speed_sq) - (3.0 * SOURCE) * along
    flow = [scaled * speed[n] for n in range(3)]
    pull = [(3.0 * SOURCE) * force[n] for n in range(3)]
    linear = [3.0 * flow[n] + pull[n] for n in range(3)]
    square = [4.5 * flow[n] + 3.0 * pull[n] for n in range(3)]
    posts = [(1.0 - OMEGA) * f[0] + WEIGHTS[0] * base]
    for member in range(1, 19, 2):
        vector = LATTICE[member]
        even = WEIGHTS[member] * (base + dot_c(vector, speed) * dot_c(vector, square))
        odd = WEIGHTS[member] * dot_c(vector, linear)
        posts.append((1.0 - OMEGA) * f[member] + (even + odd))
        posts.append((1.0 - OMEGA) * f[member + 1] + (even - odd))
    return posts


def send_faces(post_ref, x_up, x_down, y_up, y_down):
    planes, width_x, width_y = post_ref.shape[1], post_ref.shape[2], post_ref.shape[3]
    for out, members, row in ((x_up, X_UP, width_x - 1), (x_down, X_DOWN, 0)):
        out[...] = jnp.zeros_like(out)
        for place, member in enumerate(members):
            for z in range(planes):
                number = place * planes + z
                out[number : number + 1, :] = post_ref[member, z, row : row + 1, :]
    lane = iota((width_x, LANES), 1)
    count = 5 * planes
    for out, members, start, at in ((y_up, Y_UP, width_y - LANES, LANES - 1), (y_down, Y_DOWN, 0, 0)):
        total = jnp.zeros((width_x, LANES), F32)
        for place, member in enumerate(members):
            for z in range(planes):
                number = place * planes + z
                block = post_ref[member, z, :, start : start + LANES]
                if LATTICE[member][0]:
                    block = pltpu.roll(block, LATTICE[member][0] % width_x, 0)
                if (number - at) % LANES:
                    block = pltpu.roll(block, (number - at) % LANES, 1)
                total = jnp.where(lane == number, block, total)
        packed = jnp.zeros((8, LANES), F32)
        group = iota((8, LANES), 1) // count
        for number in range(width_x // 8):
            piece = total[number * 8 : number * 8 + 8]
            if number:
                piece = pltpu.roll(piece, number * count, 1)
            packed = jnp.where(group == number, piece, packed)
        out[...] = packed


def corner_kernel(planes, width_x, y_up, y_down, x_low, x_high, out_up, out_down):
    count = 5 * planes
    width_y = x_low.shape[1]
    lane, row = iota((8, LANES), 1), iota((8, LANES), 0)
    for source, out, members, start, at in (
        (y_up, out_up, Y_UP, width_y - LANES, LANES - 1),
        (y_down, out_down, Y_DOWN, 0, 0),
    ):
        block = source[...]
        for place, member in enumerate(members):
            along = LATTICE[member][0]
            if along == 0:
                continue
            halo, order = (x_low, X_UP) if along == 1 else (x_high, X_DOWN)
            group, sub = (0, 0) if along == 1 else (width_x // 8 - 1, 7)
            for z in range(planes):
                number = order.index(member) * planes + z
                target = group * count + place * planes + z
                piece = jnp.broadcast_to(halo[number : number + 1, start : start + LANES], (8, LANES))
                if (target - at) % LANES:
                    piece = pltpu.roll(piece, (target - at) % LANES, 1)
                block = jnp.where((lane == target) & (row == sub), piece, block)
        out[...] = block


def stream(post_ref, x_low, x_high, y_low, y_high, out_ref):
    planes, width_x, width_y = post_ref.shape[1], post_ref.shape[2], post_ref.shape[3]
    count = 5 * planes
    rows = iota((width_x, width_y), 0)
    lane = iota((width_x, LANES), 1)
    low, high = y_low[...], y_high[...]
    for member in range(19):
        along_x, along_y, along_z = LATTICE[member]
        for z in range(planes):
            block = post_ref[member, z]
            if along_x == 1:
                number = X_UP.index(member) * planes + z
                block = jnp.where(rows == 0, x_low[number : number + 1, :], pltpu.roll(block, 1, 0))
            elif along_x == -1:
                number = X_DOWN.index(member) * planes + z
                block = jnp.where(
                    rows == width_x - 1,
                    x_high[number : number + 1, :],
                    pltpu.roll(block, width_x - 1, 0),
                )
            to = (z + along_z) % planes
            if along_y == 0:
                out_ref[member, to] = block
                continue
            halo, order, at = (low, Y_UP, 0) if along_y == 1 else (high, Y_DOWN, LANES - 1)
            number = order.index(member) * planes + z
            edge = []
            for group in range(width_x // 8):
                shift = (at - group * count - number) % LANES
                edge.append(pltpu.roll(halo, shift, 1) if shift else halo)
            edge = jnp.concatenate(edge, axis=0)
            block = pltpu.roll(block, along_y % width_y, 1)
            start = 0 if along_y == 1 else width_y - LANES
            first = jnp.where(lane == at, edge, block[:, start : start + LANES])
            if along_y == 1:
                block = jnp.concatenate([first, block[:, LANES:]], axis=1)
            else:
                block = jnp.concatenate([block[:, :start], first], axis=1)
            out_ref[member, to] = block


def blocks(planes, width_x, width_y, body):
    per = width_x // 8

    @pl.loop(0, planes * per)
    def _(index):
        z = index // per
        row = pl.multiple_of((index % per) * 8, 8)
        flat = pl.multiple_of(index * 8, 8)
        for start in range(0, width_y, LANES):
            body(z, pl.ds(row, 8), flat, pl.ds(start, LANES))


def spread_kernel(cap, step, planes, width_x, recv_ref, force_ref):
    first = gather_octet(recv_ref, cap, 2 * step)
    second = gather_octet(recv_ref, cap, 2 * step + 1)
    spread(first, second, planes, width_x, force_ref.shape[1], force_ref)


def first_kernel(cap, recv_ref, f_in, force_ref, post_ref, x_up, x_down, y_up, y_down, f_ref, sems):
    copies = fetch([(f_in, f_ref)], sems)
    planes, width_x, width_y = f_ref.shape[1], f_ref.shape[2], f_ref.shape[3]
    spread_kernel(cap, 0, planes, width_x, recv_ref, force_ref)
    size = planes * width_x
    for copy in copies:
        copy.wait()

    def body(z, row, flat, lanes):
        f = [f_ref[member, z, row, lanes] for member in range(19)]
        force = [force_ref[pl.ds(number * size + flat, 8), lanes] for number in range(3)]
        density, momenta = moments(f)
        for member, value in enumerate(collide(f, density, momenta, force)):
            post_ref[member, z, row, lanes] = value

    blocks(planes, width_x, width_y, body)
    send_faces(post_ref, x_up, x_down, y_up, y_down)


def middle_kernel(
    post_in, x_low, x_high, y_low, y_high, force_ref, next_ref, probe_ref, post_ref, x_up, x_down, y_up, y_down, f_ref
):
    planes, width_x, width_y = post_in.shape[1], post_in.shape[2], post_in.shape[3]
    size = planes * width_x
    stream(post_in, x_low, x_high, y_low, y_high, f_ref)

    def body(z, row, flat, lanes):
        f = [f_ref[member, z, row, lanes] for member in range(19)]
        density, momenta = moments(f)
        inverse = 1.0 / density
        force = []
        for number in range(3):
            at = pl.ds(number * size + flat, 8)
            probe_ref[at, lanes] = (momenta[number] + 0.5 * force_ref[at, lanes]) * inverse
            force.append(next_ref[at, lanes])
        for member, value in enumerate(collide(f, density, momenta, force)):
            post_ref[member, z, row, lanes] = value

    blocks(planes, width_x, width_y, body)
    send_faces(post_ref, x_up, x_down, y_up, y_down)


def sample_kernel(cap, step, planes, width_x, recv_ref, probe_ref, out_ref):
    first = gather_octet(recv_ref, cap, 2 * step)
    out_ref[...] = jnp.zeros_like(out_ref)
    for number, row in enumerate(sample(first, planes, width_x, probe_ref.shape[1], probe_ref)):
        out_ref[number : number + 1, :] = row


def send_back(cap, rows, out_ref):
    devices, steps = out_ref.shape[0], out_ref.shape[1]
    per = LANES // cap
    group = iota((steps, LANES), 1) // cap
    for device in range(devices):
        line, place = device // per, device % per
        total = jnp.zeros((steps, LANES), F32)
        for number in range(3):
            piece = rows[number * steps : (number + 1) * steps, line * LANES : (line + 1) * LANES]
            shift = (number - place) * cap % LANES
            if shift:
                piece = pltpu.roll(piece, shift, 1)
            total = jnp.where(group == number, piece, total)
        out_ref[device] = total


def last_kernel(
    cap, step, post_in, x_low, x_high, y_low, y_high, force_ref, recv_ref, sampled_ref, f_ref, out_ref, probe_ref, rows
):
    planes, width_x, width_y = post_in.shape[1], post_in.shape[2], post_in.shape[3]
    size = planes * width_x
    stream(post_in, x_low, x_high, y_low, y_high, f_ref)

    def body(z, row, flat, lanes):
        f = [f_ref[member, z, row, lanes] for member in range(19)]
        density, momenta = moments(f)
        inverse = 1.0 / density
        for number in range(3):
            at = pl.ds(number * size + flat, 8)
            probe_ref[at, lanes] = (momenta[number] + 0.5 * force_ref[at, lanes]) * inverse

    blocks(planes, width_x, width_y, body)
    first = gather_octet(recv_ref, cap, 2 * step)
    steps = out_ref.shape[1]
    for number, row in enumerate(sample(first, planes, width_x, width_y, probe_ref)):
        for other in range(step):
            rows[steps * number + other : steps * number + other + 1, :] = sampled_ref[number : number + 1, :]
        rows[steps * number + step : steps * number + step + 1, :] = row
    send_back(cap, rows, out_ref)


def call(kernel, outs, scratch=(), flops=0, moved=0, limit=40, fetched=(False,)):
    shapes = [jax.ShapeDtypeStruct(shape, kind) for shape, kind in outs]
    specs = [pl.BlockSpec(memory_space=pltpu.HBM if own else pltpu.VMEM) for own in fetched]
    return pl.pallas_call(
        kernel,
        out_shape=shapes,
        scratch_shapes=list(scratch),
        **({"in_specs": specs} if any(fetched) else {}),
        cost_estimate=pl.CostEstimate(flops=flops, bytes_accessed=moved, transcendentals=0),
        compiler_params=pltpu.CompilerParams(vmem_limit_bytes=limit * 1024 * 1024),
    )


def pair(up, down, axis):
    count = lax.axis_size(axis)
    forward = [(i, (i + 1) % count) for i in range(count)]
    backward = [(target, source) for source, target in forward]
    return lax.ppermute(up, axis, forward), lax.ppermute(down, axis, backward)


def exchange(faces, planes, width_x):
    x_up, x_down, y_up, y_down = faces
    x_low, x_high = pair(x_up, x_down, "gx")

    def kernel(*refs):
        corner_kernel(planes, width_x, *refs)

    y_up, y_down = call(kernel, [((8, LANES), F32)] * 2, moved=300000)(y_up, y_down, x_low, x_high)
    y_low, y_high = pair(y_up, y_down, "gy")
    return x_low, x_high, y_low, y_high


def local(populations_in, marker_force, marker_frac, marker_cell, marker_tile):
    devices = lax.axis_size("gx") * lax.axis_size("gy")
    steps, owned = marker_force.shape[0], marker_force.shape[2]
    cap = max(2, 2 * owned // devices)
    slots = devices * cap
    planes, width_x, width_y = populations_in.shape[1:]
    size = planes * width_x
    by_comp = lambda x: jnp.transpose(x, (1, 0, 2))

    def pack(*refs):
        pack_kernel(devices, cap, steps, *refs)

    outgoing, slot = call(
        pack,
        [((devices, 8, LANES), F32), ((steps, owned), jnp.int32)],
        [
            pltpu.VMEM((16, owned), F32),
            pltpu.VMEM((steps * owned // LANES, LANES), jnp.int32),
            pltpu.VMEM((3, steps, owned), jnp.int32),
            pltpu.VMEM((3, steps, owned), F32),
            pltpu.VMEM((3, steps, owned), F32),
            pltpu.SemaphoreType.DMA((4,)),
        ],
        fetched=(True,) * 4,
        limit=63,
    )(
        marker_tile.reshape(steps * owned // LANES, LANES),
        by_comp(marker_cell),
        by_comp(marker_frac),
        by_comp(marker_force),
    )
    arrived = lax.all_to_all(outgoing, ("gx", "gy"), split_axis=0, concat_axis=0, tiled=True)

    field = ((3 * size, width_y), F32)
    pops = (populations_in.shape, F32)
    rows_x = -(-5 * planes // 8) * 8
    faces = [((rows_x, width_y), F32)] * 2 + [((8, LANES), F32)] * 2

    def first(*refs):
        first_kernel(cap, *refs)

    force_0, post, *sent = call(
        first,
        [field, pops] + faces,
        [pltpu.VMEM(pops[0], F32), pltpu.SemaphoreType.DMA((1,))],
        fetched=(False, True),
    )(arrived, populations_in)
    halos = exchange(sent, planes, width_x)

    def second_spread(*refs):
        spread_kernel(cap, 1, planes, width_x, *refs)

    (force_1,) = call(second_spread, [field], flops=10**9, moved=10**6)(arrived)

    probe, post, *sent = call(middle_kernel, [field, pops] + faces, [pltpu.VMEM(pops[0], F32)])(
        post, *halos, force_0, force_1
    )
    halos = exchange(sent, planes, width_x)

    def first_sample(*refs):
        sample_kernel(cap, 0, planes, width_x, *refs)

    (sampled,) = call(first_sample, [((8, slots), F32)], flops=10**9, moved=10**6)(arrived, probe)

    def last(*refs):
        last_kernel(cap, 1, *refs)

    fields, back = call(
        last,
        [pops, ((devices, steps, LANES), F32)],
        [pltpu.VMEM(field[0], F32), pltpu.VMEM((8, slots), F32)],
    )(post, *halos, force_1, arrived, sampled)
    returned = lax.all_to_all(back, ("gx", "gy"), split_axis=0, concat_axis=0, tiled=True)

    def unpack(*refs):
        unpack_kernel(cap, steps, *refs)

    (velocity,) = call(unpack, [((3, steps, owned), F32)])(returned, slot)
    return fields, by_comp(velocity)


def solution(mesh):
    return jax.shard_map(
        local,
        mesh=mesh,
        in_specs=(
            P(None, None, "gx", "gy"),
            P(None, None, ("gx", "gy")),
            P(None, None, ("gx", "gy")),
            P(None, None, ("gx", "gy")),
            P(None, ("gx", "gy"), None),
        ),
        out_specs=(P(None, None, "gx", "gy"), P(None, None, ("gx", "gy"))),
        check_vma=False,
    )
```

```python
import jax
import jax.numpy as jnp
from jax import lax
from jax.experimental import pallas as pl
from jax.experimental.pallas import tpu as pltpu
from jax.sharding import PartitionSpec as P

LATTICE = [
    (0, 0, 0),
    (1, 0, 0),
    (-1, 0, 0),
    (0, 1, 0),
    (0, -1, 0),
    (0, 0, 1),
    (0, 0, -1),
    (1, 1, 0),
    (-1, -1, 0),
    (1, -1, 0),
    (-1, 1, 0),
    (1, 0, 1),
    (-1, 0, -1),
    (1, 0, -1),
    (-1, 0, 1),
    (0, 1, 1),
    (0, -1, -1),
    (0, 1, -1),
    (0, -1, 1),
]
WEIGHTS = [1.0 / 3.0] + [1.0 / 18.0] * 6 + [1.0 / 36.0] * 12
relax_time = 0.8
OMEGA = 1.0 / relax_time
SOURCE = 1.0 - 0.5 / relax_time
LANES = 128

BF = jnp.bfloat16
F32 = jnp.float32


def split2(x):
    high = x.astype(BF)
    low = (x - high.astype(F32)).astype(BF)
    return high, low


def split3(x):
    high = x.astype(BF)
    rest = x - high.astype(F32)
    middle = rest.astype(BF)
    low = (rest - middle.astype(F32)).astype(BF)
    return high, middle, low


def nt(a, b):
    return lax.dot_general(a, b, (((1,), (1,)), ((), ())), preferred_element_type=F32)


def nn(a, b):
    return lax.dot_general(a, b, (((1,), (0,)), ((), ())), preferred_element_type=F32)


def iota(shape, dim):
    return lax.broadcasted_iota(jnp.int32, shape, dim)


RING = 8
SIDE = LANES


def slot_table(slot, slots):
    owned = slot.shape[1]
    return jnp.where(iota((slots, owned), 0) == slot, 1.0, 0.0).astype(BF)


def fetch(pairs, sems):
    copies = [pltpu.make_async_copy(source, target, sems.at[n]) for n, (source, target) in enumerate(pairs)]
    for copy in copies:
        copy.start()
    return copies


def ghosts(step, steps, count_gx, count_gy, width_x, width_y, tiles, cell_x, cell_y):
    reach = steps - step
    along = []
    tiles = tiles.astype(F32)
    gx = jnp.floor((tiles + 0.5) * (1.0 / count_gy))
    for cell, width, place, count in (
        (cell_x, width_x, gx, count_gx),
        (cell_y, width_y, tiles - gx * count_gy, count_gy),
    ):
        above, below = cell >= width - 1 - reach, cell <= reach - 1
        place_up = jnp.where(place == count - 1, 0.0, place + 1.0)
        place_down = jnp.where(place == 0, count - 1.0, place - 1.0)
        along.append(
            (
                jnp.where(above | below, 1.0, 0.0),
                place,
                jnp.where(above, place_up, place_down),
                cell,
                jnp.where(above, cell - width, cell + width),
            )
        )
    (near_x, here_x, there_x, in_x, out_x), (near_y, here_y, there_y, in_y, out_y) = along
    return [
        (jnp.where(near_x > 0, there_x * count_gy + here_y, -1.0), out_x, in_y),
        (jnp.where(near_y > 0, here_x * count_gy + there_y, -1.0), in_x, out_y),
        (jnp.where(near_x * near_y > 0, there_x * count_gy + there_y, -1.0), out_x, out_y),
    ]


def pack(grid, steps, cap, step_rows, out_ref, slot_ref, rows, turn=None):
    count_gx, count_gy, width_x, width_y = grid
    devices, half = count_gx * count_gy, cap // 2
    owned = rows.shape[1]
    slots = devices * cap
    earlier = jnp.where(iota((owned, owned), 0) < iota((owned, owned), 1), 1.0, 0.0).astype(BF)
    column = iota((devices, owned), 0).astype(F32)
    octets, extras, most = [], [], []
    for step in range(steps):
        tiles, values = step_rows(step)
        beside = ghosts(step, steps, *grid, tiles, values[0], values[1])
        member = [jnp.where(column == tile, 1.0, 0.0) for tile in [tiles.astype(F32)] + [b[0] for b in beside]]
        before = nn(jnp.concatenate(member, axis=0).astype(BF), earlier)
        before = [before[n * devices : (n + 1) * devices] for n in range(4)]
        if turn is None:
            rank = jnp.sum(before[0] * member[0], axis=0, keepdims=True)
            slot = tiles * cap + rank.astype(jnp.int32)
            slot_ref[step : step + 1, :] = slot
            rows[...] = jnp.zeros_like(rows)
            for number, value in enumerate(values):
                rows[number : number + 1, :] = value
            packed = nt(jnp.concatenate(split3(rows[...]), axis=0), slot_table(slot, slots))
            packed = packed[0:16] + packed[16:32] + packed[32:48]
            octets.append((packed[0:8], packed[8:16]))
        taken = jnp.zeros((devices, 1), F32)
        extra = jnp.zeros((48, devices * half), F32)
        for number, (tile, cell_x, cell_y) in enumerate(beside):
            rank = jnp.sum((before[number + 1] + taken) * member[number + 1], axis=0, keepdims=True)
            taken = taken + jnp.sum(member[number + 1], axis=1, keepdims=True)
            if turn is not None:
                rank = rank - turn * half
            fits = (tile >= 0) & (rank >= 0) & (rank < half)
            slot = jnp.where(fits, tile * half + rank, -1.0).astype(jnp.int32)
            rows[...] = jnp.zeros_like(rows)
            for place, value in zip((1, 2, 3, 4, 5, 6, 7, 9, 10), [cell_x, cell_y] + values[2:]):
                rows[place : place + 1, :] = value
            extra = extra + nt(jnp.concatenate(split3(rows[...]), axis=0), slot_table(slot, devices * half))
        extra = extra[0:16] + extra[16:32] + extra[32:48]
        extras.append((extra[0:8], extra[8:16]))
        most.append(jnp.max(taken, axis=0, keepdims=True))
    lane, row = iota((8, LANES), 1), iota((8, LANES), 0)

    def placed(octet, device, width, offset):
        line, place = device * width // LANES, device * width % LANES
        piece = octet[:, line * LANES : (line + 1) * LANES]
        shift = (offset - place) % LANES
        if shift:
            piece = pltpu.roll(piece, shift, 1)
        return jnp.where((lane >= offset) & (lane < offset + width), piece, 0.0)

    heading = jnp.zeros((8, LANES), F32)
    for step in range(steps):
        start = (2 * step + 1) * cap + half
        heading = jnp.where((row == 3) & (lane >= start) & (lane < start + half), most[step], heading)
    for device in range(devices):
        block = heading
        for step in range(steps):
            start = 2 * step * cap
            if turn is None:
                block = block + placed(octets[step][0], device, cap, start)
                block = block + placed(octets[step][1], device, cap, start + cap)
            block = block + placed(extras[step][0], device, half, start + cap)
            block = block + placed(extras[step][1], device, half, start + cap + half)
        out_ref[device] = block


def marker_rows(tile_ref, cell_ref, frac_ref, force_ref):
    lines = cell_ref.shape[2] // LANES

    def step_rows(step):
        tiles = jnp.concatenate(
            [tile_ref[step * lines + r : step * lines + r + 1, :] for r in range(lines)], axis=1
        )
        values = [cell_ref[n, step : step + 1, :].astype(F32) for n in range(3)]
        values += [frac_ref[n, step : step + 1, :] for n in range(3)]
        values += [force_ref[n, step : step + 1, :] for n in range(3)]
        return tiles, values

    return step_rows


def pack_kernel(
    grid, steps, cap, tile_in, cell_in, frac_in, force_in, f_in, out_ref, slot_ref, x_up, x_down,
    rows, tile_ref, cell_ref, frac_ref, force_ref, near_ref, far_ref, sems,
):
    width_x = f_in.shape[2]
    copies = fetch(
        [
            (tile_in, tile_ref),
            (cell_in, cell_ref),
            (frac_in, frac_ref),
            (force_in, force_ref),
            (f_in.at[:, :, pl.ds(0, 8), :], near_ref),
            (f_in.at[:, :, pl.ds(width_x - 8, 8), :], far_ref),
        ],
        sems,
    )
    for copy in copies[:4]:
        copy.wait()
    pack(grid, steps, cap, marker_rows(tile_ref, cell_ref, frac_ref, force_ref), out_ref, slot_ref, rows)
    for copy in copies[4:]:
        copy.wait()
    planes = f_in.shape[1]
    for member in range(19):
        for z in range(planes):
            plane = member * planes + z
            x_up[2 * plane : 2 * plane + 2, :] = far_ref[member, z, 6:8, :]
            x_down[2 * plane : 2 * plane + 2, :] = near_ref[member, z, 0:2, :]


def turn_kernel(grid, steps, cap, turn_ref, tile_ref, cell_ref, frac_ref, force_ref, out_ref, rows):
    step_rows = marker_rows(tile_ref, cell_ref, frac_ref, force_ref)
    pack(grid, steps, cap, step_rows, out_ref, None, rows, turn_ref[0].astype(F32))


def gather(recv_ref, offset, width):
    devices = recv_ref.shape[0]
    per = LANES // width
    group = iota((8, LANES), 1) // width
    pieces = []
    for line in range(devices // per):
        total = jnp.zeros((8, LANES), F32)
        for place in range(per):
            piece = recv_ref[line * per + place]
            shift = (place * width - offset) % LANES
            if shift:
                piece = pltpu.roll(piece, shift, 1)
            total = jnp.where(group == place, piece, total)
        pieces.append(total)
    return jnp.concatenate(pieces, axis=1)


def unpack_kernel(cap, steps, recv_ref, slot_ref, out_ref):
    devices = recv_ref.shape[0]
    per = LANES // cap
    group = iota((steps, LANES), 1) // cap
    comps = []
    for number in range(3):
        pieces = []
        for line in range(devices // per):
            total = jnp.zeros((steps, LANES), F32)
            for place in range(per):
                piece = recv_ref[line * per + place]
                shift = (place - number) * cap % LANES
                if shift:
                    piece = pltpu.roll(piece, shift, 1)
                total = jnp.where(group == place, piece, total)
            pieces.append(total)
        comps.append(jnp.concatenate(pieces, axis=1))
    slots = devices * cap
    for step in range(steps):
        rows = jnp.concatenate([comp[step : step + 1] for comp in comps] + [jnp.zeros((13, slots), F32)], axis=0)
        found = nn(jnp.concatenate(split3(rows), axis=0), slot_table(slot_ref[step : step + 1, :], slots))
        found = found[0:8] + found[16:24] + found[32:40]
        for number in range(3):
            out_ref[number, step : step + 1, :] = found[number : number + 1]


def line_weights(cell, frac, extent):
    grid = iota((extent, cell.shape[1]), 0).astype(F32)
    return jnp.where(grid == cell, 1.0 - frac, jnp.where(grid == cell + 1.0, frac, 0.0))


def y_table(cell, frac, extent):
    grid = iota((extent, cell.shape[1]), 0).astype(F32)
    lower, upper = grid == cell, grid == cell + 1.0
    tables = []
    for low, high in zip(split2(1.0 - frac), split2(frac)):
        low, high = low.astype(F32), high.astype(F32)
        tables.append(jnp.where(lower, low, jnp.where(upper, high, 0.0)).astype(BF))
    return tables


def plane_table(rows, planes, width_x):
    kernel_x = line_weights(rows[0:1], rows[3:4], width_x)
    kernel_z = line_weights(rows[2:3], rows[5:6], 8)
    return [kernel_z[z : z + 1] * kernel_x for z in range(planes)]


def product(table, along_y):
    high, low = split2(table)
    return nt(high, along_y[0]) + nt(high, along_y[1]) + nt(low, along_y[0])


def spread_own(first, second, planes, width_x, width_y, force_ref):
    tall = width_x + RING
    table = jnp.concatenate(plane_table(first, planes, width_x), axis=0)
    along_y = y_table(first[1:2], first[4:5], width_y)
    for number, strength in enumerate((first[6:7], first[7:8], second[0:1])):
        found = product(table * strength, along_y)
        for z in range(planes):
            at = (number * planes + z) * tall
            force_ref[at : at + width_x, 0:width_y] = found[z * width_x : (z + 1) * width_x]


def spread_ghosts(first, second, planes, width_x, width_y, force_ref, add):
    tall, wide = width_x + RING, width_y + SIDE
    cell_x = jnp.where(first[1:2] < 0, first[1:2] + tall, first[1:2])
    cell_y = jnp.where(first[2:3] < 0, first[2:3] + wide, first[2:3])
    kernel_x = line_weights(cell_x, first[4:5], tall)
    kernel_z = line_weights(first[3:4], first[6:7], 8)
    along_y = y_table(cell_y, first[5:6], wide)
    side_y = [table[width_y:] for table in along_y]
    ring = [kernel_z[z : z + 1] * kernel_x[width_x:] for z in range(planes)]
    side = [kernel_z[z : z + 1] * kernel_x[0:width_x] for z in range(planes)]
    ring, side = jnp.concatenate(ring, axis=0), jnp.concatenate(side, axis=0)
    for number, strength in enumerate((first[7:8], second[1:2], second[2:3])):
        found_ring = product(ring * strength, along_y)
        found_side = product(side * strength, side_y)
        for z in range(planes):
            at = (number * planes + z) * tall
            part_ring = found_ring[z * RING : (z + 1) * RING]
            part_side = found_side[z * width_x : (z + 1) * width_x]
            if add:
                part_ring = part_ring + force_ref[at + width_x : at + tall, :]
                part_side = part_side + force_ref[at : at + width_x, width_y:]
            force_ref[at + width_x : at + tall, :] = part_ring
            force_ref[at : at + width_x, width_y:] = part_side


def spread_kernel(cap, steps, planes, width_x, width_y, recv_ref, *outs):
    forces, own_ref, most_ref = outs[:steps], outs[steps], outs[steps + 1]
    half = cap // 2
    most = jnp.zeros((1, 1), F32)
    for step in range(steps):
        start = 2 * step * cap
        first = gather(recv_ref, start, cap)
        own_ref[8 * step : 8 * step + 8, :] = first
        second = gather(recv_ref, start + cap, cap)
        spread_own(first, second, planes, width_x, width_y, forces[step])
        first = gather(recv_ref, start + cap, half)
        second = gather(recv_ref, start + cap + half, half)
        spread_ghosts(first, second, planes, width_x, width_y, forces[step], False)
        most = jnp.maximum(most, jnp.max(second[3:4], axis=1, keepdims=True))
    most_ref[...] = jnp.broadcast_to(most, most_ref.shape)


def more_kernel(cap, steps, planes, width_x, width_y, recv_ref, *refs):
    half = cap // 2
    for step in range(steps):
        start = (2 * step + 1) * cap
        force_ref = refs[steps + step]
        force_ref[...] = refs[step][...]
        first, second = gather(recv_ref, start, half), gather(recv_ref, start + half, half)
        spread_ghosts(first, second, planes, width_x, width_y, force_ref, True)


def sample(first, planes, width_x, width_y, probe_ref):
    table = jnp.concatenate(plane_table(first, planes, width_x), axis=0)
    along_y = y_table(first[1:2], first[4:5], width_y)
    size = planes * width_x
    rows = []
    for number in range(3):
        high, low = split2(probe_ref[number * size : (number + 1) * size, :])
        found = nn(high, along_y[0]) + nn(high, along_y[1]) + nn(low, along_y[0])
        rows.append(jnp.sum(found * table, axis=0, keepdims=True))
    return rows


def moments(f):
    density = f[0]
    diff = {}
    for member in range(1, 19, 2):
        density = density + (f[member] + f[member + 1])
        diff[member] = f[member] - f[member + 1]
    momenta = []
    for number in range(3):
        total = None
        for member in range(1, 19, 2):
            sign = LATTICE[member][number]
            if sign == 0:
                continue
            if total is None:
                total = diff[member] if sign == 1 else -diff[member]
            else:
                total = total + diff[member] if sign == 1 else total - diff[member]
        momenta.append(total)
    return density, momenta


def dot_c(vector, comps):
    total = None
    for number in range(3):
        if vector[number] == 0:
            continue
        if total is None:
            total = comps[number] if vector[number] == 1 else -comps[number]
        else:
            total = total + comps[number] if vector[number] == 1 else total - comps[number]
    return total


def collide(f, density, momenta, force):
    inverse = 1.0 / density
    speed = [(momenta[n] + 0.5 * force[n]) * inverse for n in range(3)]
    scaled = OMEGA * density
    speed_sq = speed[0] * speed[0] + speed[1] * speed[1] + speed[2] * speed[2]
    along = speed[0] * force[0] + speed[1] * force[1] + speed[2] * force[2]
    base = scaled * (1.0 - 1.5 * speed_sq) - (3.0 * SOURCE) * along
    flow = [scaled * speed[n] for n in range(3)]
    pull = [(3.0 * SOURCE) * force[n] for n in range(3)]
    linear = [3.0 * flow[n] + pull[n] for n in range(3)]
    square = [4.5 * flow[n] + 3.0 * pull[n] for n in range(3)]
    posts = [(1.0 - OMEGA) * f[0] + WEIGHTS[0] * base]
    for member in range(1, 19, 2):
        vector = LATTICE[member]
        even = WEIGHTS[member] * (base + dot_c(vector, speed) * dot_c(vector, square))
        odd = WEIGHTS[member] * dot_c(vector, linear)
        posts.append((1.0 - OMEGA) * f[member] + (even + odd))
        posts.append((1.0 - OMEGA) * f[member + 1] + (even - odd))
    return posts


def columns_kernel(f_ref, up, down):
    planes, width_x, width_y = f_ref.shape[1], f_ref.shape[2], f_ref.shape[3]
    lane = iota((width_x, LANES), 1)
    for out, start, at in ((up, width_y - LANES, LANES - 2), (down, 0, 0)):
        lines = out.shape[1] // LANES
        totals = [jnp.zeros((width_x, LANES), F32) for _ in range(lines)]
        for plane in range(19 * planes):
            line, target = divmod(2 * plane, LANES)
            block = f_ref[plane // planes, plane % planes, :, start : start + LANES]
            shift = (target - at) % LANES
            if shift:
                block = pltpu.roll(block, shift, 1)
            totals[line] = jnp.where((lane == target) | (lane == target + 1), block, totals[line])
        for line in range(lines):
            out[:, line * LANES : (line + 1) * LANES] = totals[line]


def corner_kernel(up, down, x_low, x_high, out_up, out_down):
    width_x, width_y = up.shape[0], x_low.shape[1]
    count = x_low.shape[0]
    for source, out, start, at in ((up, out_up, width_y - LANES, LANES - 2), (down, out_down, 0, 0)):
        out[0:width_x, :] = source[...]
        out[width_x:, :] = jnp.zeros((out.shape[0] - width_x, out.shape[1]), F32)
        for number, halo in enumerate((x_low, x_high)):
            for line in range(out.shape[1] // LANES):
                last = min(count, (line + 1) * LANES)
                block = halo[line * LANES : last, start : start + LANES]
                if last < (line + 1) * LANES:
                    block = jnp.concatenate([block, jnp.zeros(((line + 1) * LANES - last, LANES), F32)], axis=0)
                turned = jnp.transpose(block)
                row = width_x + 2 * number
                out[row : row + 2, line * LANES : (line + 1) * LANES] = turned[at : at + 2]


def ring_cells(x_low, x_high, y_low, y_high, f_ref):
    planes, tall, wide = f_ref.shape[1], f_ref.shape[2], f_ref.shape[3]
    width_x, width_y = tall - RING, wide - SIDE
    lane = iota((width_x, LANES), 1)
    wide_lane = iota((LANES, LANES), 1)
    for line in range(y_low.shape[1] // LANES):
        at = slice(line * LANES, (line + 1) * LANES)
        pad = jnp.zeros((LANES - 8, LANES), F32)
        low = jnp.transpose(jnp.concatenate([y_low[width_x:, at], pad], axis=0))
        high = jnp.transpose(jnp.concatenate([y_high[width_x:, at], pad], axis=0))
        corner_low = jnp.where(wide_lane >= LANES - 2, pltpu.roll(low, LANES - 2, 1), high)
        corner_high = jnp.where(
            wide_lane >= LANES - 2, pltpu.roll(low, LANES - 4, 1), pltpu.roll(high, LANES - 2, 1)
        )
        for plane in range(line * LANES // 2, min((line + 1) * LANES // 2, 19 * planes)):
            member, z = divmod(plane, planes)
            here = 2 * plane - line * LANES
            f_ref[member, z, tall - 2 : tall, 0:width_y] = x_low[2 * plane : 2 * plane + 2, :]
            f_ref[member, z, width_x : width_x + 2, 0:width_y] = x_high[2 * plane : 2 * plane + 2, :]
            f_ref[member, z, tall - 2 : tall, width_y:] = corner_low[here : here + 2]
            f_ref[member, z, width_x : width_x + 2, width_y:] = corner_high[here : here + 2]
            below, above = y_low[0:width_x, at], y_high[0:width_x, at]
            if (LANES - 2 - here) % LANES:
                below = pltpu.roll(below, (LANES - 2 - here) % LANES, 1)
            if here:
                above = pltpu.roll(above, LANES - here, 1)
            f_ref[member, z, 0:width_x, width_y:] = jnp.where(lane >= LANES - 2, below, above)


def shifted(block, member):
    along_x, along_y, _ = LATTICE[member]
    if along_x:
        block = pltpu.roll(block, along_x % block.shape[0], 0)
    if along_y:
        block = pltpu.roll(block, along_y % block.shape[1], 1)
    return block


MOVED = [i for i in range(19) if LATTICE[i][0] or LATTICE[i][1]]


def main_kernel(
    cap, steps, f_ref, x_low, x_high, y_low, y_high, force_0, force_1, own_ref, out_ref, back_ref, before, after, probe_0, probe_1, rows
):
    planes, width_x, width_y = f_ref.shape[1], f_ref.shape[2], f_ref.shape[3]
    tall, wide = before.shape[2], before.shape[3]
    ring_cells(x_low, x_high, y_low, y_high, before)

    def blocks(body, own_body):
        @pl.loop(0, planes * (width_x // 8))
        def _(index):
            z = index // (width_x // 8)
            row = pl.multiple_of((index % (width_x // 8)) * 8, 8)
            for start in range(0, width_y, LANES):
                own_body(z, row, pl.ds(start, LANES), pl.multiple_of(index * 8, 8))
            body(z, row, pl.ds(width_y, LANES))

        @pl.loop(0, planes)
        def _(z):
            for start in range(0, wide, LANES):
                body(z, width_x, pl.ds(start, LANES))

    def force_at(ref, z, row, lanes):
        return [ref[pl.ds(pl.multiple_of((n * planes + z) * tall + row, 8), 8), lanes] for n in range(3)]

    def first_body(source, z, row, lanes):
        at = pl.ds(row, 8)
        f = [source[member, z, at, lanes] for member in range(19)]
        density, momenta = moments(f)
        for member, value in enumerate(collide(f, density, momenta, force_at(force_0, z, row, lanes))):
            before[member, z, at, lanes] = value

    blocks(
        lambda z, row, lanes: first_body(before, z, row, lanes),
        lambda z, row, lanes, flat: first_body(f_ref, z, row, lanes),
    )
    for member in MOVED:
        for z in range(planes):
            after[member, (z + LATTICE[member][2]) % planes] = shifted(before[member, z], member)

    def second_body(z, row, lanes, flat=None):
        at = pl.ds(row, 8)
        f = []
        for member in range(19):
            if member in MOVED:
                f.append(after[member, z, at, lanes])
            else:
                f.append(before[member, lax.rem(z - LATTICE[member][2] + planes, planes), at, lanes])
        density, momenta = moments(f)
        if flat is not None:
            inverse = 1.0 / density
            for number, force in enumerate(force_at(force_0, z, row, lanes)):
                probe_0[pl.ds(pl.multiple_of(number * planes * width_x + flat, 8), 8), lanes] = (
                    momenta[number] + 0.5 * force
                ) * inverse
        for member, value in enumerate(collide(f, density, momenta, force_at(force_1, z, row, lanes))):
            after[member, z, at, lanes] = value

    blocks(second_body, second_body)
    for member in range(19):
        for z in range(planes):
            to = (z + LATTICE[member][2]) % planes
            out_ref[member, to] = shifted(after[member, z], member)[0:width_x, 0:width_y]

    @pl.loop(0, planes * (width_x // 8))
    def _(index):
        z = index // (width_x // 8)
        row = pl.multiple_of((index % (width_x // 8)) * 8, 8)
        flat = pl.multiple_of(index * 8, 8)
        for start in range(0, width_y, LANES):
            lanes = pl.ds(start, LANES)
            density, momenta = moments([out_ref[member, z, pl.ds(row, 8), lanes] for member in range(19)])
            inverse = 1.0 / density
            for number, force in enumerate(force_at(force_1, z, row, lanes)):
                probe_1[pl.ds(pl.multiple_of(number * planes * width_x + flat, 8), 8), lanes] = (
                    momenta[number] + 0.5 * force
                ) * inverse

    for step, probe_ref in enumerate((probe_0, probe_1)):
        first = own_ref[8 * step : 8 * step + 8, :]
        for number, row in enumerate(sample(first, planes, width_x, width_y, probe_ref)):
            rows[steps * number + step : steps * number + step + 1, :] = row
    send_back(cap, rows, back_ref)


def send_back(cap, rows, out_ref):
    devices, steps = out_ref.shape[0], out_ref.shape[1]
    per = LANES // cap
    group = iota((steps, LANES), 1) // cap
    for device in range(devices):
        line, place = device // per, device % per
        total = jnp.zeros((steps, LANES), F32)
        for number in range(3):
            piece = rows[number * steps : (number + 1) * steps, line * LANES : (line + 1) * LANES]
            shift = (number - place) * cap % LANES
            if shift:
                piece = pltpu.roll(piece, shift, 1)
            total = jnp.where(group == number, piece, total)
        out_ref[device] = total


def call(kernel, outs, scratch=(), flops=0, moved=0, limit=40, fetched=(False,)):
    shapes = [jax.ShapeDtypeStruct(shape, kind) for shape, kind in outs]
    specs = [pl.BlockSpec(memory_space=pltpu.HBM if own else pltpu.VMEM) for own in fetched]
    return pl.pallas_call(
        kernel,
        out_shape=shapes,
        scratch_shapes=list(scratch),
        **({"in_specs": specs} if any(fetched) else {}),
        cost_estimate=pl.CostEstimate(flops=flops, bytes_accessed=moved, transcendentals=0),
        compiler_params=pltpu.CompilerParams(vmem_limit_bytes=limit * 1024 * 1024),
    )


def pair(up, down, axis):
    count = lax.axis_size(axis)
    forward = [(i, (i + 1) % count) for i in range(count)]
    backward = [(target, source) for source, target in forward]
    return lax.ppermute(up, axis, forward), lax.ppermute(down, axis, backward)


def local(populations_in, marker_force, marker_frac, marker_cell, marker_tile):
    count_gx, count_gy = lax.axis_size("gx"), lax.axis_size("gy")
    devices = count_gx * count_gy
    steps, owned = marker_force.shape[0], marker_force.shape[2]
    cap = max(2, 2 * owned // devices)
    half, slots = cap // 2, devices * cap
    planes, width_x, width_y = populations_in.shape[1:]
    tall, wide = width_x + RING, width_y + SIDE
    grid = (count_gx, count_gy, width_x, width_y)
    by_comp = lambda x: jnp.transpose(x, (1, 0, 2))
    markers = (
        marker_tile.reshape(steps * owned // LANES, LANES),
        by_comp(marker_cell),
        by_comp(marker_frac),
        by_comp(marker_force),
    )
    message = ((devices, 8, LANES), F32)
    rows = pltpu.VMEM((16, owned), F32)

    def send(outgoing):
        return lax.all_to_all(outgoing, ("gx", "gy"), split_axis=0, concat_axis=0, tiled=True)

    def pack_markers(*refs):
        pack_kernel(grid, steps, cap, *refs)

    lines = 2 * 19 * planes
    face = ((lines, width_y), F32)
    outgoing, slot, x_up, x_down = call(
        pack_markers,
        [message, ((steps, owned), jnp.int32), face, face],
        [
            rows,
            pltpu.VMEM((steps * owned // LANES, LANES), jnp.int32),
            pltpu.VMEM((3, steps, owned), jnp.int32),
            pltpu.VMEM((3, steps, owned), F32),
            pltpu.VMEM((3, steps, owned), F32),
            pltpu.VMEM((19, planes, 8, width_y), F32),
            pltpu.VMEM((19, planes, 8, width_y), F32),
            pltpu.SemaphoreType.DMA((6,)),
        ],
        fetched=(True,) * 5,
        limit=63,
    )(*markers, populations_in)
    arrived = send(outgoing)

    x_low, x_high = pair(x_up, x_down, "gx")
    packed = -(-lines // LANES) * LANES
    y_up, y_down = call(columns_kernel, [((width_x, packed), F32)] * 2)(populations_in)
    y_up, y_down = call(corner_kernel, [((width_x + 8, packed), F32)] * 2)(y_up, y_down, x_low, x_high)
    y_low, y_high = pair(y_up, y_down, "gy")

    field = ((3 * planes * tall, wide), F32)

    def spread_markers(*refs):
        spread_kernel(cap, steps, planes, width_x, width_y, *refs)

    *forces, own, most = call(
        spread_markers, [field] * steps + [((8 * steps, slots), F32), ((8, LANES), F32)], flops=4 * 10**9, moved=10**6
    )(arrived)
    most = most[0, 0]

    def again(state):
        return (state[0] * half).astype(F32) < most

    def more(state):
        turn, *forces = state

        def turn_markers(*refs):
            turn_kernel(grid, steps, cap, *refs)

        def add_markers(*refs):
            more_kernel(cap, steps, planes, width_x, width_y, *refs)

        spec = [pl.BlockSpec(memory_space=pltpu.SMEM)] + [pl.BlockSpec(memory_space=pltpu.VMEM)] * 4
        (outgoing,) = pl.pallas_call(
            turn_markers,
            out_shape=[jax.ShapeDtypeStruct(*message)],
            in_specs=spec,
            scratch_shapes=[rows],
            compiler_params=pltpu.CompilerParams(vmem_limit_bytes=40 * 1024 * 1024),
        )(turn.reshape(1), *markers)
        return (turn + 1, *call(add_markers, [field] * steps)(send(outgoing), *forces))

    _, force_0, force_1 = lax.while_loop(again, more, (jnp.int32(1), *forces))

    def main(*refs):
        main_kernel(cap, steps, *refs)

    own_field = pltpu.VMEM((3 * planes * width_x, width_y), F32)
    extended = pltpu.VMEM((19, planes, tall, wide), F32)
    fields, back = call(
        main,
        [(populations_in.shape, F32), ((devices, steps, LANES), F32)],
        [extended, extended, own_field, own_field, pltpu.VMEM((8, slots), F32)],
    )(populations_in, x_low, x_high, y_low, y_high, force_0, force_1, own)
    returned = send(back)

    def unpack(*refs):
        unpack_kernel(cap, steps, *refs)

    (velocity,) = call(unpack, [((3, steps, owned), F32)])(returned, slot)
    return fields, by_comp(velocity)


def solution(mesh):
    return jax.shard_map(
        local,
        mesh=mesh,
        in_specs=(
            P(None, None, "gx", "gy"),
            P(None, None, ("gx", "gy")),
            P(None, None, ("gx", "gy")),
            P(None, None, ("gx", "gy")),
            P(None, ("gx", "gy"), None),
        ),
        out_specs=(P(None, None, "gx", "gy"), P(None, None, ("gx", "gy"))),
        check_vma=False,
    )
```

```python
import jax
import jax.numpy as jnp
from jax import lax
from jax.experimental import pallas as pl
from jax.experimental.pallas import tpu as pltpu
from jax.sharding import PartitionSpec as P

LATTICE = [
    (0, 0, 0),
    (1, 0, 0),
    (-1, 0, 0),
    (0, 1, 0),
    (0, -1, 0),
    (0, 0, 1),
    (0, 0, -1),
    (1, 1, 0),
    (-1, -1, 0),
    (1, -1, 0),
    (-1, 1, 0),
    (1, 0, 1),
    (-1, 0, -1),
    (1, 0, -1),
    (-1, 0, 1),
    (0, 1, 1),
    (0, -1, -1),
    (0, 1, -1),
    (0, -1, 1),
]
WEIGHTS = [1.0 / 3.0] + [1.0 / 18.0] * 6 + [1.0 / 36.0] * 12
relax_time = 0.8
OMEGA = 1.0 / relax_time
SOURCE = 1.0 - 0.5 / relax_time
LANES = 128

BF = jnp.bfloat16
F32 = jnp.float32


def split2(x):
    high = x.astype(BF)
    low = (x - high.astype(F32)).astype(BF)
    return high, low


def split3(x):
    high = x.astype(BF)
    rest = x - high.astype(F32)
    middle = rest.astype(BF)
    low = (rest - middle.astype(F32)).astype(BF)
    return high, middle, low


def nt(a, b):
    return lax.dot_general(a, b, (((1,), (1,)), ((), ())), preferred_element_type=F32)


def nn(a, b):
    return lax.dot_general(a, b, (((1,), (0,)), ((), ())), preferred_element_type=F32)


def iota(shape, dim):
    return lax.broadcasted_iota(jnp.int32, shape, dim)


RING = 8
SIDE = LANES


def slot_table(slot, slots):
    owned = slot.shape[1]
    return jnp.where(iota((slots, owned), 0) == slot, 1.0, 0.0).astype(BF)


def fetch(pairs, sems):
    copies = [pltpu.make_async_copy(source, target, sems.at[n]) for n, (source, target) in enumerate(pairs)]
    for copy in copies:
        copy.start()
    return copies


def ghosts(step, steps, count_gx, count_gy, width_x, width_y, tiles, cell_x, cell_y):
    reach = steps - step
    along = []
    tiles = tiles.astype(F32)
    gx = jnp.floor((tiles + 0.5) * (1.0 / count_gy))
    for cell, width, place, count in (
        (cell_x, width_x, gx, count_gx),
        (cell_y, width_y, tiles - gx * count_gy, count_gy),
    ):
        above, below = cell >= width - 1 - reach, cell <= reach - 1
        place_up = jnp.where(place == count - 1, 0.0, place + 1.0)
        place_down = jnp.where(place == 0, count - 1.0, place - 1.0)
        along.append(
            (
                jnp.where(above | below, 1.0, 0.0),
                place,
                jnp.where(above, place_up, place_down),
                cell,
                jnp.where(above, cell - width, cell + width),
            )
        )
    (near_x, here_x, there_x, in_x, out_x), (near_y, here_y, there_y, in_y, out_y) = along
    return [
        (jnp.where(near_x > 0, there_x * count_gy + here_y, -1.0), out_x, in_y),
        (jnp.where(near_y > 0, here_x * count_gy + there_y, -1.0), in_x, out_y),
        (jnp.where(near_x * near_y > 0, there_x * count_gy + there_y, -1.0), out_x, out_y),
    ]


def pack(grid, steps, cap, step_rows, out_ref, slot_ref, rows, turn=None):
    count_gx, count_gy, width_x, width_y = grid
    devices, half = count_gx * count_gy, cap // 2
    owned = rows.shape[1]
    slots = devices * cap
    earlier = jnp.where(iota((owned, owned), 0) < iota((owned, owned), 1), 1.0, 0.0).astype(BF)
    column = iota((devices, owned), 0).astype(F32)
    octets, extras, most = [], [], []
    for step in range(steps):
        tiles, values = step_rows(step)
        beside = ghosts(step, steps, *grid, tiles, values[0], values[1])
        member = [jnp.where(column == tile, 1.0, 0.0) for tile in [tiles.astype(F32)] + [b[0] for b in beside]]
        before = nn(jnp.concatenate(member, axis=0).astype(BF), earlier)
        before = [before[n * devices : (n + 1) * devices] for n in range(4)]
        if turn is None:
            rank = jnp.sum(before[0] * member[0], axis=0, keepdims=True)
            slot = tiles * cap + rank.astype(jnp.int32)
            slot_ref[step : step + 1, :] = slot
            rows[...] = jnp.zeros_like(rows)
            for number, value in enumerate(values):
                rows[number : number + 1, :] = value
            packed = nt(jnp.concatenate(split3(rows[...]), axis=0), slot_table(slot, slots))
            packed = packed[0:16] + packed[16:32] + packed[32:48]
            octets.append((packed[0:8], packed[8:16]))
        taken = jnp.zeros((devices, 1), F32)
        extra = jnp.zeros((48, devices * half), F32)
        for number, (tile, cell_x, cell_y) in enumerate(beside):
            rank = jnp.sum((before[number + 1] + taken) * member[number + 1], axis=0, keepdims=True)
            taken = taken + jnp.sum(member[number + 1], axis=1, keepdims=True)
            if turn is not None:
                rank = rank - turn * half
            fits = (tile >= 0) & (rank >= 0) & (rank < half)
            slot = jnp.where(fits, tile * half + rank, -1.0).astype(jnp.int32)
            rows[...] = jnp.zeros_like(rows)
            for place, value in zip((1, 2, 3, 4, 5, 6, 7, 9, 10), [cell_x, cell_y] + values[2:]):
                rows[place : place + 1, :] = value
            extra = extra + nt(jnp.concatenate(split3(rows[...]), axis=0), slot_table(slot, devices * half))
        extra = extra[0:16] + extra[16:32] + extra[32:48]
        extras.append((extra[0:8], extra[8:16]))
        most.append(jnp.max(taken, axis=0, keepdims=True))
    lane, row = iota((8, LANES), 1), iota((8, LANES), 0)

    def placed(octet, device, width, offset):
        line, place = device * width // LANES, device * width % LANES
        piece = octet[:, line * LANES : (line + 1) * LANES]
        shift = (offset - place) % LANES
        if shift:
            piece = pltpu.roll(piece, shift, 1)
        return jnp.where((lane >= offset) & (lane < offset + width), piece, 0.0)

    heading = jnp.zeros((8, LANES), F32)
    for step in range(steps):
        start = (2 * step + 1) * cap + half
        heading = jnp.where((row == 3) & (lane >= start) & (lane < start + half), most[step], heading)
    for device in range(devices):
        block = heading
        for step in range(steps):
            start = 2 * step * cap
            if turn is None:
                block = block + placed(octets[step][0], device, cap, start)
                block = block + placed(octets[step][1], device, cap, start + cap)
            block = block + placed(extras[step][0], device, half, start + cap)
            block = block + placed(extras[step][1], device, half, start + cap + half)
        out_ref[device] = block


def marker_rows(tile_ref, cell_ref, frac_ref, force_ref):
    lines = cell_ref.shape[2] // LANES

    def step_rows(step):
        tiles = jnp.concatenate(
            [tile_ref[step * lines + r : step * lines + r + 1, :] for r in range(lines)], axis=1
        )
        values = [cell_ref[n, step : step + 1, :].astype(F32) for n in range(3)]
        values += [frac_ref[n, step : step + 1, :] for n in range(3)]
        values += [force_ref[n, step : step + 1, :] for n in range(3)]
        return tiles, values

    return step_rows


def pack_kernel(
    grid, steps, cap, tile_in, cell_in, frac_in, force_in, after_ref, out_ref, slot_ref,
    rows, tile_ref, cell_ref, frac_ref, force_ref, sems,
):
    copies = fetch([(tile_in, tile_ref), (cell_in, cell_ref), (frac_in, frac_ref), (force_in, force_ref)], sems)
    for copy in copies:
        copy.wait()
    pack(grid, steps, cap, marker_rows(tile_ref, cell_ref, frac_ref, force_ref), out_ref, slot_ref, rows)


def strips_kernel(f_in, x_up, x_down, near_ref, far_ref, sems):
    planes, width_x = f_in.shape[1], f_in.shape[2]
    copies = fetch(
        [
            (f_in.at[:, :, pl.ds(width_x - 8, 8), :], far_ref),
            (f_in.at[:, :, pl.ds(0, 8), :], near_ref),
        ],
        sems,
    )
    for copy, out, source, start in ((copies[0], x_up, far_ref, 6), (copies[1], x_down, near_ref, 0)):
        copy.wait()
        for plane in range(19 * planes):
            out[2 * plane : 2 * plane + 2, :] = source[plane // planes, plane % planes, start : start + 2, :]


def turn_kernel(grid, steps, cap, turn_ref, tile_ref, cell_ref, frac_ref, force_ref, out_ref, rows):
    step_rows = marker_rows(tile_ref, cell_ref, frac_ref, force_ref)
    pack(grid, steps, cap, step_rows, out_ref, None, rows, turn_ref[0].astype(F32))


def gather(recv_ref, offset, width):
    devices = recv_ref.shape[0]
    per = LANES // width
    group = iota((8, LANES), 1) // width
    pieces = []
    for line in range(devices // per):
        total = jnp.zeros((8, LANES), F32)
        for place in range(per):
            piece = recv_ref[line * per + place]
            shift = (place * width - offset) % LANES
            if shift:
                piece = pltpu.roll(piece, shift, 1)
            total = jnp.where(group == place, piece, total)
        pieces.append(total)
    return jnp.concatenate(pieces, axis=1)


def unpack_kernel(cap, steps, recv_ref, slot_ref, out_ref):
    devices = recv_ref.shape[0]
    per = LANES // cap
    group = iota((steps, LANES), 1) // cap
    comps = []
    for number in range(3):
        pieces = []
        for line in range(devices // per):
            total = jnp.zeros((steps, LANES), F32)
            for place in range(per):
                piece = recv_ref[line * per + place]
                shift = (place - number) * cap % LANES
                if shift:
                    piece = pltpu.roll(piece, shift, 1)
                total = jnp.where(group == place, piece, total)
            pieces.append(total)
        comps.append(jnp.concatenate(pieces, axis=1))
    slots = devices * cap
    for step in range(steps):
        rows = jnp.concatenate([comp[step : step + 1] for comp in comps] + [jnp.zeros((13, slots), F32)], axis=0)
        found = nn(jnp.concatenate(split3(rows), axis=0), slot_table(slot_ref[step : step + 1, :], slots))
        found = found[0:8] + found[16:24] + found[32:40]
        for number in range(3):
            out_ref[number, step : step + 1, :] = found[number : number + 1]


def line_weights(cell, frac, extent):
    grid = iota((extent, cell.shape[1]), 0).astype(F32)
    return jnp.where(grid == cell, 1.0 - frac, jnp.where(grid == cell + 1.0, frac, 0.0))


def y_table(cell, frac, extent):
    grid = iota((extent, cell.shape[1]), 0).astype(F32)
    lower, upper = grid == cell, grid == cell + 1.0
    tables = []
    for low, high in zip(split2(1.0 - frac), split2(frac)):
        low, high = low.astype(F32), high.astype(F32)
        tables.append(jnp.where(lower, low, jnp.where(upper, high, 0.0)).astype(BF))
    return tables


def plane_table(rows, planes, width_x):
    kernel_x = line_weights(rows[0:1], rows[3:4], width_x)
    kernel_z = line_weights(rows[2:3], rows[5:6], 8)
    return [kernel_z[z : z + 1] * kernel_x for z in range(planes)]


def product(table, along_y):
    high, low = split2(table)
    high_y, low_y = along_y
    return nt(
        jnp.concatenate([high, low, high], axis=1), jnp.concatenate([high_y, high_y, low_y], axis=1)
    )


def spread_own(first, second, planes, width_x, width_y, force_ref):
    tall = width_x + RING
    table = jnp.concatenate(plane_table(first, planes, width_x), axis=0)
    along_y = y_table(first[1:2], first[4:5], width_y)
    strengths = (first[6:7], first[7:8], second[0:1])
    found = product(jnp.concatenate([table * strength for strength in strengths], axis=0), along_y)
    for number in range(3 * planes):
        force_ref[number * tall : number * tall + width_x, 0:width_y] = found[number * width_x : (number + 1) * width_x]


def spread_ghosts(first, second, planes, width_x, width_y, force_ref, add):
    tall, wide = width_x + RING, width_y + SIDE
    cell_x = jnp.where(first[1:2] < 0, first[1:2] + tall, first[1:2])
    cell_y = jnp.where(first[2:3] < 0, first[2:3] + wide, first[2:3])
    kernel_x = line_weights(cell_x, first[4:5], tall)
    kernel_z = line_weights(first[3:4], first[6:7], 8)
    along_y = y_table(cell_y, first[5:6], wide)
    side_y = [table[width_y:] for table in along_y]
    ring = [kernel_z[z : z + 1] * kernel_x[width_x:] for z in range(planes)]
    side = [kernel_z[z : z + 1] * kernel_x[0:width_x] for z in range(planes)]
    ring, side = jnp.concatenate(ring, axis=0), jnp.concatenate(side, axis=0)
    strengths = (first[7:8], second[1:2], second[2:3])
    found_ring = product(jnp.concatenate([ring * strength for strength in strengths], axis=0), along_y)
    found_side = product(jnp.concatenate([side * strength for strength in strengths], axis=0), side_y)
    for number in range(3 * planes):
        at = number * tall
        part_ring = found_ring[number * RING : (number + 1) * RING]
        part_side = found_side[number * width_x : (number + 1) * width_x]
        if add:
            part_ring = part_ring + force_ref[at + width_x : at + tall, :]
            part_side = part_side + force_ref[at : at + width_x, width_y:]
        force_ref[at + width_x : at + tall, :] = part_ring
        force_ref[at : at + width_x, width_y:] = part_side


def spread_kernel(cap, steps, planes, width_x, width_y, recv_ref, *outs):
    forces, own_ref, most_ref = outs[:steps], outs[steps], outs[steps + 1]
    half = cap // 2
    most = jnp.float32(0)
    for step in range(steps):
        start = 2 * step * cap
        first = gather(recv_ref, start, cap)
        own_ref[8 * step : 8 * step + 8, :] = first
        second = gather(recv_ref, start + cap, cap)
        spread_own(first, second, planes, width_x, width_y, forces[step])
        first = gather(recv_ref, start + cap, half)
        second = gather(recv_ref, start + cap + half, half)
        spread_ghosts(first, second, planes, width_x, width_y, forces[step], False)
        most = jnp.maximum(most, jnp.max(second[3:4]))
    most_ref[0] = most


def more_kernel(cap, steps, planes, width_x, width_y, recv_ref, *refs):
    half = cap // 2
    for step in range(steps):
        start = (2 * step + 1) * cap
        force_ref = refs[steps + step]
        force_ref[...] = refs[step][...]
        first, second = gather(recv_ref, start, half), gather(recv_ref, start + half, half)
        spread_ghosts(first, second, planes, width_x, width_y, force_ref, True)


def sample(first, planes, width_x, width_y, probe_ref):
    table = jnp.concatenate(plane_table(first, planes, width_x), axis=0)
    along_y = y_table(first[1:2], first[4:5], width_y)
    size = planes * width_x
    high, low = split2(probe_ref[...])
    high_y, low_y = along_y
    found = nn(jnp.concatenate([high, low, high], axis=1), jnp.concatenate([high_y, high_y, low_y], axis=0))
    rows = [jnp.sum(found[n * size : (n + 1) * size] * table, axis=0, keepdims=True) for n in range(3)]
    return rows


def moments(f):
    density = f[0]
    diff = {}
    for member in range(1, 19, 2):
        density = density + (f[member] + f[member + 1])
        diff[member] = f[member] - f[member + 1]
    momenta = []
    for number in range(3):
        total = None
        for member in range(1, 19, 2):
            sign = LATTICE[member][number]
            if sign == 0:
                continue
            if total is None:
                total = diff[member] if sign == 1 else -diff[member]
            else:
                total = total + diff[member] if sign == 1 else total - diff[member]
        momenta.append(total)
    return density, momenta


def dot_c(vector, comps):
    total = None
    for number in range(3):
        if vector[number] == 0:
            continue
        if total is None:
            total = comps[number] if vector[number] == 1 else -comps[number]
        else:
            total = total + comps[number] if vector[number] == 1 else total - comps[number]
    return total


def collide(f, density, momenta, force):
    inverse = 1.0 / density
    speed = [(momenta[n] + 0.5 * force[n]) * inverse for n in range(3)]
    scaled = OMEGA * density
    speed_sq = speed[0] * speed[0] + speed[1] * speed[1] + speed[2] * speed[2]
    along = speed[0] * force[0] + speed[1] * force[1] + speed[2] * force[2]
    base = scaled * (1.0 - 1.5 * speed_sq) - (3.0 * SOURCE) * along
    flow = [scaled * speed[n] for n in range(3)]
    pull = [(3.0 * SOURCE) * force[n] for n in range(3)]
    linear = [3.0 * flow[n] + pull[n] for n in range(3)]
    square = [4.5 * flow[n] + 3.0 * pull[n] for n in range(3)]
    posts = [(1.0 - OMEGA) * f[0] + WEIGHTS[0] * base]
    for member in range(1, 19, 2):
        vector = LATTICE[member]
        even = WEIGHTS[member] * (base + dot_c(vector, speed) * dot_c(vector, square))
        odd = WEIGHTS[member] * dot_c(vector, linear)
        posts.append((1.0 - OMEGA) * f[member] + (even + odd))
        posts.append((1.0 - OMEGA) * f[member + 1] + (even - odd))
    return posts


def columns_kernel(f_in, after_ref, up, down, far_ref, near_ref, sems):
    planes, width_x, width_y = f_in.shape[1], f_in.shape[2], f_in.shape[3]
    copies = fetch(
        [
            (f_in.at[:, :, :, pl.ds(width_y - LANES, LANES)], far_ref),
            (f_in.at[:, :, :, pl.ds(0, LANES)], near_ref),
        ],
        sems,
    )
    lane = iota((width_x, LANES), 1)
    for copy, out, source, at in ((copies[0], up, far_ref, LANES - 2), (copies[1], down, near_ref, 0)):
        copy.wait()
        lines = out.shape[1] // LANES
        totals = [jnp.zeros((width_x, LANES), F32) for _ in range(lines)]
        for plane in range(19 * planes):
            line, target = divmod(2 * plane, LANES)
            block = source[plane // planes, plane % planes]
            shift = (target - at) % LANES
            if shift:
                block = pltpu.roll(block, shift, 1)
            totals[line] = jnp.where((lane == target) | (lane == target + 1), block, totals[line])
        for line in range(lines):
            out[:, line * LANES : (line + 1) * LANES] = totals[line]


def corner_kernel(up, down, x_low, x_high, out_up, out_down):
    width_x, width_y = up.shape[0], x_low.shape[1]
    count = x_low.shape[0]
    for source, out, start, at in ((up, out_up, width_y - LANES, LANES - 2), (down, out_down, 0, 0)):
        out[0:width_x, :] = source[...]
        out[width_x:, :] = jnp.zeros((out.shape[0] - width_x, out.shape[1]), F32)
        for number, halo in enumerate((x_low, x_high)):
            for line in range(out.shape[1] // LANES):
                last = min(count, (line + 1) * LANES)
                block = halo[line * LANES : last, start : start + LANES]
                if last < (line + 1) * LANES:
                    block = jnp.concatenate([block, jnp.zeros(((line + 1) * LANES - last, LANES), F32)], axis=0)
                turned = jnp.transpose(block)
                row = width_x + 2 * number
                out[row : row + 2, line * LANES : (line + 1) * LANES] = turned[at : at + 2]


def ring_cells(x_low, x_high, y_low, y_high, f_ref):
    planes, tall, wide = f_ref.shape[1], f_ref.shape[2], f_ref.shape[3]
    width_x, width_y = tall - RING, wide - SIDE
    lane = iota((width_x, LANES), 1)
    wide_lane = iota((LANES, LANES), 1)
    for line in range(y_low.shape[1] // LANES):
        at = slice(line * LANES, (line + 1) * LANES)
        pad = jnp.zeros((LANES - 8, LANES), F32)
        low = jnp.transpose(jnp.concatenate([y_low[width_x:, at], pad], axis=0))
        high = jnp.transpose(jnp.concatenate([y_high[width_x:, at], pad], axis=0))
        corner_low = jnp.where(wide_lane >= LANES - 2, pltpu.roll(low, LANES - 2, 1), high)
        corner_high = jnp.where(
            wide_lane >= LANES - 2, pltpu.roll(low, LANES - 4, 1), pltpu.roll(high, LANES - 2, 1)
        )
        for plane in range(line * LANES // 2, min((line + 1) * LANES // 2, 19 * planes)):
            member, z = divmod(plane, planes)
            here = 2 * plane - line * LANES
            f_ref[member, z, tall - 2 : tall, 0:width_y] = x_low[2 * plane : 2 * plane + 2, :]
            f_ref[member, z, width_x : width_x + 2, 0:width_y] = x_high[2 * plane : 2 * plane + 2, :]
            f_ref[member, z, tall - 2 : tall, width_y:] = corner_low[here : here + 2]
            f_ref[member, z, width_x : width_x + 2, width_y:] = corner_high[here : here + 2]
            below, above = y_low[0:width_x, at], y_high[0:width_x, at]
            if (LANES - 2 - here) % LANES:
                below = pltpu.roll(below, (LANES - 2 - here) % LANES, 1)
            if here:
                above = pltpu.roll(above, LANES - here, 1)
            f_ref[member, z, 0:width_x, width_y:] = jnp.where(lane >= LANES - 2, below, above)


def shifted(block, member):
    along_x, along_y, _ = LATTICE[member]
    if along_x:
        block = pltpu.roll(block, along_x % block.shape[0], 0)
    if along_y:
        block = pltpu.roll(block, along_y % block.shape[1], 1)
    return block


MOVED = [i for i in range(19) if LATTICE[i][0] or LATTICE[i][1]]


def main_kernel(
    cap, steps, f_in, x_low, x_high, y_low, y_high, force_0, force_1, own_ref, out_ref, back_ref,
    before, after, probe_0, probe_1, rows, sems,
):
    planes, width_x, width_y = f_in.shape[1], f_in.shape[2], f_in.shape[3]
    tall, wide = before.shape[2], before.shape[3]
    copies = fetch(
        [
            (f_in.at[:, z], before.at[:, z, pl.ds(0, width_x), pl.ds(0, width_y)])
            for z in range(planes)
        ],
        sems,
    )
    ring_cells(x_low, x_high, y_low, y_high, before)

    def blocks(body, own_body):
        @pl.loop(0, planes * (width_x // 8))
        def _(index):
            z = index // (width_x // 8)
            row = pl.multiple_of((index % (width_x // 8)) * 8, 8)
            for start in range(0, width_y, LANES):
                own_body(z, row, pl.ds(start, LANES), pl.multiple_of(index * 8, 8))
            body(z, row, pl.ds(width_y, LANES))

        @pl.loop(0, planes)
        def _(z):
            for start in range(0, wide, LANES):
                body(z, width_x, pl.ds(start, LANES))

    def force_at(ref, z, row, lanes):
        return [ref[pl.ds(pl.multiple_of((n * planes + z) * tall + row, 8), 8), lanes] for n in range(3)]

    def first_body(z, row, lanes, flat=None):
        at = pl.ds(row, 8)
        f = [before[member, z, at, lanes] for member in range(19)]
        density, momenta = moments(f)
        for member, value in enumerate(collide(f, density, momenta, force_at(force_0, z, row, lanes))):
            before[member, z, at, lanes] = value

    for copy in copies:
        copy.wait()
    blocks(first_body, first_body)
    for member in MOVED:
        for z in range(planes):
            after[member, (z + LATTICE[member][2]) % planes] = shifted(before[member, z], member)

    def second_body(z, row, lanes, flat=None):
        at = pl.ds(row, 8)
        f = []
        for member in range(19):
            if member in MOVED:
                f.append(after[member, z, at, lanes])
            else:
                f.append(before[member, lax.rem(z - LATTICE[member][2] + planes, planes), at, lanes])
        density, momenta = moments(f)
        if flat is not None:
            inverse = 1.0 / density
            for number, force in enumerate(force_at(force_0, z, row, lanes)):
                probe_0[pl.ds(pl.multiple_of(number * planes * width_x + flat, 8), 8), lanes] = (
                    momenta[number] + 0.5 * force
                ) * inverse
        for member, value in enumerate(collide(f, density, momenta, force_at(force_1, z, row, lanes))):
            after[member, z, at, lanes] = value

    blocks(second_body, second_body)
    for member in range(19):
        for z in range(planes):
            to = (z + LATTICE[member][2]) % planes
            out_ref[member, to] = shifted(after[member, z], member)[0:width_x, 0:width_y]

    @pl.loop(0, planes * (width_x // 8))
    def _(index):
        z = index // (width_x // 8)
        row = pl.multiple_of((index % (width_x // 8)) * 8, 8)
        flat = pl.multiple_of(index * 8, 8)
        for start in range(0, width_y, LANES):
            lanes = pl.ds(start, LANES)
            density, momenta = moments([out_ref[member, z, pl.ds(row, 8), lanes] for member in range(19)])
            inverse = 1.0 / density
            for number, force in enumerate(force_at(force_1, z, row, lanes)):
                probe_1[pl.ds(pl.multiple_of(number * planes * width_x + flat, 8), 8), lanes] = (
                    momenta[number] + 0.5 * force
                ) * inverse

    for step, probe_ref in enumerate((probe_0, probe_1)):
        first = own_ref[8 * step : 8 * step + 8, :]
        for number, row in enumerate(sample(first, planes, width_x, width_y, probe_ref)):
            rows[steps * number + step : steps * number + step + 1, :] = row
    send_back(cap, rows, back_ref)


def send_back(cap, rows, out_ref):
    devices, steps = out_ref.shape[0], out_ref.shape[1]
    per = LANES // cap
    group = iota((steps, LANES), 1) // cap
    for device in range(devices):
        line, place = device // per, device % per
        total = jnp.zeros((steps, LANES), F32)
        for number in range(3):
            piece = rows[number * steps : (number + 1) * steps, line * LANES : (line + 1) * LANES]
            shift = (number - place) * cap % LANES
            if shift:
                piece = pltpu.roll(piece, shift, 1)
            total = jnp.where(group == number, piece, total)
        out_ref[device] = total


def call(kernel, outs, scratch=(), flops=0, moved=0, limit=40, fetched=(False,)):
    shapes = [jax.ShapeDtypeStruct(shape, kind) for shape, kind in outs]
    out_specs = [pl.BlockSpec(memory_space=pltpu.SMEM if len(shape) == 1 else pltpu.VMEM) for shape, _ in outs]
    specs = [pl.BlockSpec(memory_space=pltpu.HBM if own else pltpu.VMEM) for own in fetched]
    return pl.pallas_call(
        kernel,
        out_shape=shapes,
        out_specs=out_specs,
        scratch_shapes=list(scratch),
        **({"in_specs": specs} if any(fetched) else {}),
        cost_estimate=pl.CostEstimate(flops=flops, bytes_accessed=moved, transcendentals=0),
        compiler_params=pltpu.CompilerParams(vmem_limit_bytes=limit * 1024 * 1024),
    )


def pair(up, down, axis):
    count = lax.axis_size(axis)
    forward = [(i, (i + 1) % count) for i in range(count)]
    backward = [(target, source) for source, target in forward]
    return lax.ppermute(up, axis, forward), lax.ppermute(down, axis, backward)


def local(populations_in, marker_force, marker_frac, marker_cell, marker_tile):
    count_gx, count_gy = lax.axis_size("gx"), lax.axis_size("gy")
    devices = count_gx * count_gy
    steps, owned = marker_force.shape[0], marker_force.shape[2]
    cap = max(2, 2 * owned // devices)
    half, slots = cap // 2, devices * cap
    planes, width_x, width_y = populations_in.shape[1:]
    tall, wide = width_x + RING, width_y + SIDE
    grid = (count_gx, count_gy, width_x, width_y)
    by_comp = lambda x: jnp.transpose(x, (1, 0, 2))
    markers = (
        marker_tile.reshape(steps * owned // LANES, LANES),
        by_comp(marker_cell),
        by_comp(marker_frac),
        by_comp(marker_force),
    )
    message = ((devices, 8, LANES), F32)
    rows = pltpu.VMEM((16, owned), F32)

    def send(outgoing):
        return lax.all_to_all(outgoing, ("gx", "gy"), split_axis=0, concat_axis=0, tiled=True)

    def pack_markers(*refs):
        pack_kernel(grid, steps, cap, *refs)

    lines = 2 * 19 * planes
    face = ((lines, width_y), F32)
    x_up, x_down = call(
        strips_kernel,
        [face, face],
        [
            pltpu.VMEM((19, planes, 8, width_y), F32),
            pltpu.VMEM((19, planes, 8, width_y), F32),
            pltpu.SemaphoreType.DMA((2,)),
        ],
        fetched=(True,),
        limit=63,
    )(populations_in)
    outgoing, slot = call(
        pack_markers,
        [message, ((steps, owned), jnp.int32)],
        [
            rows,
            pltpu.VMEM((steps * owned // LANES, LANES), jnp.int32),
            pltpu.VMEM((3, steps, owned), jnp.int32),
            pltpu.VMEM((3, steps, owned), F32),
            pltpu.VMEM((3, steps, owned), F32),
            pltpu.SemaphoreType.DMA((4,)),
        ],
        fetched=(True,) * 5,
        limit=63,
    )(*markers, x_up)
    arrived = send(outgoing)

    x_low, x_high = pair(x_up, x_down, "gx")
    packed = -(-lines // LANES) * LANES
    y_up, y_down = call(
        columns_kernel,
        [((width_x, packed), F32)] * 2,
        [
            pltpu.VMEM((19, planes, width_x, LANES), F32),
            pltpu.VMEM((19, planes, width_x, LANES), F32),
            pltpu.SemaphoreType.DMA((2,)),
        ],
        fetched=(True,) * 2,
        limit=63,
    )(populations_in, slot)
    y_up, y_down = call(corner_kernel, [((width_x + 8, packed), F32)] * 2)(y_up, y_down, x_low, x_high)
    y_low, y_high = pair(y_up, y_down, "gy")

    field = ((3 * planes * tall, wide), F32)

    def spread_markers(*refs):
        spread_kernel(cap, steps, planes, width_x, width_y, *refs)

    *forces, own, most = call(
        spread_markers, [field] * steps + [((8 * steps, slots), F32), ((1,), F32)], flops=4 * 10**9, moved=10**6
    )(arrived)
    most = most.reshape(())

    def again(state):
        return (state[0] * half).astype(F32) < most

    def more(state):
        turn, *forces = state

        def turn_markers(*refs):
            turn_kernel(grid, steps, cap, *refs)

        def add_markers(*refs):
            more_kernel(cap, steps, planes, width_x, width_y, *refs)

        spec = [pl.BlockSpec(memory_space=pltpu.SMEM)] + [pl.BlockSpec(memory_space=pltpu.VMEM)] * 4
        (outgoing,) = pl.pallas_call(
            turn_markers,
            out_shape=[jax.ShapeDtypeStruct(*message)],
            in_specs=spec,
            scratch_shapes=[rows],
            compiler_params=pltpu.CompilerParams(vmem_limit_bytes=40 * 1024 * 1024),
        )(turn.reshape(1), *markers)
        return (turn + 1, *call(add_markers, [field] * steps)(send(outgoing), *forces))

    _, force_0, force_1 = lax.while_loop(again, more, (jnp.int32(1), *forces))

    def main(*refs):
        main_kernel(cap, steps, *refs)

    own_field = pltpu.VMEM((3 * planes * width_x, width_y), F32)
    extended = pltpu.VMEM((19, planes, tall, wide), F32)
    fields, back = call(
        main,
        [(populations_in.shape, F32), ((devices, steps, LANES), F32)],
        [extended, extended, own_field, own_field, pltpu.VMEM((8, slots), F32), pltpu.SemaphoreType.DMA((planes,))],
        fetched=(True,) + (False,) * 7,
        limit=50,
    )(populations_in, x_low, x_high, y_low, y_high, force_0, force_1, own)
    returned = send(back)

    def unpack(*refs):
        unpack_kernel(cap, steps, *refs)

    (velocity,) = call(unpack, [((3, steps, owned), F32)])(returned, slot)
    return fields, by_comp(velocity)


def solution(mesh):
    return jax.shard_map(
        local,
        mesh=mesh,
        in_specs=(
            P(None, None, "gx", "gy"),
            P(None, None, ("gx", "gy")),
            P(None, None, ("gx", "gy")),
            P(None, None, ("gx", "gy")),
            P(None, ("gx", "gy"), None),
        ),
        out_specs=(P(None, None, "gx", "gy"), P(None, None, ("gx", "gy"))),
        check_vma=False,
    )
```

```python
import jax
import jax.numpy as jnp
from jax import lax
from jax.experimental import pallas as pl
from jax.experimental.pallas import tpu as pltpu
from jax.sharding import PartitionSpec as P

LATTICE = [
    (0, 0, 0),
    (1, 0, 0),
    (-1, 0, 0),
    (0, 1, 0),
    (0, -1, 0),
    (0, 0, 1),
    (0, 0, -1),
    (1, 1, 0),
    (-1, -1, 0),
    (1, -1, 0),
    (-1, 1, 0),
    (1, 0, 1),
    (-1, 0, -1),
    (1, 0, -1),
    (-1, 0, 1),
    (0, 1, 1),
    (0, -1, -1),
    (0, 1, -1),
    (0, -1, 1),
]
WEIGHTS = [1.0 / 3.0] + [1.0 / 18.0] * 6 + [1.0 / 36.0] * 12
relax_time = 0.8
OMEGA = 1.0 / relax_time
SOURCE = 1.0 - 0.5 / relax_time
LANES = 128

BF = jnp.bfloat16
F32 = jnp.float32


def split2(x):
    high = x.astype(BF)
    low = (x - high.astype(F32)).astype(BF)
    return high, low


def split3(x):
    high = x.astype(BF)
    rest = x - high.astype(F32)
    middle = rest.astype(BF)
    low = (rest - middle.astype(F32)).astype(BF)
    return high, middle, low


def nt(a, b):
    return lax.dot_general(a, b, (((1,), (1,)), ((), ())), preferred_element_type=F32)


def nn(a, b):
    return lax.dot_general(a, b, (((1,), (0,)), ((), ())), preferred_element_type=F32)


def iota(shape, dim):
    return lax.broadcasted_iota(jnp.int32, shape, dim)


RING = 8
SIDE = LANES


def slot_table(slot, slots):
    owned = slot.shape[1]
    return jnp.where(iota((slots, owned), 0) == slot, 1.0, 0.0).astype(BF)


def fetch(pairs, sems):
    copies = [pltpu.make_async_copy(source, target, sems.at[n]) for n, (source, target) in enumerate(pairs)]
    for copy in copies:
        copy.start()
    return copies


def ghosts(step, steps, count_gx, count_gy, width_x, width_y, tiles, cell_x, cell_y):
    reach = steps - step
    tiles = tiles.astype(F32)
    gx = jnp.floor((tiles + 0.5) * (1.0 / count_gy))
    along = []
    for cell, width, place, count in (
        (cell_x, width_x, gx, count_gx),
        (cell_y, width_y, tiles - gx * count_gy, count_gy),
    ):
        above, below = cell >= width - 1 - reach, cell <= reach - 1
        place_up = jnp.where(place == count - 1, 0.0, place + 1.0)
        place_down = jnp.where(place == 0, count - 1.0, place - 1.0)
        along.append((jnp.where(above | below, 1.0, 0.0), place, jnp.where(above, place_up, place_down)))
    (near_x, here_x, there_x), (near_y, here_y, there_y) = along
    return [
        jnp.where(near_x > 0, there_x * count_gy + here_y, -1.0),
        jnp.where(near_y > 0, here_x * count_gy + there_y, -1.0),
        jnp.where(near_x * near_y > 0, there_x * count_gy + there_y, -1.0),
    ]


def pack(grid, steps, cap, step_rows, out_ref, slot_ref, rows, turn=None):
    count_gx, count_gy, width_x, width_y = grid
    devices, half = count_gx * count_gy, cap // 2
    owned = rows.shape[1]
    slots, spare = devices * cap, devices * half
    earlier = jnp.where(iota((owned, owned), 0) < iota((owned, owned), 1), 1.0, 0.0).astype(BF)
    column = iota((devices, owned), 0).astype(F32)
    octets, extras, most = [], [], []
    given = [step_rows(step) for step in range(steps)]
    asked = []
    for step, (tiles, values) in enumerate(given):
        asked.append([tiles.astype(F32)] + ghosts(step, steps, *grid, tiles, values[0], values[1]))
    member = [[jnp.where(column == tile, 1.0, 0.0) for tile in tiles] for tiles in asked]
    before = nn(jnp.concatenate(sum(member, []), axis=0).astype(BF), earlier)
    before = [before[n * devices : (n + 1) * devices] for n in range(4 * steps)]
    for step, (tiles, values) in enumerate(given):
        if turn is None:
            rank = jnp.sum(before[4 * step] * member[step][0], axis=0, keepdims=True)
            slot = tiles * cap + rank.astype(jnp.int32)
            slot_ref[step : step + 1, :] = slot
            rows[...] = jnp.zeros_like(rows)
            for number, value in enumerate(values):
                rows[number : number + 1, :] = value
            packed = nt(jnp.concatenate(split3(rows[...]), axis=0), slot_table(slot, slots))
            packed = packed[0:16] + packed[16:32] + packed[32:48]
            octets.append((packed[0:8], packed[8:16]))
        taken = [jnp.zeros((devices, 1), F32)]
        places = []
        for number in range(1, 4):
            here = member[step][number]
            rank = jnp.sum((before[4 * step + number] + taken[-1]) * here, axis=0, keepdims=True)
            taken.append(taken[-1] + jnp.sum(here, axis=1, keepdims=True))
            if turn is not None:
                rank = rank - turn * half
            tile = asked[step][number]
            places.append(jnp.where((tile >= 0) & (rank >= 0) & (rank < half), tile * half + rank, -1.0).astype(jnp.int32))
        grid_slots = iota((spare, owned), 0)
        chosen = (grid_slots == places[0]) | (grid_slots == places[1]) | (grid_slots == places[2])
        rows[...] = jnp.zeros_like(rows)
        for place, value in zip((1, 2, 3, 4, 5, 6, 7, 9, 10), values):
            rows[place : place + 1, :] = value
        extra = nt(jnp.concatenate(split3(rows[...]), axis=0), jnp.where(chosen, 1.0, 0.0).astype(BF))
        extra = extra[0:16] + extra[16:32] + extra[32:48]
        lanes, sender = iota((devices, spare), 1), iota((devices, spare), 0)
        ends = [
            jnp.sum(jnp.where(lanes // half == sender, end, 0.0), axis=0, keepdims=True) for end in (taken[1], taken[2])
        ]
        rank = (iota((1, spare), 1) % half).astype(F32)
        if turn is not None:
            rank = rank + turn * half
        in_x = (rank < ends[0]) | (rank >= ends[1])
        in_y = rank >= ends[0]
        first = []
        for cell, width, moved in ((extra[1:2], width_x, in_x), (extra[2:3], width_y, in_y)):
            first.append(cell + jnp.where(moved, jnp.where(cell * 2 < width, width * 1.0, -1.0 * width), 0.0))
        extras.append((jnp.concatenate([extra[0:1]] + first + [extra[3:8]], axis=0), extra[8:16]))
        most.append(jnp.max(taken[3], axis=0, keepdims=True))
    lane, row = iota((8, LANES), 1), iota((8, LANES), 0)

    def placed(octet, device, width, offset):
        line, place = device * width // LANES, device * width % LANES
        piece = octet[:, line * LANES : (line + 1) * LANES]
        shift = (offset - place) % LANES
        if shift:
            piece = pltpu.roll(piece, shift, 1)
        return jnp.where((lane >= offset) & (lane < offset + width), piece, 0.0)

    heading = jnp.zeros((8, LANES), F32)
    for step in range(steps):
        start = (2 * step + 1) * cap + half
        heading = jnp.where((row == 3) & (lane >= start) & (lane < start + half), most[step], heading)
    for device in range(devices):
        block = heading
        for step in range(steps):
            start = 2 * step * cap
            if turn is None:
                block = block + placed(octets[step][0], device, cap, start)
                block = block + placed(octets[step][1], device, cap, start + cap)
            block = block + placed(extras[step][0], device, half, start + cap)
            block = block + placed(extras[step][1], device, half, start + cap + half)
        out_ref[device] = block


def marker_rows(tile_ref, cell_ref, frac_ref, force_ref):
    lines = cell_ref.shape[2] // LANES

    def step_rows(step):
        tiles = jnp.concatenate(
            [tile_ref[step * lines + r : step * lines + r + 1, :] for r in range(lines)], axis=1
        )
        values = [cell_ref[n, step : step + 1, :].astype(F32) for n in range(3)]
        values += [frac_ref[n, step : step + 1, :] for n in range(3)]
        values += [force_ref[n, step : step + 1, :] for n in range(3)]
        return tiles, values

    return step_rows


def pack_kernel(
    grid, steps, cap, tile_in, cell_in, frac_in, force_in, out_ref, slot_ref,
    rows, tile_ref, cell_ref, frac_ref, force_ref, sems,
):
    copies = fetch([(tile_in, tile_ref), (cell_in, cell_ref), (frac_in, frac_ref), (force_in, force_ref)], sems)
    for copy in copies:
        copy.wait()
    pack(grid, steps, cap, marker_rows(tile_ref, cell_ref, frac_ref, force_ref), out_ref, slot_ref, rows)


def columns_kernel(f_in, after_ref, up, down, far_ref, near_ref, sems):
    width_y = f_in.shape[3]
    copies = fetch(
        [
            (f_in.at[:, :, :, pl.ds(width_y - LANES, LANES)], far_ref),
            (f_in.at[:, :, :, pl.ds(0, LANES)], near_ref),
        ],
        sems,
    )
    for copy, out, source, at in ((copies[0], up, far_ref, LANES - 2), (copies[1], down, near_ref, 0)):
        copy.wait()
        columns(source, out, at)


def face_rows(members, planes):
    first = 19 * planes
    second = {member: first + n * planes for n, member in enumerate(members)}
    return first, second, first + len(members) * planes


def strips_kernel(f_in, after_ref, x_up, x_down, near_ref, far_ref, sems):
    planes, width_x = f_in.shape[1], f_in.shape[2]
    copies = fetch(
        [
            (f_in.at[:, :, pl.ds(width_x - 8, 8), :], far_ref),
            (f_in.at[:, :, pl.ds(0, 8), :], near_ref),
        ],
        sems,
    )
    for copy, out, source, members, row, inner in (
        (copies[0], x_up, far_ref, X_UP, 7, 6),
        (copies[1], x_down, near_ref, X_DOWN, 0, 1),
    ):
        copy.wait()
        _, second, third = face_rows(members, planes)
        for z in range(planes):
            for member in range(19):
                at = member * planes + z
                out[at : at + 1, :] = source[member, z, row : row + 1, :]
            for member, at in second.items():
                out[at + z : at + z + 1, :] = source[member, z, inner : inner + 1, :]
            density, momenta = moments([source[member, z] for member in range(19)])
            for number, value in enumerate([density] + momenta):
                at = third + number * planes + z
                out[at : at + 1, :] = value[inner : inner + 1]


def turn_kernel(grid, steps, cap, turn_ref, tile_ref, cell_ref, frac_ref, force_ref, out_ref, rows):
    step_rows = marker_rows(tile_ref, cell_ref, frac_ref, force_ref)
    pack(grid, steps, cap, step_rows, out_ref, None, rows, turn_ref[0].astype(F32))


def gather(recv_ref, offset, width):
    devices = recv_ref.shape[0]
    per = LANES // width
    group = iota((8, LANES), 1) // width
    pieces = []
    for line in range(devices // per):
        total = jnp.zeros((8, LANES), F32)
        for place in range(per):
            piece = recv_ref[line * per + place]
            shift = (place * width - offset) % LANES
            if shift:
                piece = pltpu.roll(piece, shift, 1)
            total = jnp.where(group == place, piece, total)
        pieces.append(total)
    return jnp.concatenate(pieces, axis=1)


def unpack_kernel(cap, steps, recv_ref, slot_ref, out_ref):
    devices = recv_ref.shape[0]
    per = LANES // cap
    group = iota((steps, LANES), 1) // cap
    comps = []
    for number in range(3):
        pieces = []
        for line in range(devices // per):
            total = jnp.zeros((steps, LANES), F32)
            for place in range(per):
                piece = recv_ref[line * per + place]
                shift = (place - number) * cap % LANES
                if shift:
                    piece = pltpu.roll(piece, shift, 1)
                total = jnp.where(group == place, piece, total)
            pieces.append(total)
        comps.append(jnp.concatenate(pieces, axis=1))
    slots = devices * cap
    for step in range(steps):
        rows = jnp.concatenate([comp[step : step + 1] for comp in comps] + [jnp.zeros((13, slots), F32)], axis=0)
        found = nn(jnp.concatenate(split3(rows), axis=0), slot_table(slot_ref[step : step + 1, :], slots))
        found = found[0:8] + found[16:24] + found[32:40]
        for number in range(3):
            out_ref[number, step : step + 1, :] = found[number : number + 1]


def line_weights(cell, frac, extent):
    grid = iota((extent, cell.shape[1]), 0).astype(F32)
    return jnp.where(grid == cell, 1.0 - frac, jnp.where(grid == cell + 1.0, frac, 0.0))


def y_table(cell, frac, extent):
    grid = iota((extent, cell.shape[1]), 0).astype(F32)
    lower, upper = grid == cell, grid == cell + 1.0
    tables = []
    for low, high in zip(split2(1.0 - frac), split2(frac)):
        low, high = low.astype(F32), high.astype(F32)
        tables.append(jnp.where(lower, low, jnp.where(upper, high, 0.0)).astype(BF))
    return tables


def plane_table(rows, planes, width_x):
    kernel_x = line_weights(rows[0:1], rows[3:4], width_x)
    kernel_z = line_weights(rows[2:3], rows[5:6], 8)
    return [kernel_z[z : z + 1] * kernel_x for z in range(planes)]


def product(table, along_y):
    high, low = split2(table)
    high_y, low_y = along_y
    return nt(
        jnp.concatenate([high, low, high], axis=1), jnp.concatenate([high_y, high_y, low_y], axis=1)
    )


def spread_own(first, second, planes, width_x, width_y, force_ref):
    tall = width_x + RING
    table = jnp.concatenate(plane_table(first, planes, width_x), axis=0)
    along_y = y_table(first[1:2], first[4:5], width_y)
    strengths = (first[6:7], first[7:8], second[0:1])
    found = product(jnp.concatenate([table * strength for strength in strengths], axis=0), along_y)
    for number in range(3 * planes):
        force_ref[number * tall : number * tall + width_x, 0:width_y] = found[number * width_x : (number + 1) * width_x]


def spread_ghosts(first, second, planes, width_x, width_y, force_ref, add):
    tall, wide = width_x + RING, width_y + SIDE
    cell_x = jnp.where(first[1:2] < 0, first[1:2] + tall, first[1:2])
    cell_y = jnp.where(first[2:3] < 0, first[2:3] + wide, first[2:3])
    kernel_x = line_weights(cell_x, first[4:5], tall)
    kernel_z = line_weights(first[3:4], first[6:7], 8)
    along_y = y_table(cell_y, first[5:6], wide)
    side_y = [table[width_y:] for table in along_y]
    ring = [kernel_z[z : z + 1] * kernel_x[width_x:] for z in range(planes)]
    side = [kernel_z[z : z + 1] * kernel_x[0:width_x] for z in range(planes)]
    ring, side = jnp.concatenate(ring, axis=0), jnp.concatenate(side, axis=0)
    strengths = (first[7:8], second[1:2], second[2:3])
    found_ring = product(jnp.concatenate([ring * strength for strength in strengths], axis=0), along_y)
    found_side = product(jnp.concatenate([side * strength for strength in strengths], axis=0), side_y)
    for number in range(3 * planes):
        at = number * tall
        part_ring = found_ring[number * RING : (number + 1) * RING]
        part_side = found_side[number * width_x : (number + 1) * width_x]
        if add:
            part_ring = part_ring + force_ref[at + width_x : at + tall, :]
            part_side = part_side + force_ref[at : at + width_x, width_y:]
        force_ref[at + width_x : at + tall, :] = part_ring
        force_ref[at : at + width_x, width_y:] = part_side


def spread_kernel(cap, step, planes, width_x, width_y, recv_ref, *refs):
    force_ref, own_ref, turns_ref = refs[-3:]
    start, half = 2 * step * cap, cap // 2
    first = gather(recv_ref, start, cap)
    own_ref[...] = first
    second = gather(recv_ref, start + cap, cap)
    spread_own(first, second, planes, width_x, width_y, force_ref)
    first = gather(recv_ref, start + cap, half)
    second = gather(recv_ref, start + cap + half, half)
    spread_ghosts(first, second, planes, width_x, width_y, force_ref, False)
    turns = (jnp.max(second[3:4]).astype(jnp.int32) + half - 1) // half
    turns_ref[0] = jnp.maximum(turns, refs[0][0]) if step else turns


def more_kernel(cap, steps, planes, width_x, width_y, recv_ref, *refs):
    half = cap // 2
    for step in range(steps):
        start = (2 * step + 1) * cap
        force_ref = refs[steps + step]
        force_ref[...] = refs[step][...]
        first, second = gather(recv_ref, start, half), gather(recv_ref, start + half, half)
        spread_ghosts(first, second, planes, width_x, width_y, force_ref, True)


def sample(first, planes, width_x, width_y, probe_ref):
    table = jnp.concatenate(plane_table(first, planes, width_x), axis=0)
    along_y = y_table(first[1:2], first[4:5], width_y)
    size = planes * width_x
    high, low = split2(probe_ref[...])
    high_y, low_y = along_y
    found = nn(jnp.concatenate([high, low, high], axis=1), jnp.concatenate([high_y, high_y, low_y], axis=0))
    rows = [jnp.sum(found[n * size : (n + 1) * size] * table, axis=0, keepdims=True) for n in range(3)]
    return rows


def moments(f):
    density = f[0]
    diff = {}
    for member in range(1, 19, 2):
        density = density + (f[member] + f[member + 1])
        diff[member] = f[member] - f[member + 1]
    momenta = []
    for number in range(3):
        total = None
        for member in range(1, 19, 2):
            sign = LATTICE[member][number]
            if sign == 0:
                continue
            if total is None:
                total = diff[member] if sign == 1 else -diff[member]
            else:
                total = total + diff[member] if sign == 1 else total - diff[member]
        momenta.append(total)
    return density, momenta


def dot_c(vector, comps):
    total = None
    for number in range(3):
        if vector[number] == 0:
            continue
        if total is None:
            total = comps[number] if vector[number] == 1 else -comps[number]
        else:
            total = total + comps[number] if vector[number] == 1 else total - comps[number]
    return total


def collide(f, density, momenta, force):
    inverse = 1.0 / density
    speed = [(momenta[n] + 0.5 * force[n]) * inverse for n in range(3)]
    scaled = OMEGA * density
    speed_sq = speed[0] * speed[0] + speed[1] * speed[1] + speed[2] * speed[2]
    along = speed[0] * force[0] + speed[1] * force[1] + speed[2] * force[2]
    base = scaled * (1.0 - 1.5 * speed_sq) - (3.0 * SOURCE) * along
    flow = [scaled * speed[n] for n in range(3)]
    pull = [(3.0 * SOURCE) * force[n] for n in range(3)]
    linear = [3.0 * flow[n] + pull[n] for n in range(3)]
    square = [4.5 * flow[n] + 3.0 * pull[n] for n in range(3)]
    posts = [(1.0 - OMEGA) * f[0] + WEIGHTS[0] * base]
    for member in range(1, 19, 2):
        vector = LATTICE[member]
        even = WEIGHTS[member] * (base + dot_c(vector, speed) * dot_c(vector, square))
        odd = WEIGHTS[member] * dot_c(vector, linear)
        posts.append((1.0 - OMEGA) * f[member] + (even + odd))
        posts.append((1.0 - OMEGA) * f[member + 1] + (even - odd))
    return posts


def columns(source, out, at):
    planes, width_x = source.shape[1], source.shape[2]
    lane = iota((width_x, LANES), 1)
    lines = out.shape[1] // LANES
    totals = [jnp.zeros((width_x, LANES), F32) for _ in range(lines)]
    for plane in range(19 * planes):
        line, target = divmod(2 * plane, LANES)
        block = source[plane // planes, plane % planes]
        shift = (target - at) % LANES
        if shift:
            block = pltpu.roll(block, shift, 1)
        totals[line] = jnp.where((lane == target) | (lane == target + 1), block, totals[line])
    for line in range(lines):
        out[:, line * LANES : (line + 1) * LANES] = totals[line]


def corner_kernel(up, down, x_low, x_high, after_0, after_1, out_up, out_down):
    width_x, width_y = up.shape[0], x_low.shape[1]
    count = x_low.shape[0]
    pad = jnp.zeros((LANES - count, LANES), F32)
    for source, out, start, at in ((up, out_up, width_y - LANES, LANES - 2), (down, out_down, 0, 0)):
        out[0:width_x, :] = source[...]
        out[width_x:, :] = jnp.zeros((out.shape[0] - width_x, out.shape[1]), F32)
        for number, halo in enumerate((x_low, x_high)):
            turned = jnp.transpose(jnp.concatenate([halo[:, start : start + LANES], pad], axis=0))
            row = width_x + 2 * number
            out[row : row + 2, 0:LANES] = turned[at : at + 2]


def ring_rows(x_low, x_high, f_ref, ring_ref):
    planes, tall = f_ref.shape[1], f_ref.shape[2]
    for halo, members, row, inner in ((x_low, X_UP, RING - 1, RING - 2), (x_high, X_DOWN, 0, 1)):
        _, second, third = face_rows(members, planes)
        for z in range(planes):
            for member in range(19):
                places = [(row, member * planes + z)]
                if member in second:
                    places.append((inner, second[member] + z))
                for line, at in places:
                    line += tall - RING
                    f_ref[member, z, line : line + 1, :] = halo[at : at + 1, :]
            for number in range(4):
                at = third + number * planes + z
                ring_ref[number, z, inner : inner + 1, :] = halo[at : at + 1, :]


def side_cells(y_low, y_high, f_ref, ring_ref):
    planes, tall = f_ref.shape[1], f_ref.shape[2]
    width_x = tall - RING
    lane = iota((width_x, LANES), 1)
    wide_lane = iota((LANES, LANES), 1)
    pad = jnp.zeros((LANES - 8, LANES), F32)
    low = jnp.transpose(jnp.concatenate([y_low[width_x:, 0:LANES], pad], axis=0))
    high = jnp.transpose(jnp.concatenate([y_high[width_x:, 0:LANES], pad], axis=0))
    near = wide_lane >= LANES - 2
    ring_rows(
        jnp.where(near, pltpu.roll(low, LANES - 2, 1), high),
        jnp.where(near, pltpu.roll(low, LANES - 4, 1), pltpu.roll(high, LANES - 2, 1)),
        f_ref,
        ring_ref,
    )
    for plane in range(19 * planes):
        line, here = divmod(2 * plane, LANES)
        below = y_low[0:width_x, line * LANES : (line + 1) * LANES]
        above = y_high[0:width_x, line * LANES : (line + 1) * LANES]
        if (LANES - 2 - here) % LANES:
            below = pltpu.roll(below, (LANES - 2 - here) % LANES, 1)
        if here:
            above = pltpu.roll(above, LANES - here, 1)
        f_ref[plane // planes, plane % planes, 0:width_x, :] = jnp.where(lane >= LANES - 2, below, above)


def shifted(block, member):
    along_x, along_y, _ = LATTICE[member]
    if along_x:
        block = pltpu.roll(block, along_x % block.shape[0], 0)
    if along_y:
        block = pltpu.roll(block, along_y % block.shape[1], 1)
    return block


X_UP = [i for i in range(19) if LATTICE[i][0] == 1]
X_DOWN = [i for i in range(19) if LATTICE[i][0] == -1]
MOVED = [i for i in range(19) if LATTICE[i][0] or LATTICE[i][1]]


def force_at(ref, planes, tall, z, row, lanes):
    return [ref[pl.ds(pl.multiple_of((n * planes + z) * tall + row, 8), 8), lanes] for n in range(3)]


def for_rows(planes, width_x, body):
    @pl.loop(0, planes * (width_x // 8))
    def _(index):
        row = pl.multiple_of((index % (width_x // 8)) * 8, 8)
        body(index // (width_x // 8), row, pl.multiple_of(index * 8, 8))


def collide_block(f_ref, ring_ref, force_ref, z, row, lanes, force_lanes):
    planes, tall = f_ref.shape[1], f_ref.shape[2]
    at = pl.ds(row, 8)
    f = [f_ref[member, z, at, lanes] for member in range(19)]
    density, momenta = moments(f)
    if ring_ref is not None:
        outer = (iota((8, LANES), 0) == 1) | (iota((8, LANES), 0) == RING - 2)
        density = jnp.where(outer, ring_ref[0, z, :, lanes], density)
        momenta = [jnp.where(outer, ring_ref[n + 1, z, :, lanes], momenta[n]) for n in range(3)]
    force = force_at(force_ref, planes, tall, z, row, force_lanes)
    for member, value in enumerate(collide(f, density, momenta, force)):
        f_ref[member, z, at, lanes] = value


def first_kernel(f_in, x_low, x_high, force_ref, f_ref, ring_ref, sems):
    planes, width_x, width_y = f_in.shape[1], f_in.shape[2], f_in.shape[3]
    copies = fetch([(f_in.at[:, z], f_ref.at[:, z, pl.ds(0, width_x), :]) for z in range(planes)], sems)
    ring_rows(x_low, x_high, f_ref, ring_ref)

    @pl.loop(0, planes)
    def _(z):
        for start in range(0, width_y, LANES):
            lanes = pl.ds(start, LANES)
            collide_block(f_ref, ring_ref, force_ref, z, width_x, lanes, lanes)

    for z in range(planes):
        copies[z].wait()

        @pl.loop(0, width_x // 8)
        def _(index):
            row = pl.multiple_of(index * 8, 8)
            for start in range(0, width_y, LANES):
                lanes = pl.ds(start, LANES)
                collide_block(f_ref, None, force_ref, z, row, lanes, lanes)


def main_kernel(
    cap, steps, before, y_low, y_high, force_0, force_1, own_0, own_1, out_hbm, back_ref,
    side, after, ring_ref, probe_0, probe_1, rows, out_ref, sems,
):
    planes, tall, width_y = before.shape[1], before.shape[2], before.shape[3]
    width_x, wide = tall - RING, after.shape[3]
    side_cells(y_low, y_high, side, ring_ref)
    far, all_lanes = pl.ds(width_y, LANES), pl.ds(0, LANES)

    def side_body(z, row, flat):
        collide_block(side, None, force_0, z, row, all_lanes, far)

    for_rows(planes, width_x, side_body)

    @pl.loop(0, planes)
    def _(z):
        collide_block(side, ring_ref, force_0, z, width_x, all_lanes, far)

    for member in MOVED:
        for z in range(planes):
            block = jnp.concatenate([before[member, z], side[member, z]], axis=1)
            after[member, (z + LATTICE[member][2]) % planes] = shifted(block, member)

    def second_block(z, row, start, flat=None, kept=range(19)):
        at, lanes = pl.ds(row, 8), pl.ds(start, LANES)
        f = []
        for member in range(19):
            if member in MOVED:
                f.append(after[member, z, at, lanes])
                continue
            other = lax.rem(z - LATTICE[member][2] + planes, planes)
            f.append(before[member, other, at, lanes] if start < width_y else side[member, other, at, all_lanes])
        density, momenta = moments(f)
        if flat is not None:
            inverse = 1.0 / density
            for number, force in enumerate(force_at(force_0, planes, tall, z, row, lanes)):
                probe_0[pl.ds(pl.multiple_of(number * planes * width_x + flat, 8), 8), lanes] = (
                    momenta[number] + 0.5 * force
                ) * inverse
        values = collide(f, density, momenta, force_at(force_1, planes, tall, z, row, lanes))
        for member in kept:
            after[member, z, at, lanes] = values[member]

    def second_body(z, row, flat):
        for start in range(0, width_y, LANES):
            second_block(z, row, start, flat)
        second_block(z, row, width_y, kept=[i for i in range(19) if LATTICE[i][1]])

    for_rows(planes, width_x, second_body)

    @pl.loop(0, planes)
    def _(z):
        for start in range(0, wide, LANES):
            second_block(z, width_x, start, kept=[i for i in range(19) if LATTICE[i][0]])

    def sample_step(step, own_ref, probe_ref):
        for number, row in enumerate(sample(own_ref[...], planes, width_x, width_y, probe_ref)):
            rows[steps * number + step : steps * number + step + 1, :] = row

    sample_step(0, own_0, probe_0)
    copies = []
    for member in range(19):
        for z in range(planes):
            to = (z + LATTICE[member][2]) % planes
            out_ref[member, to] = shifted(after[member, z], member)[0:width_x, 0:width_y]
        copies.append(pltpu.make_async_copy(out_ref.at[member], out_hbm.at[member], sems.at[member]))
        copies[-1].start()

    def last_body(z, row, flat):
        for start in range(0, width_y, LANES):
            lanes = pl.ds(start, LANES)
            density, momenta = moments([out_ref[member, z, pl.ds(row, 8), lanes] for member in range(19)])
            inverse = 1.0 / density
            for number, force in enumerate(force_at(force_1, planes, tall, z, row, lanes)):
                probe_1[pl.ds(pl.multiple_of(number * planes * width_x + flat, 8), 8), lanes] = (
                    momenta[number] + 0.5 * force
                ) * inverse

    for_rows(planes, width_x, last_body)

    sample_step(1, own_1, probe_1)
    send_back(cap, rows, back_ref)
    for copy in copies:
        copy.wait()


def send_back(cap, rows, out_ref):
    devices, steps = out_ref.shape[0], out_ref.shape[1]
    per = LANES // cap
    group = iota((steps, LANES), 1) // cap
    for device in range(devices):
        line, place = device // per, device % per
        total = jnp.zeros((steps, LANES), F32)
        for number in range(3):
            piece = rows[number * steps : (number + 1) * steps, line * LANES : (line + 1) * LANES]
            shift = (number - place) * cap % LANES
            if shift:
                piece = pltpu.roll(piece, shift, 1)
            total = jnp.where(group == number, piece, total)
        out_ref[device] = total


def call(kernel, outs, scratch=(), flops=0, moved=0, limit=24, fetched=(False,), stored=None):
    shapes = [jax.ShapeDtypeStruct(shape, kind) for shape, kind in outs]
    out_specs = [pl.BlockSpec(memory_space=pltpu.SMEM if len(shape) == 1 else pltpu.VMEM) for shape, _ in outs]
    if stored:
        out_specs = [pl.BlockSpec(memory_space=pltpu.HBM if own else pltpu.VMEM) for own in stored]
    places = {True: pltpu.HBM, False: pltpu.VMEM, None: pltpu.SMEM}
    specs = [pl.BlockSpec(memory_space=places[own]) for own in fetched]
    made = pl.pallas_call(
        kernel,
        out_shape=shapes,
        out_specs=out_specs,
        scratch_shapes=list(scratch),
        **({"in_specs": specs} if fetched != (False,) else {}),
        cost_estimate=pl.CostEstimate(flops=flops, bytes_accessed=moved, transcendentals=0),
        compiler_params=pltpu.CompilerParams(vmem_limit_bytes=limit * 1024 * 1024),
    )
    if not any(fetched):
        return made
    return lambda *args: made(
        *[pltpu.with_memory_space_constraint(x, pltpu.HBM) if own else x for x, own in zip(args, fetched)]
    )


def pair(up, down, axis):
    count = lax.axis_size(axis)
    forward = [(i, (i + 1) % count) for i in range(count)]
    backward = [(target, source) for source, target in forward]
    return lax.ppermute(up, axis, forward), lax.ppermute(down, axis, backward)


def local(populations_in, marker_force, marker_frac, marker_cell, marker_tile):
    count_gx, count_gy = lax.axis_size("gx"), lax.axis_size("gy")
    devices = count_gx * count_gy
    steps, owned = marker_force.shape[0], marker_force.shape[2]
    cap = max(2, 2 * owned // devices)
    half, slots = cap // 2, devices * cap
    planes, width_x, width_y = populations_in.shape[1:]
    tall, wide = width_x + RING, width_y + SIDE
    grid = (count_gx, count_gy, width_x, width_y)
    by_comp = lambda x: jnp.transpose(x, (1, 0, 2))
    markers = (
        marker_tile.reshape(steps * owned // LANES, LANES),
        by_comp(marker_cell),
        by_comp(marker_frac),
        by_comp(marker_force),
    )
    message = ((devices, 8, LANES), F32)
    rows = pltpu.VMEM((16, owned), F32)

    def send(outgoing):
        return lax.all_to_all(outgoing, ("gx", "gy"), split_axis=0, concat_axis=0, tiled=True)

    def pack_markers(*refs):
        pack_kernel(grid, steps, cap, *refs)

    face = (((19 + len(X_UP) + 4) * planes, width_y), F32)
    packed = -(-2 * 19 * planes // LANES) * LANES
    outgoing, slot = call(
        pack_markers,
        [message, ((steps, owned), jnp.int32)],
        [
            rows,
            pltpu.VMEM((steps * owned // LANES, LANES), jnp.int32),
            pltpu.VMEM((3, steps, owned), jnp.int32),
            pltpu.VMEM((3, steps, owned), F32),
            pltpu.VMEM((3, steps, owned), F32),
            pltpu.SemaphoreType.DMA((4,)),
        ],
        fetched=(True,) * 4,
    )(*markers)
    x_up, x_down = call(
        strips_kernel,
        [face, face],
        [
            pltpu.VMEM((19, planes, 8, width_y), F32),
            pltpu.VMEM((19, planes, 8, width_y), F32),
            pltpu.SemaphoreType.DMA((2,)),
        ],
        fetched=(True, False),
    )(populations_in, slot)
    y_up, y_down = call(
        columns_kernel,
        [((width_x, packed), F32)] * 2,
        [
            pltpu.VMEM((19, planes, width_x, LANES), F32),
            pltpu.VMEM((19, planes, width_x, LANES), F32),
            pltpu.SemaphoreType.DMA((2,)),
        ],
        fetched=(True, False),
    )(populations_in, x_up)
    arrived = send(outgoing)

    x_low, x_high = pair(x_up, x_down, "gx")
    field = ((3 * planes * tall, wide), F32)
    parts = []
    for step in range(steps):

        def spread_markers(*refs, step=step):
            spread_kernel(cap, step, planes, width_x, width_y, *refs)

        outs = [field, ((8, slots), F32), ((1,), jnp.int32)]
        scalars = (False, None)[: step + 1]
        parts.append(call(spread_markers, outs, fetched=scalars)(arrived, *[part[2] for part in parts[-1:]]))
    (force_0, own_0, _), (force_1, own_1, turns) = parts
    turns = turns.reshape(())

    y_up, y_down = call(corner_kernel, [((width_x + 8, packed), F32)] * 2)(y_up, y_down, x_low, x_high, own_0, own_1)
    y_low, y_high = pair(y_up, y_down, "gy")

    def again(state):
        return state[0] < turns

    def more(state):
        turn, *forces = state

        def turn_markers(*refs):
            turn_kernel(grid, steps, cap, *refs)

        def add_markers(*refs):
            more_kernel(cap, steps, planes, width_x, width_y, *refs)

        spec = [pl.BlockSpec(memory_space=pltpu.SMEM)] + [pl.BlockSpec(memory_space=pltpu.VMEM)] * 4
        (outgoing,) = pl.pallas_call(
            turn_markers,
            out_shape=[jax.ShapeDtypeStruct(*message)],
            in_specs=spec,
            scratch_shapes=[rows],
            compiler_params=pltpu.CompilerParams(vmem_limit_bytes=24 * 1024 * 1024),
        )(turn.reshape(1), *markers)
        return (turn + 1, *call(add_markers, [field] * steps)(send(outgoing), *forces))

    _, force_0, force_1 = lax.while_loop(again, more, (jnp.int32(1), force_0, force_1))

    (before,) = call(
        first_kernel,
        [((19, planes, tall, width_y), F32)],
        [pltpu.VMEM((4, planes, RING, width_y), F32), pltpu.SemaphoreType.DMA((planes,))],
        fetched=(True,) + (False,) * 3,
    )(populations_in, x_low, x_high, force_0)

    def main(*refs):
        main_kernel(cap, steps, *refs)

    own_field = pltpu.VMEM((3 * planes * width_x, width_y), F32)
    fields, back = call(
        main,
        [(populations_in.shape, F32), ((devices, steps, LANES), F32)],
        [
            pltpu.VMEM((19, planes, tall, LANES), F32),
            pltpu.VMEM((19, planes, tall, wide), F32),
            pltpu.VMEM((4, planes, RING, LANES), F32),
            own_field,
            own_field,
            pltpu.VMEM((8, slots), F32),
            pltpu.VMEM(populations_in.shape, F32),
            pltpu.SemaphoreType.DMA((19,)),
        ],
        stored=(True, False),
    )(before, y_low, y_high, force_0, force_1, own_0, own_1)
    returned = send(back)

    def unpack(*refs):
        unpack_kernel(cap, steps, *refs)

    (velocity,) = call(unpack, [((3, steps, owned), F32)])(returned, slot)
    return fields, by_comp(velocity)


def solution(mesh):
    return jax.shard_map(
        local,
        mesh=mesh,
        in_specs=(
            P(None, None, "gx", "gy"),
            P(None, None, ("gx", "gy")),
            P(None, None, ("gx", "gy")),
            P(None, None, ("gx", "gy")),
            P(None, ("gx", "gy"), None),
        ),
        out_specs=(P(None, None, "gx", "gy"), P(None, None, ("gx", "gy"))),
        check_vma=False,
    )
```

```python
import jax
import jax.numpy as jnp
from jax import lax
from jax.experimental import pallas as pl
from jax.experimental.pallas import tpu as pltpu
from jax.sharding import PartitionSpec as P

LATTICE = [
    (0, 0, 0),
    (1, 0, 0),
    (-1, 0, 0),
    (0, 1, 0),
    (0, -1, 0),
    (0, 0, 1),
    (0, 0, -1),
    (1, 1, 0),
    (-1, -1, 0),
    (1, -1, 0),
    (-1, 1, 0),
    (1, 0, 1),
    (-1, 0, -1),
    (1, 0, -1),
    (-1, 0, 1),
    (0, 1, 1),
    (0, -1, -1),
    (0, 1, -1),
    (0, -1, 1),
]
WEIGHTS = [1.0 / 3.0] + [1.0 / 18.0] * 6 + [1.0 / 36.0] * 12
relax_time = 0.8
OMEGA = 1.0 / relax_time
SOURCE = 1.0 - 0.5 / relax_time
LANES = 128

BF = jnp.bfloat16
F32 = jnp.float32


def split2(x):
    high = x.astype(BF)
    low = (x - high.astype(F32)).astype(BF)
    return high, low


def split3(x):
    high = x.astype(BF)
    rest = x - high.astype(F32)
    middle = rest.astype(BF)
    low = (rest - middle.astype(F32)).astype(BF)
    return high, middle, low


def nt(a, b):
    return lax.dot_general(a, b, (((1,), (1,)), ((), ())), preferred_element_type=F32)


def nn(a, b):
    return lax.dot_general(a, b, (((1,), (0,)), ((), ())), preferred_element_type=F32)


def iota(shape, dim):
    return lax.broadcasted_iota(jnp.int32, shape, dim)


RING = 8
SIDE = LANES


def slot_table(slot, slots):
    owned = slot.shape[1]
    return jnp.where(iota((slots, owned), 0) == slot, 1.0, 0.0).astype(BF)


def fetch(pairs, sems):
    copies = [pltpu.make_async_copy(source, target, sems.at[n]) for n, (source, target) in enumerate(pairs)]
    for copy in copies:
        copy.start()
    return copies


def ghosts(step, steps, count_gx, count_gy, width_x, width_y, tiles, cell_x, cell_y):
    reach = steps - step
    tiles = tiles.astype(F32)
    gx = jnp.floor((tiles + 0.5) * (1.0 / count_gy))
    along = []
    for cell, width, place, count in (
        (cell_x, width_x, gx, count_gx),
        (cell_y, width_y, tiles - gx * count_gy, count_gy),
    ):
        above, below = cell >= width - 1 - reach, cell <= reach - 1
        place_up = jnp.where(place == count - 1, 0.0, place + 1.0)
        place_down = jnp.where(place == 0, count - 1.0, place - 1.0)
        along.append((jnp.where(above | below, 1.0, 0.0), place, jnp.where(above, place_up, place_down)))
    (near_x, here_x, there_x), (near_y, here_y, there_y) = along
    return [
        jnp.where(near_x > 0, there_x * count_gy + here_y, -1.0),
        jnp.where(near_y > 0, here_x * count_gy + there_y, -1.0),
        jnp.where(near_x * near_y > 0, there_x * count_gy + there_y, -1.0),
    ]


def pack(grid, steps, cap, step_rows, out_ref, slot_ref, rows, turn=None):
    count_gx, count_gy, width_x, width_y = grid
    devices, half = count_gx * count_gy, cap // 2
    owned = rows.shape[1]
    slots, spare = devices * cap, devices * half
    earlier = jnp.where(iota((owned, owned), 0) < iota((owned, owned), 1), 1.0, 0.0).astype(BF)
    column = iota((devices, owned), 0).astype(F32)
    octets, extras, most = [], [], []
    given = [step_rows(step) for step in range(steps)]
    asked = []
    for step, (tiles, values) in enumerate(given):
        asked.append([tiles.astype(F32)] + ghosts(step, steps, *grid, tiles, values[0], values[1]))
    member = [[jnp.where(column == tile, 1.0, 0.0) for tile in tiles] for tiles in asked]
    before = nn(jnp.concatenate(sum(member, []), axis=0).astype(BF), earlier)
    before = [before[n * devices : (n + 1) * devices] for n in range(4 * steps)]
    for step, (tiles, values) in enumerate(given):
        if turn is None:
            rank = jnp.sum(before[4 * step] * member[step][0], axis=0, keepdims=True)
            slot = tiles * cap + rank.astype(jnp.int32)
            slot_ref[step : step + 1, :] = slot
            rows[...] = jnp.zeros_like(rows)
            for number, value in enumerate(values):
                rows[number : number + 1, :] = value
            packed = nt(jnp.concatenate(split3(rows[...]), axis=0), slot_table(slot, slots))
            packed = packed[0:16] + packed[16:32] + packed[32:48]
            octets.append((packed[0:8], packed[8:16]))
        taken = [jnp.zeros((devices, 1), F32)]
        places = []
        for number in range(1, 4):
            here = member[step][number]
            rank = jnp.sum((before[4 * step + number] + taken[-1]) * here, axis=0, keepdims=True)
            taken.append(taken[-1] + jnp.sum(here, axis=1, keepdims=True))
            if turn is not None:
                rank = rank - turn * half
            tile = asked[step][number]
            places.append(jnp.where((tile >= 0) & (rank >= 0) & (rank < half), tile * half + rank, -1.0).astype(jnp.int32))
        grid_slots = iota((spare, owned), 0)
        chosen = (grid_slots == places[0]) | (grid_slots == places[1]) | (grid_slots == places[2])
        rows[...] = jnp.zeros_like(rows)
        for place, value in zip((1, 2, 3, 4, 5, 6, 7, 9, 10), values):
            rows[place : place + 1, :] = value
        extra = nt(jnp.concatenate(split3(rows[...]), axis=0), jnp.where(chosen, 1.0, 0.0).astype(BF))
        extra = extra[0:16] + extra[16:32] + extra[32:48]
        lanes, sender = iota((devices, spare), 1), iota((devices, spare), 0)
        ends = [
            jnp.sum(jnp.where(lanes // half == sender, end, 0.0), axis=0, keepdims=True) for end in (taken[1], taken[2])
        ]
        rank = (iota((1, spare), 1) % half).astype(F32)
        if turn is not None:
            rank = rank + turn * half
        in_x = (rank < ends[0]) | (rank >= ends[1])
        in_y = rank >= ends[0]
        first = []
        for cell, width, moved in ((extra[1:2], width_x, in_x), (extra[2:3], width_y, in_y)):
            first.append(cell + jnp.where(moved, jnp.where(cell * 2 < width, width * 1.0, -1.0 * width), 0.0))
        extras.append((jnp.concatenate([extra[0:1]] + first + [extra[3:8]], axis=0), extra[8:16]))
        most.append(jnp.max(taken[3], axis=0, keepdims=True))
    lane, row = iota((8, LANES), 1), iota((8, LANES), 0)

    def placed(octet, device, width, offset):
        line, place = device * width // LANES, device * width % LANES
        piece = octet[:, line * LANES : (line + 1) * LANES]
        shift = (offset - place) % LANES
        if shift:
            piece = pltpu.roll(piece, shift, 1)
        return jnp.where((lane >= offset) & (lane < offset + width), piece, 0.0)

    heading = jnp.zeros((8, LANES), F32)
    for step in range(steps):
        start = (2 * step + 1) * cap + half
        heading = jnp.where((row == 3) & (lane >= start) & (lane < start + half), most[step], heading)
    for device in range(devices):
        block = heading
        for step in range(steps):
            start = 2 * step * cap
            if turn is None:
                block = block + placed(octets[step][0], device, cap, start)
                block = block + placed(octets[step][1], device, cap, start + cap)
            block = block + placed(extras[step][0], device, half, start + cap)
            block = block + placed(extras[step][1], device, half, start + cap + half)
        out_ref[device] = block


def marker_rows(tile_ref, cell_ref, frac_ref, force_ref):
    lines = cell_ref.shape[2] // LANES

    def step_rows(step):
        tiles = jnp.concatenate(
            [tile_ref[step * lines + r : step * lines + r + 1, :] for r in range(lines)], axis=1
        )
        values = [cell_ref[n, step : step + 1, :].astype(F32) for n in range(3)]
        values += [frac_ref[n, step : step + 1, :] for n in range(3)]
        values += [force_ref[n, step : step + 1, :] for n in range(3)]
        return tiles, values

    return step_rows


def pack_kernel(
    grid, steps, cap, tile_in, cell_in, frac_in, force_in, out_ref, slot_ref,
    rows, tile_ref, cell_ref, frac_ref, force_ref, sems,
):
    copies = fetch([(tile_in, tile_ref), (cell_in, cell_ref), (frac_in, frac_ref), (force_in, force_ref)], sems)
    for copy in copies:
        copy.wait()
    pack(grid, steps, cap, marker_rows(tile_ref, cell_ref, frac_ref, force_ref), out_ref, slot_ref, rows)


def columns_kernel(f_in, after_ref, up, down, far_ref, near_ref, sems):
    width_y = f_in.shape[3]
    copies = fetch(
        [
            (f_in.at[:, :, :, pl.ds(width_y - LANES, LANES)], far_ref),
            (f_in.at[:, :, :, pl.ds(0, LANES)], near_ref),
        ],
        sems,
    )
    for copy, out, source, at in ((copies[0], up, far_ref, LANES - 2), (copies[1], down, near_ref, 0)):
        copy.wait()
        columns(source, out, at)


def face_rows(members, planes):
    first = 19 * planes
    second = {member: first + n * planes for n, member in enumerate(members)}
    return first, second, first + len(members) * planes


def strips_kernel(f_in, after_ref, x_up, x_down, near_ref, far_ref, sems):
    planes, width_x = f_in.shape[1], f_in.shape[2]
    copies = fetch(
        [
            (f_in.at[:, :, pl.ds(width_x - 8, 8), :], far_ref),
            (f_in.at[:, :, pl.ds(0, 8), :], near_ref),
        ],
        sems,
    )
    for copy, out, source, members, row, inner in (
        (copies[0], x_up, far_ref, X_UP, 7, 6),
        (copies[1], x_down, near_ref, X_DOWN, 0, 1),
    ):
        copy.wait()
        _, second, third = face_rows(members, planes)
        for z in range(planes):
            for member in range(19):
                at = member * planes + z
                out[at : at + 1, :] = source[member, z, row : row + 1, :]
            for member, at in second.items():
                out[at + z : at + z + 1, :] = source[member, z, inner : inner + 1, :]
            density, momenta = moments([source[member, z] for member in range(19)])
            for number, value in enumerate([density] + momenta):
                at = third + number * planes + z
                out[at : at + 1, :] = value[inner : inner + 1]


def turn_kernel(grid, steps, cap, turn_ref, tile_ref, cell_ref, frac_ref, force_ref, out_ref, rows):
    step_rows = marker_rows(tile_ref, cell_ref, frac_ref, force_ref)
    pack(grid, steps, cap, step_rows, out_ref, None, rows, turn_ref[0].astype(F32))


def gather(recv_ref, offset, width):
    devices = recv_ref.shape[0]
    per = LANES // width
    group = iota((8, LANES), 1) // width
    pieces = []
    for line in range(devices // per):
        total = jnp.zeros((8, LANES), F32)
        for place in range(per):
            piece = recv_ref[line * per + place]
            shift = (place * width - offset) % LANES
            if shift:
                piece = pltpu.roll(piece, shift, 1)
            total = jnp.where(group == place, piece, total)
        pieces.append(total)
    return jnp.concatenate(pieces, axis=1)


def unpack_kernel(cap, steps, recv_ref, slot_ref, out_ref):
    devices = recv_ref.shape[0]
    per = LANES // cap
    group = iota((steps, LANES), 1) // cap
    comps = []
    for number in range(3):
        pieces = []
        for line in range(devices // per):
            total = jnp.zeros((steps, LANES), F32)
            for place in range(per):
                piece = recv_ref[line * per + place]
                shift = (place - number) * cap % LANES
                if shift:
                    piece = pltpu.roll(piece, shift, 1)
                total = jnp.where(group == place, piece, total)
            pieces.append(total)
        comps.append(jnp.concatenate(pieces, axis=1))
    slots = devices * cap
    for step in range(steps):
        rows = jnp.concatenate([comp[step : step + 1] for comp in comps] + [jnp.zeros((13, slots), F32)], axis=0)
        found = nn(jnp.concatenate(split3(rows), axis=0), slot_table(slot_ref[step : step + 1, :], slots))
        found = found[0:8] + found[16:24] + found[32:40]
        for number in range(3):
            out_ref[number, step : step + 1, :] = found[number : number + 1]


def line_weights(cell, frac, extent):
    grid = iota((extent, cell.shape[1]), 0).astype(F32)
    return jnp.where(grid == cell, 1.0 - frac, jnp.where(grid == cell + 1.0, frac, 0.0))


def y_table(cell, frac, extent):
    grid = iota((extent, cell.shape[1]), 0).astype(F32)
    lower, upper = grid == cell, grid == cell + 1.0
    tables = []
    for low, high in zip(split2(1.0 - frac), split2(frac)):
        low, high = low.astype(F32), high.astype(F32)
        tables.append(jnp.where(lower, low, jnp.where(upper, high, 0.0)).astype(BF))
    return tables


def plane_table(rows, planes, width_x):
    kernel_x = line_weights(rows[0:1], rows[3:4], width_x)
    kernel_z = line_weights(rows[2:3], rows[5:6], 8)
    return [kernel_z[z : z + 1] * kernel_x for z in range(planes)]


def product(table, along_y):
    high, low = split2(table)
    high_y, low_y = along_y
    return nt(
        jnp.concatenate([high, low, high], axis=1), jnp.concatenate([high_y, high_y, low_y], axis=1)
    )


def spread_own(first, second, planes, width_x, width_y, force_ref):
    tall = width_x + RING
    table = jnp.concatenate(plane_table(first, planes, width_x), axis=0)
    along_y = y_table(first[1:2], first[4:5], width_y)
    strengths = (first[6:7], first[7:8], second[0:1])
    found = product(jnp.concatenate([table * strength for strength in strengths], axis=0), along_y)
    for number in range(3 * planes):
        force_ref[number * tall : number * tall + width_x, 0:width_y] = found[number * width_x : (number + 1) * width_x]


def spread_ghosts(first, second, planes, width_x, width_y, force_ref, add):
    tall, wide = width_x + RING, width_y + SIDE
    cell_x = jnp.where(first[1:2] < 0, first[1:2] + tall, first[1:2])
    cell_y = jnp.where(first[2:3] < 0, first[2:3] + wide, first[2:3])
    kernel_x = line_weights(cell_x, first[4:5], tall)
    kernel_z = line_weights(first[3:4], first[6:7], 8)
    along_y = y_table(cell_y, first[5:6], wide)
    side_y = [table[width_y:] for table in along_y]
    ring = [kernel_z[z : z + 1] * kernel_x[width_x:] for z in range(planes)]
    side = [kernel_z[z : z + 1] * kernel_x[0:width_x] for z in range(planes)]
    ring, side = jnp.concatenate(ring, axis=0), jnp.concatenate(side, axis=0)
    strengths = (first[7:8], second[1:2], second[2:3])
    found_ring = product(jnp.concatenate([ring * strength for strength in strengths], axis=0), along_y)
    found_side = product(jnp.concatenate([side * strength for strength in strengths], axis=0), side_y)
    for number in range(3 * planes):
        at = number * tall
        part_ring = found_ring[number * RING : (number + 1) * RING]
        part_side = found_side[number * width_x : (number + 1) * width_x]
        if add:
            part_ring = part_ring + force_ref[at + width_x : at + tall, :]
            part_side = part_side + force_ref[at : at + width_x, width_y:]
        force_ref[at + width_x : at + tall, :] = part_ring
        force_ref[at : at + width_x, width_y:] = part_side


def spread_kernel(cap, steps, planes, width_x, width_y, recv_ref, *refs):
    forces, owns, turns_ref = refs[:steps], refs[steps : 2 * steps], refs[2 * steps]
    half = cap // 2
    most = jnp.zeros((1, recv_ref.shape[0] * half), F32)
    for step in range(steps):
        start = 2 * step * cap
        first = gather(recv_ref, start, cap)
        owns[step][...] = first
        second = gather(recv_ref, start + cap, cap)
        spread_own(first, second, planes, width_x, width_y, forces[step])
        first = gather(recv_ref, start + cap, half)
        second = gather(recv_ref, start + cap + half, half)
        spread_ghosts(first, second, planes, width_x, width_y, forces[step], False)
        most = jnp.maximum(most, second[3:4])
    turns_ref[0] = (jnp.max(most).astype(jnp.int32) + half - 1) // half


def more_kernel(cap, steps, planes, width_x, width_y, recv_ref, *refs):
    half = cap // 2
    for step in range(steps):
        start = (2 * step + 1) * cap
        force_ref = refs[steps + step]
        force_ref[...] = refs[step][...]
        first, second = gather(recv_ref, start, half), gather(recv_ref, start + half, half)
        spread_ghosts(first, second, planes, width_x, width_y, force_ref, True)


def sample(first, planes, width_x, width_y, probe_ref):
    table = jnp.concatenate(plane_table(first, planes, width_x), axis=0)
    along_y = y_table(first[1:2], first[4:5], width_y)
    size = planes * width_x
    high, low = split2(probe_ref[...])
    high_y, low_y = along_y
    found = nn(jnp.concatenate([high, low, high], axis=1), jnp.concatenate([high_y, high_y, low_y], axis=0))
    rows = [jnp.sum(found[n * size : (n + 1) * size] * table, axis=0, keepdims=True) for n in range(3)]
    return rows


def moments(f):
    density = f[0]
    diff = {}
    for member in range(1, 19, 2):
        density = density + (f[member] + f[member + 1])
        diff[member] = f[member] - f[member + 1]
    momenta = []
    for number in range(3):
        total = None
        for member in range(1, 19, 2):
            sign = LATTICE[member][number]
            if sign == 0:
                continue
            if total is None:
                total = diff[member] if sign == 1 else -diff[member]
            else:
                total = total + diff[member] if sign == 1 else total - diff[member]
        momenta.append(total)
    return density, momenta


def dot_c(vector, comps):
    total = None
    for number in range(3):
        if vector[number] == 0:
            continue
        if total is None:
            total = comps[number] if vector[number] == 1 else -comps[number]
        else:
            total = total + comps[number] if vector[number] == 1 else total - comps[number]
    return total


def collide(f, density, momenta, force):
    inverse = 1.0 / density
    speed = [(momenta[n] + 0.5 * force[n]) * inverse for n in range(3)]
    scaled = OMEGA * density
    speed_sq = speed[0] * speed[0] + speed[1] * speed[1] + speed[2] * speed[2]
    along = speed[0] * force[0] + speed[1] * force[1] + speed[2] * force[2]
    base = scaled * (1.0 - 1.5 * speed_sq) - (3.0 * SOURCE) * along
    flow = [scaled * speed[n] for n in range(3)]
    pull = [(3.0 * SOURCE) * force[n] for n in range(3)]
    linear = [3.0 * flow[n] + pull[n] for n in range(3)]
    square = [4.5 * flow[n] + 3.0 * pull[n] for n in range(3)]
    posts = [(1.0 - OMEGA) * f[0] + WEIGHTS[0] * base]
    for member in range(1, 19, 2):
        vector = LATTICE[member]
        even = WEIGHTS[member] * (base + dot_c(vector, speed) * dot_c(vector, square))
        odd = WEIGHTS[member] * dot_c(vector, linear)
        posts.append((1.0 - OMEGA) * f[member] + (even + odd))
        posts.append((1.0 - OMEGA) * f[member + 1] + (even - odd))
    return posts


def columns(source, out, at):
    planes, width_x = source.shape[1], source.shape[2]
    lane = iota((width_x, LANES), 1)
    lines = out.shape[1] // LANES
    totals = [jnp.zeros((width_x, LANES), F32) for _ in range(lines)]
    for plane in range(19 * planes):
        line, target = divmod(2 * plane, LANES)
        block = source[plane // planes, plane % planes]
        shift = (target - at) % LANES
        if shift:
            block = pltpu.roll(block, shift, 1)
        totals[line] = jnp.where((lane == target) | (lane == target + 1), block, totals[line])
    for line in range(lines):
        out[:, line * LANES : (line + 1) * LANES] = totals[line]


def corner_kernel(up, down, x_low, x_high, after_0, after_1, out_up, out_down):
    width_x, width_y = up.shape[0], x_low.shape[1]
    count = x_low.shape[0]
    pad = jnp.zeros((LANES - count, LANES), F32)
    for source, out, start, at in ((up, out_up, width_y - LANES, LANES - 2), (down, out_down, 0, 0)):
        out[0:width_x, :] = source[...]
        out[width_x:, :] = jnp.zeros((out.shape[0] - width_x, out.shape[1]), F32)
        for number, halo in enumerate((x_low, x_high)):
            turned = jnp.transpose(jnp.concatenate([halo[:, start : start + LANES], pad], axis=0))
            row = width_x + 2 * number
            out[row : row + 2, 0:LANES] = turned[at : at + 2]


def ring_rows(x_low, x_high, f_ref, ring_ref):
    planes, tall = f_ref.shape[1], f_ref.shape[2]
    for halo, members, row, inner in ((x_low, X_UP, RING - 1, RING - 2), (x_high, X_DOWN, 0, 1)):
        _, second, third = face_rows(members, planes)
        for z in range(planes):
            for member in range(19):
                places = [(row, member * planes + z)]
                if member in second:
                    places.append((inner, second[member] + z))
                for line, at in places:
                    line += tall - RING
                    f_ref[member, z, line : line + 1, :] = halo[at : at + 1, :]
            for number in range(4):
                at = third + number * planes + z
                ring_ref[number, z, inner : inner + 1, :] = halo[at : at + 1, :]


def side_cells(y_low, y_high, f_ref, ring_ref):
    planes, tall = f_ref.shape[1], f_ref.shape[2]
    width_x = tall - RING
    lane = iota((width_x, LANES), 1)
    wide_lane = iota((LANES, LANES), 1)
    pad = jnp.zeros((LANES - 8, LANES), F32)
    low = jnp.transpose(jnp.concatenate([y_low[width_x:, 0:LANES], pad], axis=0))
    high = jnp.transpose(jnp.concatenate([y_high[width_x:, 0:LANES], pad], axis=0))
    near = wide_lane >= LANES - 2
    ring_rows(
        jnp.where(near, pltpu.roll(low, LANES - 2, 1), high),
        jnp.where(near, pltpu.roll(low, LANES - 4, 1), pltpu.roll(high, LANES - 2, 1)),
        f_ref,
        ring_ref,
    )
    for plane in range(19 * planes):
        line, here = divmod(2 * plane, LANES)
        below = y_low[0:width_x, line * LANES : (line + 1) * LANES]
        above = y_high[0:width_x, line * LANES : (line + 1) * LANES]
        if (LANES - 2 - here) % LANES:
            below = pltpu.roll(below, (LANES - 2 - here) % LANES, 1)
        if here:
            above = pltpu.roll(above, LANES - here, 1)
        f_ref[plane // planes, plane % planes, 0:width_x, :] = jnp.where(lane >= LANES - 2, below, above)


def shifted(block, member):
    along_x, along_y, _ = LATTICE[member]
    if along_x:
        block = pltpu.roll(block, along_x % block.shape[0], 0)
    if along_y:
        block = pltpu.roll(block, along_y % block.shape[1], 1)
    return block


X_UP = [i for i in range(19) if LATTICE[i][0] == 1]
X_DOWN = [i for i in range(19) if LATTICE[i][0] == -1]
MOVED = [i for i in range(19) if LATTICE[i][0] or LATTICE[i][1]]


def force_at(ref, planes, tall, z, row, lanes):
    return [ref[pl.ds(pl.multiple_of((n * planes + z) * tall + row, 8), 8), lanes] for n in range(3)]


def for_rows(planes, width_x, body):
    @pl.loop(0, planes * (width_x // 8))
    def _(index):
        row = pl.multiple_of((index % (width_x // 8)) * 8, 8)
        body(index // (width_x // 8), row, pl.multiple_of(index * 8, 8))


def collide_block(f_ref, ring_ref, force_ref, z, row, lanes, force_lanes):
    planes, tall = f_ref.shape[1], f_ref.shape[2]
    at = pl.ds(row, 8)
    f = [f_ref[member, z, at, lanes] for member in range(19)]
    density, momenta = moments(f)
    if ring_ref is not None:
        outer = (iota((8, LANES), 0) == 1) | (iota((8, LANES), 0) == RING - 2)
        density = jnp.where(outer, ring_ref[0, z, :, lanes], density)
        momenta = [jnp.where(outer, ring_ref[n + 1, z, :, lanes], momenta[n]) for n in range(3)]
    force = force_at(force_ref, planes, tall, z, row, force_lanes)
    for member, value in enumerate(collide(f, density, momenta, force)):
        f_ref[member, z, at, lanes] = value


def first_kernel(f_in, x_low, x_high, force_ref, f_ref, ring_ref, sems):
    planes, width_x, width_y = f_in.shape[1], f_in.shape[2], f_in.shape[3]
    copies = fetch([(f_in.at[:, z], f_ref.at[:, z, pl.ds(0, width_x), :]) for z in range(planes)], sems)
    ring_rows(x_low, x_high, f_ref, ring_ref)

    @pl.loop(0, planes)
    def _(z):
        for start in range(0, width_y, LANES):
            lanes = pl.ds(start, LANES)
            collide_block(f_ref, ring_ref, force_ref, z, width_x, lanes, lanes)

    for z in range(planes):
        copies[z].wait()

        @pl.loop(0, width_x // 8)
        def _(index):
            row = pl.multiple_of(index * 8, 8)
            for start in range(0, width_y, LANES):
                lanes = pl.ds(start, LANES)
                collide_block(f_ref, None, force_ref, z, row, lanes, lanes)


def main_kernel(
    cap, steps, before, y_low, y_high, force_0, force_1, own_0, own_1, out_hbm, back_ref,
    side, after, ring_ref, probe_0, probe_1, rows, out_ref, sems,
):
    planes, tall, width_y = before.shape[1], before.shape[2], before.shape[3]
    width_x, wide = tall - RING, after.shape[3]
    side_cells(y_low, y_high, side, ring_ref)
    far, all_lanes = pl.ds(width_y, LANES), pl.ds(0, LANES)

    def side_body(z, row, flat):
        collide_block(side, None, force_0, z, row, all_lanes, far)

    for_rows(planes, width_x, side_body)

    @pl.loop(0, planes)
    def _(z):
        collide_block(side, ring_ref, force_0, z, width_x, all_lanes, far)

    for member in MOVED:
        for z in range(planes):
            block = jnp.concatenate([before[member, z], side[member, z]], axis=1)
            after[member, (z + LATTICE[member][2]) % planes] = shifted(block, member)

    def second_block(z, row, start, flat=None, kept=range(19)):
        at, lanes = pl.ds(row, 8), pl.ds(start, LANES)
        f = []
        for member in range(19):
            if member in MOVED:
                f.append(after[member, z, at, lanes])
                continue
            other = lax.rem(z - LATTICE[member][2] + planes, planes)
            f.append(before[member, other, at, lanes] if start < width_y else side[member, other, at, all_lanes])
        density, momenta = moments(f)
        if flat is not None:
            inverse = 1.0 / density
            for number, force in enumerate(force_at(force_0, planes, tall, z, row, lanes)):
                probe_0[pl.ds(pl.multiple_of(number * planes * width_x + flat, 8), 8), lanes] = (
                    momenta[number] + 0.5 * force
                ) * inverse
        values = collide(f, density, momenta, force_at(force_1, planes, tall, z, row, lanes))
        for member in kept:
            after[member, z, at, lanes] = values[member]

    def second_body(z, row, flat):
        for start in range(0, width_y, LANES):
            second_block(z, row, start, flat)
        second_block(z, row, width_y, kept=[i for i in range(19) if LATTICE[i][1]])

    for_rows(planes, width_x, second_body)

    @pl.loop(0, planes)
    def _(z):
        for start in range(0, wide, LANES):
            second_block(z, width_x, start, kept=[i for i in range(19) if LATTICE[i][0]])

    def sample_step(step, own_ref, probe_ref):
        for number, row in enumerate(sample(own_ref[...], planes, width_x, width_y, probe_ref)):
            rows[steps * number + step : steps * number + step + 1, :] = row

    sample_step(0, own_0, probe_0)
    copies = []
    for member in range(19):
        for z in range(planes):
            to = (z + LATTICE[member][2]) % planes
            out_ref[member, to] = shifted(after[member, z], member)[0:width_x, 0:width_y]
        copies.append(pltpu.make_async_copy(out_ref.at[member], out_hbm.at[member], sems.at[member]))
        copies[-1].start()

    def last_body(z, row, flat):
        for start in range(0, width_y, LANES):
            lanes = pl.ds(start, LANES)
            density, momenta = moments([out_ref[member, z, pl.ds(row, 8), lanes] for member in range(19)])
            inverse = 1.0 / density
            for number, force in enumerate(force_at(force_1, planes, tall, z, row, lanes)):
                probe_1[pl.ds(pl.multiple_of(number * planes * width_x + flat, 8), 8), lanes] = (
                    momenta[number] + 0.5 * force
                ) * inverse

    for_rows(planes, width_x, last_body)

    sample_step(1, own_1, probe_1)
    send_back(cap, rows, back_ref)
    for copy in copies:
        copy.wait()


def send_back(cap, rows, out_ref):
    devices, steps = out_ref.shape[0], out_ref.shape[1]
    per = LANES // cap
    group = iota((steps, LANES), 1) // cap
    for device in range(devices):
        line, place = device // per, device % per
        total = jnp.zeros((steps, LANES), F32)
        for number in range(3):
            piece = rows[number * steps : (number + 1) * steps, line * LANES : (line + 1) * LANES]
            shift = (number - place) * cap % LANES
            if shift:
                piece = pltpu.roll(piece, shift, 1)
            total = jnp.where(group == number, piece, total)
        out_ref[device] = total


def call(kernel, outs, scratch=(), flops=0, moved=0, limit=24, fetched=(False,), stored=None):
    shapes = [jax.ShapeDtypeStruct(shape, kind) for shape, kind in outs]
    out_specs = [pl.BlockSpec(memory_space=pltpu.SMEM if len(shape) == 1 else pltpu.VMEM) for shape, _ in outs]
    if stored:
        out_specs = [pl.BlockSpec(memory_space=pltpu.HBM if own else pltpu.VMEM) for own in stored]
    places = {True: pltpu.HBM, False: pltpu.VMEM, None: pltpu.SMEM}
    specs = [pl.BlockSpec(memory_space=places[own]) for own in fetched]
    made = pl.pallas_call(
        kernel,
        out_shape=shapes,
        out_specs=out_specs,
        scratch_shapes=list(scratch),
        **({"in_specs": specs} if fetched != (False,) else {}),
        cost_estimate=pl.CostEstimate(flops=flops, bytes_accessed=moved, transcendentals=0),
        compiler_params=pltpu.CompilerParams(vmem_limit_bytes=limit * 1024 * 1024),
    )
    if not any(fetched):
        return made
    return lambda *args: made(
        *[pltpu.with_memory_space_constraint(x, pltpu.HBM) if own else x for x, own in zip(args, fetched)]
    )


def pair(up, down, axis):
    count = lax.axis_size(axis)
    forward = [(i, (i + 1) % count) for i in range(count)]
    backward = [(target, source) for source, target in forward]
    return lax.ppermute(up, axis, forward), lax.ppermute(down, axis, backward)


def run(rounds, populations_in, marker_force, marker_frac, marker_cell, marker_tile):
    count_gx, count_gy = lax.axis_size("gx"), lax.axis_size("gy")
    devices = count_gx * count_gy
    steps, owned = marker_force.shape[0], marker_force.shape[2]
    cap = max(2, 2 * owned // devices)
    half, slots = cap // 2, devices * cap
    planes, width_x, width_y = populations_in.shape[1:]
    tall, wide = width_x + RING, width_y + SIDE
    grid = (count_gx, count_gy, width_x, width_y)
    by_comp = lambda x: jnp.transpose(x, (1, 0, 2))
    markers = (
        marker_tile.reshape(steps * owned // LANES, LANES),
        by_comp(marker_cell),
        by_comp(marker_frac),
        by_comp(marker_force),
    )
    message = ((devices, 8, LANES), F32)
    rows = pltpu.VMEM((16, owned), F32)

    def send(outgoing):
        return lax.all_to_all(outgoing, ("gx", "gy"), split_axis=0, concat_axis=0, tiled=True)

    def pack_markers(*refs):
        pack_kernel(grid, steps, cap, *refs)

    face = (((19 + len(X_UP) + 4) * planes, width_y), F32)
    packed = -(-2 * 19 * planes // LANES) * LANES
    outgoing, slot = call(
        pack_markers,
        [message, ((steps, owned), jnp.int32)],
        [
            rows,
            pltpu.VMEM((steps * owned // LANES, LANES), jnp.int32),
            pltpu.VMEM((3, steps, owned), jnp.int32),
            pltpu.VMEM((3, steps, owned), F32),
            pltpu.VMEM((3, steps, owned), F32),
            pltpu.SemaphoreType.DMA((4,)),
        ],
        fetched=(True,) * 4,
    )(*markers)
    x_up, x_down = call(
        strips_kernel,
        [face, face],
        [
            pltpu.VMEM((19, planes, 8, width_y), F32),
            pltpu.VMEM((19, planes, 8, width_y), F32),
            pltpu.SemaphoreType.DMA((2,)),
        ],
        fetched=(True, False),
    )(populations_in, slot)
    y_up, y_down = call(
        columns_kernel,
        [((width_x, packed), F32)] * 2,
        [
            pltpu.VMEM((19, planes, width_x, LANES), F32),
            pltpu.VMEM((19, planes, width_x, LANES), F32),
            pltpu.SemaphoreType.DMA((2,)),
        ],
        fetched=(True, False),
    )(populations_in, x_up)
    arrived = send(outgoing)

    x_low, x_high = pair(x_up, x_down, "gx")
    field = ((3 * planes * tall, wide), F32)

    def spread_markers(*refs):
        spread_kernel(cap, steps, planes, width_x, width_y, *refs)

    force_0, force_1, own_0, own_1, turns = call(
        spread_markers, [field] * steps + [((8, slots), F32)] * steps + [((1,), jnp.int32)]
    )(arrived)
    turns = turns.reshape(())

    y_up, y_down = call(corner_kernel, [((width_x + 8, packed), F32)] * 2)(y_up, y_down, x_low, x_high, own_0, own_1)
    y_low, y_high = pair(y_up, y_down, "gy")

    def again(state):
        return state[0] < turns

    def more(state):
        turn, *forces = state

        def turn_markers(*refs):
            turn_kernel(grid, steps, cap, *refs)

        def add_markers(*refs):
            more_kernel(cap, steps, planes, width_x, width_y, *refs)

        spec = [pl.BlockSpec(memory_space=pltpu.SMEM)] + [pl.BlockSpec(memory_space=pltpu.VMEM)] * 4
        (outgoing,) = pl.pallas_call(
            turn_markers,
            out_shape=[jax.ShapeDtypeStruct(*message)],
            in_specs=spec,
            scratch_shapes=[rows],
            compiler_params=pltpu.CompilerParams(vmem_limit_bytes=24 * 1024 * 1024),
        )(turn.reshape(1), *markers)
        return (turn + 1, *call(add_markers, [field] * steps)(send(outgoing), *forces))

    if rounds:
        _, force_0, force_1 = lax.while_loop(again, more, (jnp.int32(1), force_0, force_1))

    (before,) = call(
        first_kernel,
        [((19, planes, tall, width_y), F32)],
        [pltpu.VMEM((4, planes, RING, width_y), F32), pltpu.SemaphoreType.DMA((planes,))],
        fetched=(True,) + (False,) * 3,
    )(populations_in, x_low, x_high, force_0)

    def main(*refs):
        main_kernel(cap, steps, *refs)

    own_field = pltpu.VMEM((3 * planes * width_x, width_y), F32)
    fields, back = call(
        main,
        [(populations_in.shape, F32), ((devices, steps, LANES), F32)],
        [
            pltpu.VMEM((19, planes, tall, LANES), F32),
            pltpu.VMEM((19, planes, tall, wide), F32),
            pltpu.VMEM((4, planes, RING, LANES), F32),
            own_field,
            own_field,
            pltpu.VMEM((8, slots), F32),
            pltpu.VMEM(populations_in.shape, F32),
            pltpu.SemaphoreType.DMA((19,)),
        ],
        stored=(True, False),
    )(before, y_low, y_high, force_0, force_1, own_0, own_1)
    returned = send(back)

    def unpack(*refs):
        unpack_kernel(cap, steps, *refs)

    (velocity,) = call(unpack, [((3, steps, owned), F32)])(returned, slot)
    return fields, by_comp(velocity), turns


def local(*inputs):
    def again(state):
        return state[2] > 1

    def whole(state):
        fields, velocity, _ = run(True, *inputs)
        return fields, velocity, jnp.int32(0)

    fields, velocity, _ = lax.while_loop(again, whole, run(False, *inputs))
    return fields, velocity


def solution(mesh):
    return jax.shard_map(
        local,
        mesh=mesh,
        in_specs=(
            P(None, None, "gx", "gy"),
            P(None, None, ("gx", "gy")),
            P(None, None, ("gx", "gy")),
            P(None, None, ("gx", "gy")),
            P(None, ("gx", "gy"), None),
        ),
        out_specs=(P(None, None, "gx", "gy"), P(None, None, ("gx", "gy"))),
        check_vma=False,
    )
```

```python
import jax
import jax.numpy as jnp
from jax import lax
from jax.experimental import pallas as pl
from jax.experimental.pallas import tpu as pltpu
from jax.sharding import PartitionSpec as P

LATTICE = [
    (0, 0, 0),
    (1, 0, 0),
    (-1, 0, 0),
    (0, 1, 0),
    (0, -1, 0),
    (0, 0, 1),
    (0, 0, -1),
    (1, 1, 0),
    (-1, -1, 0),
    (1, -1, 0),
    (-1, 1, 0),
    (1, 0, 1),
    (-1, 0, -1),
    (1, 0, -1),
    (-1, 0, 1),
    (0, 1, 1),
    (0, -1, -1),
    (0, 1, -1),
    (0, -1, 1),
]
WEIGHTS = [1.0 / 3.0] + [1.0 / 18.0] * 6 + [1.0 / 36.0] * 12
relax_time = 0.8
OMEGA = 1.0 / relax_time
SOURCE = 1.0 - 0.5 / relax_time
LANES = 128

BF = jnp.bfloat16
F32 = jnp.float32


def split2(x):
    high = x.astype(BF)
    low = (x - high.astype(F32)).astype(BF)
    return high, low


def split3(x):
    high = x.astype(BF)
    rest = x - high.astype(F32)
    middle = rest.astype(BF)
    low = (rest - middle.astype(F32)).astype(BF)
    return high, middle, low


def nt(a, b):
    return lax.dot_general(a, b, (((1,), (1,)), ((), ())), preferred_element_type=F32)


def nn(a, b):
    return lax.dot_general(a, b, (((1,), (0,)), ((), ())), preferred_element_type=F32)


def iota(shape, dim):
    return lax.broadcasted_iota(jnp.int32, shape, dim)


RING = 8
SIDE = LANES


def slot_table(slot, slots):
    owned = slot.shape[1]
    return jnp.where(iota((slots, owned), 0) == slot, 1.0, 0.0).astype(BF)


def fetch(pairs, sems):
    copies = [pltpu.make_async_copy(source, target, sems.at[n]) for n, (source, target) in enumerate(pairs)]
    for copy in copies:
        copy.start()
    return copies


def ghosts(step, steps, count_gx, count_gy, width_x, width_y, tiles, cell_x, cell_y):
    reach = steps - step
    tiles = tiles.astype(F32)
    gx = jnp.floor((tiles + 0.5) * (1.0 / count_gy))
    along = []
    for cell, width, place, count in (
        (cell_x, width_x, gx, count_gx),
        (cell_y, width_y, tiles - gx * count_gy, count_gy),
    ):
        above, below = cell >= width - 1 - reach, cell <= reach - 1
        place_up = jnp.where(place == count - 1, 0.0, place + 1.0)
        place_down = jnp.where(place == 0, count - 1.0, place - 1.0)
        along.append((jnp.where(above | below, 1.0, 0.0), place, jnp.where(above, place_up, place_down)))
    (near_x, here_x, there_x), (near_y, here_y, there_y) = along
    return [
        jnp.where(near_x > 0, there_x * count_gy + here_y, -1.0),
        jnp.where(near_y > 0, here_x * count_gy + there_y, -1.0),
        jnp.where(near_x * near_y > 0, there_x * count_gy + there_y, -1.0),
    ]


def pack(grid, steps, cap, step_rows, out_ref, slot_ref, rows, turn=None):
    count_gx, count_gy, width_x, width_y = grid
    devices, half = count_gx * count_gy, cap // 2
    owned = rows.shape[1]
    slots, spare = devices * cap, devices * half
    earlier = jnp.where(iota((owned, owned), 0) < iota((owned, owned), 1), 1.0, 0.0).astype(BF)
    column = iota((devices, owned), 0).astype(F32)
    octets, extras, most = [], [], []
    given = [step_rows(step) for step in range(steps)]
    asked = []
    for step, (tiles, values) in enumerate(given):
        asked.append([tiles.astype(F32)] + ghosts(step, steps, *grid, tiles, values[0], values[1]))
    member = [[jnp.where(column == tile, 1.0, 0.0) for tile in tiles] for tiles in asked]
    before = nn(jnp.concatenate(sum(member, []), axis=0).astype(BF), earlier)
    before = [before[n * devices : (n + 1) * devices] for n in range(4 * steps)]
    for step, (tiles, values) in enumerate(given):
        if turn is None:
            rank = jnp.sum(before[4 * step] * member[step][0], axis=0, keepdims=True)
            slot = tiles * cap + rank.astype(jnp.int32)
            slot_ref[step : step + 1, :] = slot
            rows[...] = jnp.zeros_like(rows)
            for number, value in enumerate(values):
                rows[number : number + 1, :] = value
            packed = nt(jnp.concatenate(split3(rows[...]), axis=0), slot_table(slot, slots))
            packed = packed[0:16] + packed[16:32] + packed[32:48]
            octets.append((packed[0:8], packed[8:16]))
        taken = [jnp.zeros((devices, 1), F32)]
        places = []
        for number in range(1, 4):
            here = member[step][number]
            rank = jnp.sum((before[4 * step + number] + taken[-1]) * here, axis=0, keepdims=True)
            taken.append(taken[-1] + jnp.sum(here, axis=1, keepdims=True))
            if turn is not None:
                rank = rank - turn * half
            tile = asked[step][number]
            places.append(jnp.where((tile >= 0) & (rank >= 0) & (rank < half), tile * half + rank, -1.0).astype(jnp.int32))
        grid_slots = iota((spare, owned), 0)
        chosen = (grid_slots == places[0]) | (grid_slots == places[1]) | (grid_slots == places[2])
        rows[...] = jnp.zeros_like(rows)
        for place, value in zip((1, 2, 3, 4, 5, 6, 7, 9, 10), values):
            rows[place : place + 1, :] = value
        extra = nt(jnp.concatenate(split3(rows[...]), axis=0), jnp.where(chosen, 1.0, 0.0).astype(BF))
        extra = extra[0:16] + extra[16:32] + extra[32:48]
        lanes, sender = iota((devices, spare), 1), iota((devices, spare), 0)
        ends = [
            jnp.sum(jnp.where(lanes // half == sender, end, 0.0), axis=0, keepdims=True) for end in (taken[1], taken[2])
        ]
        rank = (iota((1, spare), 1) % half).astype(F32)
        if turn is not None:
            rank = rank + turn * half
        in_x = (rank < ends[0]) | (rank >= ends[1])
        in_y = rank >= ends[0]
        first = []
        for cell, width, moved in ((extra[1:2], width_x, in_x), (extra[2:3], width_y, in_y)):
            first.append(cell + jnp.where(moved, jnp.where(cell * 2 < width, width * 1.0, -1.0 * width), 0.0))
        extras.append((jnp.concatenate([extra[0:1]] + first + [extra[3:8]], axis=0), extra[8:16]))
        most.append(jnp.max(taken[3], axis=0, keepdims=True))
    lane, row = iota((8, LANES), 1), iota((8, LANES), 0)

    def placed(octet, device, width, offset):
        line, place = device * width // LANES, device * width % LANES
        piece = octet[:, line * LANES : (line + 1) * LANES]
        shift = (offset - place) % LANES
        if shift:
            piece = pltpu.roll(piece, shift, 1)
        return jnp.where((lane >= offset) & (lane < offset + width), piece, 0.0)

    heading = jnp.zeros((8, LANES), F32)
    for step in range(steps):
        start = (2 * step + 1) * cap + half
        heading = jnp.where((row == 3) & (lane >= start) & (lane < start + half), most[step], heading)
    for device in range(devices):
        block = heading
        for step in range(steps):
            start = 2 * step * cap
            if turn is None:
                block = block + placed(octets[step][0], device, cap, start)
                block = block + placed(octets[step][1], device, cap, start + cap)
            block = block + placed(extras[step][0], device, half, start + cap)
            block = block + placed(extras[step][1], device, half, start + cap + half)
        out_ref[device] = block


def marker_rows(tile_ref, cell_ref, frac_ref, force_ref):
    lines = cell_ref.shape[2] // LANES

    def step_rows(step):
        tiles = jnp.concatenate(
            [tile_ref[step * lines + r : step * lines + r + 1, :] for r in range(lines)], axis=1
        )
        values = [cell_ref[n, step : step + 1, :].astype(F32) for n in range(3)]
        values += [frac_ref[n, step : step + 1, :] for n in range(3)]
        values += [force_ref[n, step : step + 1, :] for n in range(3)]
        return tiles, values

    return step_rows


def pack_kernel(
    grid, steps, cap, tile_in, cell_in, frac_in, force_in, out_ref, slot_ref,
    rows, tile_ref, cell_ref, frac_ref, force_ref, sems,
):
    copies = fetch([(tile_in, tile_ref), (cell_in, cell_ref), (frac_in, frac_ref), (force_in, force_ref)], sems)
    for copy in copies:
        copy.wait()
    pack(grid, steps, cap, marker_rows(tile_ref, cell_ref, frac_ref, force_ref), out_ref, slot_ref, rows)


def columns_kernel(f_in, after_ref, up, down, far_ref, near_ref, sems):
    width_y = f_in.shape[3]
    copies = fetch(
        [
            (f_in.at[:, :, :, pl.ds(width_y - LANES, LANES)], far_ref),
            (f_in.at[:, :, :, pl.ds(0, LANES)], near_ref),
        ],
        sems,
    )
    for copy, out, source, at in ((copies[0], up, far_ref, LANES - 2), (copies[1], down, near_ref, 0)):
        copy.wait()
        columns(source, out, at)


def face_rows(members, planes):
    first = 19 * planes
    second = {member: first + n * planes for n, member in enumerate(members)}
    return first, second, first + len(members) * planes


def strips_kernel(f_in, after_ref, x_up, x_down, near_ref, far_ref, sems):
    planes, width_x = f_in.shape[1], f_in.shape[2]
    copies = fetch(
        [
            (f_in.at[:, :, pl.ds(width_x - 8, 8), :], far_ref),
            (f_in.at[:, :, pl.ds(0, 8), :], near_ref),
        ],
        sems,
    )
    for copy, out, source, members, row, inner in (
        (copies[0], x_up, far_ref, X_UP, 7, 6),
        (copies[1], x_down, near_ref, X_DOWN, 0, 1),
    ):
        copy.wait()
        _, second, third = face_rows(members, planes)
        for z in range(planes):
            for member in range(19):
                at = member * planes + z
                out[at : at + 1, :] = source[member, z, row : row + 1, :]
            for member, at in second.items():
                out[at + z : at + z + 1, :] = source[member, z, inner : inner + 1, :]
            density, momenta = moments([source[member, z] for member in range(19)])
            for number, value in enumerate([density] + momenta):
                at = third + number * planes + z
                out[at : at + 1, :] = value[inner : inner + 1]


def turn_kernel(grid, steps, cap, turn_ref, tile_ref, cell_ref, frac_ref, force_ref, out_ref, rows):
    step_rows = marker_rows(tile_ref, cell_ref, frac_ref, force_ref)
    pack(grid, steps, cap, step_rows, out_ref, None, rows, turn_ref[0].astype(F32))


def gather(recv_ref, offset, width):
    devices = recv_ref.shape[0]
    per = LANES // width
    group = iota((8, LANES), 1) // width
    pieces = []
    for line in range(devices // per):
        total = jnp.zeros((8, LANES), F32)
        for place in range(per):
            piece = recv_ref[line * per + place]
            shift = (place * width - offset) % LANES
            if shift:
                piece = pltpu.roll(piece, shift, 1)
            total = jnp.where(group == place, piece, total)
        pieces.append(total)
    return jnp.concatenate(pieces, axis=1)


def unpack_kernel(cap, steps, recv_ref, slot_ref, out_ref):
    devices = recv_ref.shape[0]
    per = LANES // cap
    group = iota((steps, LANES), 1) // cap
    comps = []
    for number in range(3):
        pieces = []
        for line in range(devices // per):
            total = jnp.zeros((steps, LANES), F32)
            for place in range(per):
                piece = recv_ref[line * per + place]
                shift = (place - number) * cap % LANES
                if shift:
                    piece = pltpu.roll(piece, shift, 1)
                total = jnp.where(group == place, piece, total)
            pieces.append(total)
        comps.append(jnp.concatenate(pieces, axis=1))
    slots = devices * cap
    for step in range(steps):
        rows = jnp.concatenate([comp[step : step + 1] for comp in comps] + [jnp.zeros((13, slots), F32)], axis=0)
        found = nn(jnp.concatenate(split3(rows), axis=0), slot_table(slot_ref[step : step + 1, :], slots))
        found = found[0:8] + found[16:24] + found[32:40]
        for number in range(3):
            out_ref[number, step : step + 1, :] = found[number : number + 1]


def line_weights(cell, frac, extent):
    grid = iota((extent, cell.shape[1]), 0).astype(F32)
    return jnp.where(grid == cell, 1.0 - frac, jnp.where(grid == cell + 1.0, frac, 0.0))


def y_table(cell, frac, extent):
    grid = iota((extent, cell.shape[1]), 0).astype(F32)
    lower, upper = grid == cell, grid == cell + 1.0
    tables = []
    for low, high in zip(split2(1.0 - frac), split2(frac)):
        low, high = low.astype(F32), high.astype(F32)
        tables.append(jnp.where(lower, low, jnp.where(upper, high, 0.0)).astype(BF))
    return tables


def plane_table(rows, planes, width_x):
    kernel_x = line_weights(rows[0:1], rows[3:4], width_x)
    kernel_z = line_weights(rows[2:3], rows[5:6], 8)
    return [kernel_z[z : z + 1] * kernel_x for z in range(planes)]


def product(table, along_y):
    high, low = split2(table)
    high_y, low_y = along_y
    return nt(
        jnp.concatenate([high, low, high], axis=1), jnp.concatenate([high_y, high_y, low_y], axis=1)
    )


def spread_own(first, second, planes, width_x, width_y, force_ref):
    tall = width_x + RING
    table = jnp.concatenate(plane_table(first, planes, width_x), axis=0)
    along_y = y_table(first[1:2], first[4:5], width_y)
    strengths = (first[6:7], first[7:8], second[0:1])
    found = product(jnp.concatenate([table * strength for strength in strengths], axis=0), along_y)
    for number in range(3 * planes):
        force_ref[number * tall : number * tall + width_x, 0:width_y] = found[number * width_x : (number + 1) * width_x]


def spread_ghosts(first, second, planes, width_x, width_y, force_ref, add):
    tall, wide = width_x + RING, width_y + SIDE
    cell_x = jnp.where(first[1:2] < 0, first[1:2] + tall, first[1:2])
    cell_y = jnp.where(first[2:3] < 0, first[2:3] + wide, first[2:3])
    kernel_x = line_weights(cell_x, first[4:5], tall)
    kernel_z = line_weights(first[3:4], first[6:7], 8)
    along_y = y_table(cell_y, first[5:6], wide)
    side_y = [table[width_y:] for table in along_y]
    ring = [kernel_z[z : z + 1] * kernel_x[width_x:] for z in range(planes)]
    side = [kernel_z[z : z + 1] * kernel_x[0:width_x] for z in range(planes)]
    ring, side = jnp.concatenate(ring, axis=0), jnp.concatenate(side, axis=0)
    strengths = (first[7:8], second[1:2], second[2:3])
    found_ring = product(jnp.concatenate([ring * strength for strength in strengths], axis=0), along_y)
    found_side = product(jnp.concatenate([side * strength for strength in strengths], axis=0), side_y)
    for number in range(3 * planes):
        at = number * tall
        part_ring = found_ring[number * RING : (number + 1) * RING]
        part_side = found_side[number * width_x : (number + 1) * width_x]
        if add:
            part_ring = part_ring + force_ref[at + width_x : at + tall, :]
            part_side = part_side + force_ref[at : at + width_x, width_y:]
        force_ref[at + width_x : at + tall, :] = part_ring
        force_ref[at : at + width_x, width_y:] = part_side


def spread_kernel(cap, steps, planes, width_x, width_y, recv_ref, *refs):
    forces, owns, turns_ref = refs[:steps], refs[steps : 2 * steps], refs[2 * steps]
    half = cap // 2
    most = jnp.zeros((1, recv_ref.shape[0] * half), F32)
    for step in range(steps):
        start = 2 * step * cap
        first = gather(recv_ref, start, cap)
        owns[step][...] = first
        second = gather(recv_ref, start + cap, cap)
        spread_own(first, second, planes, width_x, width_y, forces[step])
        first = gather(recv_ref, start + cap, half)
        second = gather(recv_ref, start + cap + half, half)
        spread_ghosts(first, second, planes, width_x, width_y, forces[step], False)
        most = jnp.maximum(most, second[3:4])
    turns_ref[0] = (jnp.max(most).astype(jnp.int32) + half - 1) // half


def more_kernel(cap, steps, planes, width_x, width_y, recv_ref, *refs):
    half = cap // 2
    for step in range(steps):
        start = (2 * step + 1) * cap
        force_ref = refs[steps + step]
        force_ref[...] = refs[step][...]
        first, second = gather(recv_ref, start, half), gather(recv_ref, start + half, half)
        spread_ghosts(first, second, planes, width_x, width_y, force_ref, True)


def sample(first, planes, width_x, width_y, probe_ref):
    table = jnp.concatenate(plane_table(first, planes, width_x), axis=0)
    along_y = y_table(first[1:2], first[4:5], width_y)
    size = planes * width_x
    high, low = split2(probe_ref[...])
    high_y, low_y = along_y
    found = nn(jnp.concatenate([high, low, high], axis=1), jnp.concatenate([high_y, high_y, low_y], axis=0))
    rows = [jnp.sum(found[n * size : (n + 1) * size] * table, axis=0, keepdims=True) for n in range(3)]
    return rows


def moments(f):
    density = f[0]
    diff = {}
    for member in range(1, 19, 2):
        density = density + (f[member] + f[member + 1])
        diff[member] = f[member] - f[member + 1]
    momenta = []
    for number in range(3):
        total = None
        for member in range(1, 19, 2):
            sign = LATTICE[member][number]
            if sign == 0:
                continue
            if total is None:
                total = diff[member] if sign == 1 else -diff[member]
            else:
                total = total + diff[member] if sign == 1 else total - diff[member]
        momenta.append(total)
    return density, momenta


def dot_c(vector, comps):
    total = None
    for number in range(3):
        if vector[number] == 0:
            continue
        if total is None:
            total = comps[number] if vector[number] == 1 else -comps[number]
        else:
            total = total + comps[number] if vector[number] == 1 else total - comps[number]
    return total


def collide(f, density, momenta, force):
    inverse = 1.0 / density
    speed = [(momenta[n] + 0.5 * force[n]) * inverse for n in range(3)]
    scaled = OMEGA * density
    speed_sq = speed[0] * speed[0] + speed[1] * speed[1] + speed[2] * speed[2]
    along = speed[0] * force[0] + speed[1] * force[1] + speed[2] * force[2]
    base = scaled * (1.0 - 1.5 * speed_sq) - (3.0 * SOURCE) * along
    flow = [scaled * speed[n] for n in range(3)]
    pull = [(3.0 * SOURCE) * force[n] for n in range(3)]
    linear = [3.0 * flow[n] + pull[n] for n in range(3)]
    square = [4.5 * flow[n] + 3.0 * pull[n] for n in range(3)]
    posts = [(1.0 - OMEGA) * f[0] + WEIGHTS[0] * base]
    for member in range(1, 19, 2):
        vector = LATTICE[member]
        even = WEIGHTS[member] * (base + dot_c(vector, speed) * dot_c(vector, square))
        odd = WEIGHTS[member] * dot_c(vector, linear)
        posts.append((1.0 - OMEGA) * f[member] + (even + odd))
        posts.append((1.0 - OMEGA) * f[member + 1] + (even - odd))
    return posts


def columns(source, out, at):
    planes, width_x = source.shape[1], source.shape[2]
    lane = iota((width_x, LANES), 1)
    lines = out.shape[1] // LANES
    totals = [jnp.zeros((width_x, LANES), F32) for _ in range(lines)]
    for plane in range(19 * planes):
        line, target = divmod(2 * plane, LANES)
        block = source[plane // planes, plane % planes]
        shift = (target - at) % LANES
        if shift:
            block = pltpu.roll(block, shift, 1)
        totals[line] = jnp.where((lane == target) | (lane == target + 1), block, totals[line])
    for line in range(lines):
        out[:, line * LANES : (line + 1) * LANES] = totals[line]


def corner_kernel(up, down, x_low, x_high, after_0, after_1, out_up, out_down):
    width_x, width_y = up.shape[0], x_low.shape[1]
    count = x_low.shape[0]
    pad = jnp.zeros((LANES - count, LANES), F32)
    for source, out, start, at in ((up, out_up, width_y - LANES, LANES - 2), (down, out_down, 0, 0)):
        out[0:width_x, :] = source[...]
        out[width_x:, :] = jnp.zeros((out.shape[0] - width_x, out.shape[1]), F32)
        for number, halo in enumerate((x_low, x_high)):
            turned = jnp.transpose(jnp.concatenate([halo[:, start : start + LANES], pad], axis=0))
            row = width_x + 2 * number
            out[row : row + 2, 0:LANES] = turned[at : at + 2]


def ring_rows(x_low, x_high, f_ref, ring_ref):
    planes, tall = f_ref.shape[1], f_ref.shape[2]
    for halo, members, row, inner in ((x_low, X_UP, RING - 1, RING - 2), (x_high, X_DOWN, 0, 1)):
        _, second, third = face_rows(members, planes)
        for z in range(planes):
            for member in range(19):
                places = [(row, member * planes + z)]
                if member in second:
                    places.append((inner, second[member] + z))
                for line, at in places:
                    line += tall - RING
                    f_ref[member, z, line : line + 1, :] = halo[at : at + 1, :]
            for number in range(4):
                at = third + number * planes + z
                ring_ref[number, z, inner : inner + 1, :] = halo[at : at + 1, :]


def side_cells(y_low, y_high, f_ref, ring_ref):
    planes, tall = f_ref.shape[1], f_ref.shape[2]
    width_x = tall - RING
    lane = iota((width_x, LANES), 1)
    wide_lane = iota((LANES, LANES), 1)
    pad = jnp.zeros((LANES - 8, LANES), F32)
    low = jnp.transpose(jnp.concatenate([y_low[width_x:, 0:LANES], pad], axis=0))
    high = jnp.transpose(jnp.concatenate([y_high[width_x:, 0:LANES], pad], axis=0))
    near = wide_lane >= LANES - 2
    ring_rows(
        jnp.where(near, pltpu.roll(low, LANES - 2, 1), high),
        jnp.where(near, pltpu.roll(low, LANES - 4, 1), pltpu.roll(high, LANES - 2, 1)),
        f_ref,
        ring_ref,
    )
    for plane in range(19 * planes):
        line, here = divmod(2 * plane, LANES)
        below = y_low[0:width_x, line * LANES : (line + 1) * LANES]
        above = y_high[0:width_x, line * LANES : (line + 1) * LANES]
        if (LANES - 2 - here) % LANES:
            below = pltpu.roll(below, (LANES - 2 - here) % LANES, 1)
        if here:
            above = pltpu.roll(above, LANES - here, 1)
        f_ref[plane // planes, plane % planes, 0:width_x, :] = jnp.where(lane >= LANES - 2, below, above)


def shifted(block, member):
    along_x, along_y, _ = LATTICE[member]
    if along_x:
        block = pltpu.roll(block, along_x % block.shape[0], 0)
    if along_y:
        block = pltpu.roll(block, along_y % block.shape[1], 1)
    return block


X_UP = [i for i in range(19) if LATTICE[i][0] == 1]
X_DOWN = [i for i in range(19) if LATTICE[i][0] == -1]
RUNS = [(0, 1, 0, 0), (1, 2, 1, 0), (3, 2, 0, 1), (5, 2, 0, 0), (7, 4, 1, 1), (11, 4, 1, 0), (15, 4, 0, 1)]
MOVED = [i for i in range(19) if LATTICE[i][0] or LATTICE[i][1]]


def force_at(ref, planes, tall, z, row, lanes):
    return [ref[pl.ds(pl.multiple_of((n * planes + z) * tall + row, 8), 8), lanes] for n in range(3)]


def for_rows(planes, width_x, body):
    @pl.loop(0, planes * (width_x // 8))
    def _(index):
        row = pl.multiple_of((index % (width_x // 8)) * 8, 8)
        body(index // (width_x // 8), row, pl.multiple_of(index * 8, 8))


def collide_block(f_ref, ring_ref, force_ref, z, row, lanes, force_lanes):
    planes, tall = f_ref.shape[1], f_ref.shape[2]
    at = pl.ds(row, 8)
    f = [f_ref[member, z, at, lanes] for member in range(19)]
    density, momenta = moments(f)
    if ring_ref is not None:
        outer = (iota((8, LANES), 0) == 1) | (iota((8, LANES), 0) == RING - 2)
        density = jnp.where(outer, ring_ref[0, z, :, lanes], density)
        momenta = [jnp.where(outer, ring_ref[n + 1, z, :, lanes], momenta[n]) for n in range(3)]
    force = force_at(force_ref, planes, tall, z, row, force_lanes)
    for member, value in enumerate(collide(f, density, momenta, force)):
        f_ref[member, z, at, lanes] = value


def first_kernel(f_in, x_low, x_high, force_ref, f_ref, ring_ref, sems):
    planes, width_x, width_y = f_in.shape[1], f_in.shape[2], f_in.shape[3]
    copies = fetch([(f_in.at[:, z], f_ref.at[:, z, pl.ds(0, width_x), :]) for z in range(planes)], sems)
    ring_rows(x_low, x_high, f_ref, ring_ref)

    @pl.loop(0, planes)
    def _(z):
        for start in range(0, width_y, LANES):
            lanes = pl.ds(start, LANES)
            collide_block(f_ref, ring_ref, force_ref, z, width_x, lanes, lanes)

    for z in range(planes):
        copies[z].wait()

        @pl.loop(0, width_x // 8)
        def _(index):
            row = pl.multiple_of(index * 8, 8)
            for start in range(0, width_y, LANES):
                lanes = pl.ds(start, LANES)
                collide_block(f_ref, None, force_ref, z, row, lanes, lanes)


def main_kernel(
    cap, steps, before, y_low, y_high, force_0, force_1, own_0, own_1, after_hbm, back_ref,
    side, after, ring_ref, probe_0, probe_1, rows, sems,
):
    planes, tall, width_y = before.shape[1], before.shape[2], before.shape[3]
    width_x, wide = tall - RING, after.shape[3]
    side_cells(y_low, y_high, side, ring_ref)
    far, all_lanes = pl.ds(width_y, LANES), pl.ds(0, LANES)

    def side_body(z, row, flat):
        collide_block(side, None, force_0, z, row, all_lanes, far)

    for_rows(planes, width_x, side_body)

    @pl.loop(0, planes)
    def _(z):
        collide_block(side, ring_ref, force_0, z, width_x, all_lanes, far)

    for member in MOVED:
        for z in range(planes):
            block = jnp.concatenate([before[member, z], side[member, z]], axis=1)
            after[member, (z + LATTICE[member][2]) % planes] = shifted(block, member)

    def second_block(z, row, start, flat=None, kept=range(19)):
        at, lanes = pl.ds(row, 8), pl.ds(start, LANES)
        f = []
        for member in range(19):
            if member in MOVED:
                f.append(after[member, z, at, lanes])
                continue
            other = (z - LATTICE[member][2]) % planes
            f.append(before[member, other, at, lanes] if start < width_y else side[member, other, at, all_lanes])
        density, momenta = moments(f)
        if flat is not None:
            inverse = 1.0 / density
            for number, force in enumerate(force_at(force_0, planes, tall, z, row, lanes)):
                probe_0[pl.ds(pl.multiple_of(number * planes * width_x + flat, 8), 8), lanes] = (
                    momenta[number] + 0.5 * force
                ) * inverse
        values = collide(f, density, momenta, force_at(force_1, planes, tall, z, row, lanes))
        for member in kept:
            after[member, z, at, lanes] = values[member]

    copies = []
    for z in range(planes):

        @pl.loop(0, width_x // 8)
        def _(index):
            row = pl.multiple_of(index * 8, 8)
            for start in range(0, width_y, LANES):
                second_block(z, row, start, pl.multiple_of(z * width_x + row, 8))
            second_block(z, row, width_y, kept=[i for i in range(19) if LATTICE[i][1]])

        for start in range(0, wide, LANES):
            second_block(z, width_x, start, kept=[i for i in range(19) if LATTICE[i][0]])
        for number, (first, count, along_x, along_y) in enumerate(RUNS):
            part = (pl.ds(first, count), z, pl.ds(0, tall if along_x else width_x), pl.ds(0, wide if along_y else width_y))
            copies.append(pltpu.make_async_copy(after.at[part], after_hbm.at[part], sems.at[len(RUNS) * z + number]))
            copies[-1].start()

    def sample_step(step, own_ref, probe_ref):
        for number, row in enumerate(sample(own_ref[...], planes, width_x, width_y, probe_ref)):
            rows[steps * number + step : steps * number + step + 1, :] = row

    sample_step(0, own_0, probe_0)
    for z in range(planes):

        def streamed(along_x, along_y, weight):
            total = None
            rows_used = tall if along_x else width_x
            lanes_used = wide if along_y else width_y
            for member in range(19):
                if LATTICE[member][:2] != (along_x, along_y) or weight(LATTICE[member][2]) == 0:
                    continue
                value = after[member, (z - LATTICE[member][2]) % planes, 0:rows_used, 0:lanes_used]
                value = value if weight(LATTICE[member][2]) > 0 else -value
                total = value if total is None else total + value
            if along_x:
                total = pltpu.roll(total, along_x % rows_used, 0)
            if along_y:
                total = pltpu.roll(total, along_y % lanes_used, 1)
            return total[0:width_x, 0:width_y]

        here = {(x, y): streamed(x, y, lambda cz: 1) for x in (-1, 0, 1) for y in (-1, 0, 1)}
        density = sum(here.values())
        momenta = [
            sum(here[1, y] - here[-1, y] for y in (-1, 0, 1)),
            sum(here[x, 1] - here[x, -1] for x in (-1, 0, 1)),
            sum(streamed(x, y, lambda cz: cz) for x, y in ((0, 0), (1, 0), (-1, 0), (0, 1), (0, -1))),
        ]
        inverse = 1.0 / density
        for number in range(3):
            at, to = (number * planes + z) * tall, (number * planes + z) * width_x
            probe_1[to : to + width_x, :] = (
                momenta[number] + 0.5 * force_1[at : at + width_x, 0:width_y]
            ) * inverse

    sample_step(1, own_1, probe_1)
    send_back(cap, rows, back_ref)
    for copy in copies:
        copy.wait()


def store_kernel(after_hbm, out_hbm, after, out_ref, sems, out_sems):
    planes, width_x, width_y = out_ref.shape[1], out_ref.shape[2], out_ref.shape[3]
    tall, wide = after.shape[2], after.shape[3]
    parts = [
        (pl.ds(first, count), slice(None), pl.ds(0, tall if along_x else width_x), pl.ds(0, wide if along_y else width_y))
        for first, count, along_x, along_y in RUNS
    ]
    arriving = fetch([(after_hbm.at[part], after.at[part]) for part in parts], sems)
    copies = []
    for copy, (first, count, along_x, along_y) in zip(arriving, RUNS):
        copy.wait()
        for member in range(first, first + count):
            for z in range(planes):
                block = after[member, z, 0 : tall if along_x else width_x, 0 : wide if along_y else width_y]
                out_ref[member, (z + LATTICE[member][2]) % planes] = shifted(block, member)[0:width_x, 0:width_y]
            copies.append(pltpu.make_async_copy(out_ref.at[member], out_hbm.at[member], out_sems.at[member]))
            copies[-1].start()
    for copy in copies:
        copy.wait()


def send_back(cap, rows, out_ref):
    devices, steps = out_ref.shape[0], out_ref.shape[1]
    per = LANES // cap
    group = iota((steps, LANES), 1) // cap
    for device in range(devices):
        line, place = device // per, device % per
        total = jnp.zeros((steps, LANES), F32)
        for number in range(3):
            piece = rows[number * steps : (number + 1) * steps, line * LANES : (line + 1) * LANES]
            shift = (number - place) * cap % LANES
            if shift:
                piece = pltpu.roll(piece, shift, 1)
            total = jnp.where(group == number, piece, total)
        out_ref[device] = total


def call(kernel, outs, scratch=(), flops=0, moved=0, limit=24, fetched=(False,), stored=None):
    shapes = [jax.ShapeDtypeStruct(shape, kind) for shape, kind in outs]
    out_specs = [pl.BlockSpec(memory_space=pltpu.SMEM if len(shape) == 1 else pltpu.VMEM) for shape, _ in outs]
    if stored:
        shapes = [pltpu.HBM(*out) if own else shape for out, shape, own in zip(outs, shapes, stored)]
        out_specs = [pl.BlockSpec(memory_space=pltpu.HBM if own else pltpu.VMEM) for own in stored]
    places = {True: pltpu.HBM, False: pltpu.VMEM, None: pltpu.SMEM}
    specs = [pl.BlockSpec(memory_space=places[own]) for own in fetched]
    made = pl.pallas_call(
        kernel,
        out_shape=shapes,
        out_specs=out_specs,
        scratch_shapes=list(scratch),
        **({"in_specs": specs} if fetched != (False,) else {}),
        cost_estimate=pl.CostEstimate(flops=flops, bytes_accessed=moved, transcendentals=0),
        compiler_params=pltpu.CompilerParams(vmem_limit_bytes=limit * 1024 * 1024),
    )
    if not any(fetched):
        return made
    return lambda *args: made(
        *[pltpu.with_memory_space_constraint(x, pltpu.HBM) if own else x for x, own in zip(args, fetched)]
    )


def pair(up, down, axis):
    count = lax.axis_size(axis)
    forward = [(i, (i + 1) % count) for i in range(count)]
    backward = [(target, source) for source, target in forward]
    return lax.ppermute(up, axis, forward), lax.ppermute(down, axis, backward)


def run(rounds, populations_in, marker_force, marker_frac, marker_cell, marker_tile):
    count_gx, count_gy = lax.axis_size("gx"), lax.axis_size("gy")
    devices = count_gx * count_gy
    steps, owned = marker_force.shape[0], marker_force.shape[2]
    cap = max(2, 2 * owned // devices)
    half, slots = cap // 2, devices * cap
    planes, width_x, width_y = populations_in.shape[1:]
    tall, wide = width_x + RING, width_y + SIDE
    grid = (count_gx, count_gy, width_x, width_y)
    by_comp = lambda x: jnp.transpose(x, (1, 0, 2))
    markers = (
        marker_tile.reshape(steps * owned // LANES, LANES),
        by_comp(marker_cell),
        by_comp(marker_frac),
        by_comp(marker_force),
    )
    message = ((devices, 8, LANES), F32)
    rows = pltpu.VMEM((16, owned), F32)

    def send(outgoing):
        return lax.all_to_all(outgoing, ("gx", "gy"), split_axis=0, concat_axis=0, tiled=True)

    def pack_markers(*refs):
        pack_kernel(grid, steps, cap, *refs)

    face = (((19 + len(X_UP) + 4) * planes, width_y), F32)
    packed = -(-2 * 19 * planes // LANES) * LANES
    outgoing, slot = call(
        pack_markers,
        [message, ((steps, owned), jnp.int32)],
        [
            rows,
            pltpu.VMEM((steps * owned // LANES, LANES), jnp.int32),
            pltpu.VMEM((3, steps, owned), jnp.int32),
            pltpu.VMEM((3, steps, owned), F32),
            pltpu.VMEM((3, steps, owned), F32),
            pltpu.SemaphoreType.DMA((4,)),
        ],
        fetched=(True,) * 4,
    )(*markers)
    x_up, x_down = call(
        strips_kernel,
        [face, face],
        [
            pltpu.VMEM((19, planes, 8, width_y), F32),
            pltpu.VMEM((19, planes, 8, width_y), F32),
            pltpu.SemaphoreType.DMA((2,)),
        ],
        fetched=(True, False),
    )(populations_in, slot)
    y_up, y_down = call(
        columns_kernel,
        [((width_x, packed), F32)] * 2,
        [
            pltpu.VMEM((19, planes, width_x, LANES), F32),
            pltpu.VMEM((19, planes, width_x, LANES), F32),
            pltpu.SemaphoreType.DMA((2,)),
        ],
        fetched=(True, False),
    )(populations_in, x_up)
    arrived = send(outgoing)

    x_low, x_high = pair(x_up, x_down, "gx")
    field = ((3 * planes * tall, wide), F32)

    def spread_markers(*refs):
        spread_kernel(cap, steps, planes, width_x, width_y, *refs)

    force_0, force_1, own_0, own_1, turns = call(
        spread_markers, [field] * steps + [((8, slots), F32)] * steps + [((1,), jnp.int32)]
    )(arrived)
    turns = turns.reshape(())

    y_up, y_down = call(corner_kernel, [((width_x + 8, packed), F32)] * 2)(y_up, y_down, x_low, x_high, own_0, own_1)
    y_low, y_high = pair(y_up, y_down, "gy")

    def again(state):
        return state[0] < turns

    def more(state):
        turn, *forces = state

        def turn_markers(*refs):
            turn_kernel(grid, steps, cap, *refs)

        def add_markers(*refs):
            more_kernel(cap, steps, planes, width_x, width_y, *refs)

        spec = [pl.BlockSpec(memory_space=pltpu.SMEM)] + [pl.BlockSpec(memory_space=pltpu.VMEM)] * 4
        (outgoing,) = pl.pallas_call(
            turn_markers,
            out_shape=[jax.ShapeDtypeStruct(*message)],
            in_specs=spec,
            scratch_shapes=[rows],
            compiler_params=pltpu.CompilerParams(vmem_limit_bytes=24 * 1024 * 1024),
        )(turn.reshape(1), *markers)
        return (turn + 1, *call(add_markers, [field] * steps)(send(outgoing), *forces))

    if rounds:
        _, force_0, force_1 = lax.while_loop(again, more, (jnp.int32(1), force_0, force_1))

    (before,) = call(
        first_kernel,
        [((19, planes, tall, width_y), F32)],
        [pltpu.VMEM((4, planes, RING, width_y), F32), pltpu.SemaphoreType.DMA((planes,))],
        fetched=(True,) + (False,) * 3,
    )(populations_in, x_low, x_high, force_0)

    def main(*refs):
        main_kernel(cap, steps, *refs)

    own_field = pltpu.VMEM((3 * planes * width_x, width_y), F32)
    after, back = call(
        main,
        [((19, planes, tall, wide), F32), ((devices, steps, LANES), F32)],
        [
            pltpu.VMEM((19, planes, tall, LANES), F32),
            pltpu.VMEM((19, planes, tall, wide), F32),
            pltpu.VMEM((4, planes, RING, LANES), F32),
            own_field,
            own_field,
            pltpu.VMEM((8, slots), F32),
            pltpu.SemaphoreType.DMA((len(RUNS) * planes,)),
        ],
        stored=(True, False),
    )(before, y_low, y_high, force_0, force_1, own_0, own_1)
    (fields,) = call(
        store_kernel,
        [(populations_in.shape, F32)],
        [
            pltpu.VMEM((19, planes, tall, wide), F32),
            pltpu.VMEM(populations_in.shape, F32),
            pltpu.SemaphoreType.DMA((len(RUNS),)),
            pltpu.SemaphoreType.DMA((19,)),
        ],
        fetched=(True,),
        stored=(True,),
    )(after)
    returned = send(back)

    def unpack(*refs):
        unpack_kernel(cap, steps, *refs)

    (velocity,) = call(unpack, [((3, steps, owned), F32)])(returned, slot)
    return fields, by_comp(velocity), turns


def local(*inputs):
    def again(state):
        return state[2] > 1

    def whole(state):
        fields, velocity, _ = run(True, *inputs)
        return fields, velocity, jnp.int32(0)

    fields, velocity, _ = lax.while_loop(again, whole, run(False, *inputs))
    return fields, velocity


def solution(mesh):
    return jax.shard_map(
        local,
        mesh=mesh,
        in_specs=(
            P(None, None, "gx", "gy"),
            P(None, None, ("gx", "gy")),
            P(None, None, ("gx", "gy")),
            P(None, None, ("gx", "gy")),
            P(None, ("gx", "gy"), None),
        ),
        out_specs=(P(None, None, "gx", "gy"), P(None, None, ("gx", "gy"))),
        check_vma=False,
    )
```

```python
import jax
import jax.numpy as jnp
from jax import lax
from jax.experimental import pallas as pl
from jax.experimental.pallas import tpu as pltpu
from jax.sharding import PartitionSpec as P

LATTICE = [
    (0, 0, 0),
    (1, 0, 0),
    (-1, 0, 0),
    (0, 1, 0),
    (0, -1, 0),
    (0, 0, 1),
    (0, 0, -1),
    (1, 1, 0),
    (-1, -1, 0),
    (1, -1, 0),
    (-1, 1, 0),
    (1, 0, 1),
    (-1, 0, -1),
    (1, 0, -1),
    (-1, 0, 1),
    (0, 1, 1),
    (0, -1, -1),
    (0, 1, -1),
    (0, -1, 1),
]
WEIGHTS = [1.0 / 3.0] + [1.0 / 18.0] * 6 + [1.0 / 36.0] * 12
relax_time = 0.8
OMEGA = 1.0 / relax_time
SOURCE = 1.0 - 0.5 / relax_time
LANES = 128

BF = jnp.bfloat16
F32 = jnp.float32


def split2(x):
    high = x.astype(BF)
    low = (x - high.astype(F32)).astype(BF)
    return high, low


def nt(a, b):
    return lax.dot_general(a, b, (((1,), (1,)), ((), ())), preferred_element_type=F32)


def nn(a, b):
    return lax.dot_general(a, b, (((1,), (0,)), ((), ())), preferred_element_type=F32)


def iota(shape, dim):
    return lax.broadcasted_iota(jnp.int32, shape, dim)


RING = 8
SIDE = LANES


def gather_lanes(rows, index):
    index = jnp.broadcast_to(index, (8, LANES))
    line, lane = index // LANES, index % LANES
    found = jnp.zeros((8, LANES), F32)
    for number in range(rows.shape[1] // LANES):
        piece = rows[:, number * LANES : (number + 1) * LANES]
        piece = jnp.take_along_axis(piece, lane, axis=1, mode="promise_in_bounds")
        found = jnp.where(line == number, piece, found)
    return found


def fetch(pairs, sems):
    copies = [pltpu.make_async_copy(source, target, sems.at[n]) for n, (source, target) in enumerate(pairs)]
    for copy in copies:
        copy.start()
    return copies


def ghosts(step, steps, count_gx, count_gy, width_x, width_y, tiles, cell_x, cell_y):
    reach = steps - step
    tiles = tiles.astype(F32)
    gx = jnp.floor((tiles + 0.5) * (1.0 / count_gy))
    along = []
    for cell, width, place, count in (
        (cell_x, width_x, gx, count_gx),
        (cell_y, width_y, tiles - gx * count_gy, count_gy),
    ):
        above, below = cell >= width - 1 - reach, cell <= reach - 1
        place_up = jnp.where(place == count - 1, 0.0, place + 1.0)
        place_down = jnp.where(place == 0, count - 1.0, place - 1.0)
        along.append((jnp.where(above | below, 1.0, 0.0), place, jnp.where(above, place_up, place_down)))
    (near_x, here_x, there_x), (near_y, here_y, there_y) = along
    return [
        jnp.where(near_x > 0, there_x * count_gy + here_y, -1.0),
        jnp.where(near_y > 0, here_x * count_gy + there_y, -1.0),
        jnp.where(near_x * near_y > 0, there_x * count_gy + there_y, -1.0),
    ]


def filled(rows, members, ranks, devices, width):
    owned = rows.shape[1]
    number = iota((1, owned), 1) + 1
    digits = [(number % 256).astype(F32), (number // 256).astype(F32)]
    left = jnp.concatenate([jnp.concatenate([m * digit for m in members], axis=1) for digit in digits], axis=0)
    place = (iota((LANES, owned), 0) % width).astype(F32)
    right = jnp.concatenate([jnp.where(place == rank, 1.0, 0.0) for rank in ranks], axis=1)
    found = nt(left.astype(BF), right.astype(BF))
    marker = (found[0:devices] + 256.0 * found[devices:]).astype(jnp.int32) - 1
    per = LANES // width
    group = iota((1, LANES), 1) // width
    halves = ([], [])
    for line in range(devices // per):
        index = marker[line * per : line * per + 1]
        for other in range(1, per):
            index = jnp.where(group == other, marker[line * per + other : line * per + other + 1], index)
        for half, source in zip(halves, (rows[0:8, :], rows[8:16, :])):
            half.append(gather_lanes(source, index))
    return [jnp.concatenate(half, axis=1) for half in halves]


def pack(grid, steps, cap, step_rows, out_ref, slot_ref, rows, turn=None):
    count_gx, count_gy, width_x, width_y = grid
    devices, half = count_gx * count_gy, cap // 2
    owned = rows.shape[1]
    spare = devices * half
    earlier = jnp.where(iota((owned, owned), 0) < iota((owned, owned), 1), 1.0, 0.0).astype(BF)
    column = iota((devices, owned), 0).astype(F32)
    octets, extras, most = [], [], []
    given = [step_rows(step) for step in range(steps)]
    asked = []
    for step, (tiles, values) in enumerate(given):
        asked.append([tiles.astype(F32)] + ghosts(step, steps, *grid, tiles, values[0], values[1]))
    member = [[jnp.where(column == tile, 1.0, 0.0) for tile in tiles] for tiles in asked]
    before = nn(jnp.concatenate(sum(member, []), axis=0).astype(BF), earlier)
    before = [before[n * devices : (n + 1) * devices] for n in range(4 * steps)]
    for step, (tiles, values) in enumerate(given):
        if turn is None:
            rank = jnp.sum(before[4 * step] * member[step][0], axis=0, keepdims=True)
            slot = tiles * cap + rank.astype(jnp.int32)
            slot_ref[step : step + 1, :] = slot
            rows[...] = jnp.zeros_like(rows)
            for number, value in enumerate(values):
                rows[number : number + 1, :] = value
            octets.append(filled(rows, [member[step][0]], [rank], devices, cap))
        taken = [jnp.zeros((devices, 1), F32)]
        ranks = []
        for number in range(1, 4):
            here = member[step][number]
            rank = jnp.sum((before[4 * step + number] + taken[-1]) * here, axis=0, keepdims=True)
            taken.append(taken[-1] + jnp.sum(here, axis=1, keepdims=True))
            ranks.append(rank if turn is None else rank - turn * half)
        rows[...] = jnp.zeros_like(rows)
        for place, value in zip((1, 2, 3, 4, 5, 6, 7, 9, 10), values):
            rows[place : place + 1, :] = value
        extra, more_extra = filled(rows, member[step][1:], ranks, devices, half)
        lanes, sender = iota((devices, spare), 1), iota((devices, spare), 0)
        ends = [
            jnp.sum(jnp.where(lanes // half == sender, end, 0.0), axis=0, keepdims=True) for end in (taken[1], taken[2])
        ]
        rank = (iota((1, spare), 1) % half).astype(F32)
        if turn is not None:
            rank = rank + turn * half
        in_x = (rank < ends[0]) | (rank >= ends[1])
        in_y = rank >= ends[0]
        first = []
        for cell, width, moved in ((extra[1:2], width_x, in_x), (extra[2:3], width_y, in_y)):
            first.append(cell + jnp.where(moved, jnp.where(cell * 2 < width, width * 1.0, -1.0 * width), 0.0))
        extras.append((jnp.concatenate([extra[0:1]] + first + [extra[3:8]], axis=0), more_extra))
        most.append(jnp.max(taken[3], axis=0, keepdims=True))
    lane, row = iota((8, LANES), 1), iota((8, LANES), 0)

    def placed(octet, device, width, offset):
        line, place = device * width // LANES, device * width % LANES
        piece = octet[:, line * LANES : (line + 1) * LANES]
        shift = (offset - place) % LANES
        if shift:
            piece = pltpu.roll(piece, shift, 1)
        return jnp.where((lane >= offset) & (lane < offset + width), piece, 0.0)

    heading = jnp.zeros((8, LANES), F32)
    for step in range(steps):
        start = (2 * step + 1) * cap + half
        heading = jnp.where((row == 3) & (lane >= start) & (lane < start + half), most[step], heading)
    for device in range(devices):
        block = heading
        for step in range(steps):
            start = 2 * step * cap
            if turn is None:
                block = block + placed(octets[step][0], device, cap, start)
                block = block + placed(octets[step][1], device, cap, start + cap)
            block = block + placed(extras[step][0], device, half, start + cap)
            block = block + placed(extras[step][1], device, half, start + cap + half)
        out_ref[device] = block


def marker_rows(tile_ref, cell_ref, frac_ref, force_ref):
    lines = cell_ref.shape[2] // LANES

    def step_rows(step):
        tiles = jnp.concatenate(
            [tile_ref[step * lines + r : step * lines + r + 1, :] for r in range(lines)], axis=1
        )
        values = [cell_ref[n, step : step + 1, :].astype(F32) for n in range(3)]
        values += [frac_ref[n, step : step + 1, :] for n in range(3)]
        values += [force_ref[n, step : step + 1, :] for n in range(3)]
        return tiles, values

    return step_rows


def pack_kernel(
    grid, steps, cap, tile_in, cell_in, frac_in, force_in, out_ref, slot_ref,
    rows, tile_ref, cell_ref, frac_ref, force_ref, sems,
):
    copies = fetch([(tile_in, tile_ref), (cell_in, cell_ref), (frac_in, frac_ref), (force_in, force_ref)], sems)
    for copy in copies:
        copy.wait()
    pack(grid, steps, cap, marker_rows(tile_ref, cell_ref, frac_ref, force_ref), out_ref, slot_ref, rows)


def columns_kernel(f_in, after_ref, up, down, far_ref, near_ref, sems):
    width_y = f_in.shape[3]
    copies = fetch(
        [
            (f_in.at[:, :, :, pl.ds(width_y - LANES, LANES)], far_ref),
            (f_in.at[:, :, :, pl.ds(0, LANES)], near_ref),
        ],
        sems,
    )
    for copy, out, source, at in ((copies[0], up, far_ref, LANES - 2), (copies[1], down, near_ref, 0)):
        copy.wait()
        columns(source, out, at)


def face_rows(members, planes):
    first = 19 * planes
    second = {member: first + n * planes for n, member in enumerate(members)}
    return first, second, first + len(members) * planes


def strips_kernel(f_in, after_ref, x_up, x_down, near_ref, far_ref, sems):
    planes, width_x = f_in.shape[1], f_in.shape[2]
    copies = fetch(
        [
            (f_in.at[:, :, pl.ds(width_x - 8, 8), :], far_ref),
            (f_in.at[:, :, pl.ds(0, 8), :], near_ref),
        ],
        sems,
    )
    for copy, out, source, members, row, inner in (
        (copies[0], x_up, far_ref, X_UP, 7, 6),
        (copies[1], x_down, near_ref, X_DOWN, 0, 1),
    ):
        copy.wait()
        _, second, third = face_rows(members, planes)
        for z in range(planes):
            for member in range(19):
                at = member * planes + z
                out[at : at + 1, :] = source[member, z, row : row + 1, :]
            for member, at in second.items():
                out[at + z : at + z + 1, :] = source[member, z, inner : inner + 1, :]
            density, momenta = moments([source[member, z] for member in range(19)])
            for number, value in enumerate([density] + momenta):
                at = third + number * planes + z
                out[at : at + 1, :] = value[inner : inner + 1]


def turn_kernel(grid, steps, cap, turn_ref, tile_ref, cell_ref, frac_ref, force_ref, out_ref, rows):
    step_rows = marker_rows(tile_ref, cell_ref, frac_ref, force_ref)
    pack(grid, steps, cap, step_rows, out_ref, None, rows, turn_ref[0].astype(F32))


def gather(recv_ref, offset, width):
    devices = recv_ref.shape[0]
    per = LANES // width
    group = iota((8, LANES), 1) // width
    pieces = []
    for line in range(devices // per):
        total = jnp.zeros((8, LANES), F32)
        for place in range(per):
            piece = recv_ref[line * per + place]
            shift = (place * width - offset) % LANES
            if shift:
                piece = pltpu.roll(piece, shift, 1)
            total = jnp.where(group == place, piece, total)
        pieces.append(total)
    return jnp.concatenate(pieces, axis=1)


def unpack_kernel(cap, steps, recv_ref, slot_ref, out_ref):
    devices = recv_ref.shape[0]
    per = LANES // cap
    group = iota((steps, LANES), 1) // cap
    comps = []
    for number in range(3):
        pieces = []
        for line in range(devices // per):
            total = jnp.zeros((steps, LANES), F32)
            for place in range(per):
                piece = recv_ref[line * per + place]
                shift = (place - number) * cap % LANES
                if shift:
                    piece = pltpu.roll(piece, shift, 1)
                total = jnp.where(group == place, piece, total)
            pieces.append(total)
        comps.append(jnp.concatenate(pieces, axis=1))
    for step in range(steps):
        rows = jnp.concatenate([comp[step : step + 1] for comp in comps] + [jnp.zeros((5, devices * cap), F32)], axis=0)
        for start in range(0, slot_ref.shape[1], LANES):
            found = gather_lanes(rows, slot_ref[step : step + 1, start : start + LANES])
            for number in range(3):
                out_ref[number, step : step + 1, start : start + LANES] = found[number : number + 1]


def line_weights(cell, frac, extent):
    grid = iota((extent, cell.shape[1]), 0).astype(F32)
    return jnp.where(grid == cell, 1.0 - frac, jnp.where(grid == cell + 1.0, frac, 0.0))


def y_table(cell, frac, extent):
    grid = iota((extent, cell.shape[1]), 0).astype(F32)
    lower, upper = grid == cell, grid == cell + 1.0
    tables = []
    for low, high in zip(split2(1.0 - frac), split2(frac)):
        low, high = low.astype(F32), high.astype(F32)
        tables.append(jnp.where(lower, low, jnp.where(upper, high, 0.0)).astype(BF))
    return tables


def plane_table(rows, planes, width_x):
    kernel_x = line_weights(rows[0:1], rows[3:4], width_x)
    kernel_z = line_weights(rows[2:3], rows[5:6], 8)
    return [kernel_z[z : z + 1] * kernel_x for z in range(planes)]


def product(table, along_y):
    high, low = split2(table)
    high_y, low_y = along_y
    return nt(
        jnp.concatenate([high, low, high], axis=1), jnp.concatenate([high_y, high_y, low_y], axis=1)
    )


def spread_own(first, second, planes, width_x, width_y, force_ref):
    tall = width_x + RING
    table = jnp.concatenate(plane_table(first, planes, width_x), axis=0)
    along_y = y_table(first[1:2], first[4:5], width_y)
    strengths = (first[6:7], first[7:8], second[0:1])
    found = product(jnp.concatenate([table * strength for strength in strengths], axis=0), along_y)
    for number in range(3 * planes):
        force_ref[number * tall : number * tall + width_x, 0:width_y] = found[number * width_x : (number + 1) * width_x]


def spread_ghosts(first, second, planes, width_x, width_y, force_ref, add):
    tall, wide = width_x + RING, width_y + SIDE
    cell_x = jnp.where(first[1:2] < 0, first[1:2] + tall, first[1:2])
    cell_y = jnp.where(first[2:3] < 0, first[2:3] + wide, first[2:3])
    kernel_x = line_weights(cell_x, first[4:5], tall)
    kernel_z = line_weights(first[3:4], first[6:7], 8)
    along_y = y_table(cell_y, first[5:6], wide)
    side_y = [table[width_y:] for table in along_y]
    ring = [kernel_z[z : z + 1] * kernel_x[width_x:] for z in range(planes)]
    side = [kernel_z[z : z + 1] * kernel_x[0:width_x] for z in range(planes)]
    ring, side = jnp.concatenate(ring, axis=0), jnp.concatenate(side, axis=0)
    strengths = (first[7:8], second[1:2], second[2:3])
    found_ring = product(jnp.concatenate([ring * strength for strength in strengths], axis=0), along_y)
    found_side = product(jnp.concatenate([side * strength for strength in strengths], axis=0), side_y)
    for number in range(3 * planes):
        at = number * tall
        part_ring = found_ring[number * RING : (number + 1) * RING]
        part_side = found_side[number * width_x : (number + 1) * width_x]
        if add:
            part_ring = part_ring + force_ref[at + width_x : at + tall, :]
            part_side = part_side + force_ref[at : at + width_x, width_y:]
        force_ref[at + width_x : at + tall, :] = part_ring
        force_ref[at : at + width_x, width_y:] = part_side


def spread_kernel(cap, steps, planes, width_x, width_y, recv_ref, *refs):
    forces, owns, turns_ref = refs[:steps], refs[steps : 2 * steps], refs[2 * steps]
    half = cap // 2
    most = jnp.zeros((1, recv_ref.shape[0] * half), F32)
    for step in range(steps):
        start = 2 * step * cap
        first = gather(recv_ref, start, cap)
        owns[step][...] = first
        second = gather(recv_ref, start + cap, cap)
        spread_own(first, second, planes, width_x, width_y, forces[step])
        first = gather(recv_ref, start + cap, half)
        second = gather(recv_ref, start + cap + half, half)
        spread_ghosts(first, second, planes, width_x, width_y, forces[step], False)
        most = jnp.maximum(most, second[3:4])
    turns_ref[0] = (jnp.max(most).astype(jnp.int32) + half - 1) // half


def more_kernel(cap, steps, planes, width_x, width_y, recv_ref, *refs):
    half = cap // 2
    for step in range(steps):
        start = (2 * step + 1) * cap
        force_ref = refs[steps + step]
        force_ref[...] = refs[step][...]
        first, second = gather(recv_ref, start, half), gather(recv_ref, start + half, half)
        spread_ghosts(first, second, planes, width_x, width_y, force_ref, True)


def sample(first, planes, width_x, width_y, probe_ref):
    table = jnp.concatenate(plane_table(first, planes, width_x), axis=0)
    along_y = y_table(first[1:2], first[4:5], width_y)
    size = planes * width_x
    high, low = split2(probe_ref[...])
    high_y, low_y = along_y
    found = nn(jnp.concatenate([high, low, high], axis=1), jnp.concatenate([high_y, high_y, low_y], axis=0))
    rows = [jnp.sum(found[n * size : (n + 1) * size] * table, axis=0, keepdims=True) for n in range(3)]
    return rows


def moments(f):
    density = f[0]
    diff = {}
    for member in range(1, 19, 2):
        density = density + (f[member] + f[member + 1])
        diff[member] = f[member] - f[member + 1]
    momenta = []
    for number in range(3):
        total = None
        for member in range(1, 19, 2):
            sign = LATTICE[member][number]
            if sign == 0:
                continue
            if total is None:
                total = diff[member] if sign == 1 else -diff[member]
            else:
                total = total + diff[member] if sign == 1 else total - diff[member]
        momenta.append(total)
    return density, momenta


def dot_c(vector, comps):
    total = None
    for number in range(3):
        if vector[number] == 0:
            continue
        if total is None:
            total = comps[number] if vector[number] == 1 else -comps[number]
        else:
            total = total + comps[number] if vector[number] == 1 else total - comps[number]
    return total


def collide(f, density, momenta, force):
    inverse = 1.0 / density
    speed = [(momenta[n] + 0.5 * force[n]) * inverse for n in range(3)]
    scaled = OMEGA * density
    speed_sq = speed[0] * speed[0] + speed[1] * speed[1] + speed[2] * speed[2]
    along = speed[0] * force[0] + speed[1] * force[1] + speed[2] * force[2]
    base = scaled * (1.0 - 1.5 * speed_sq) - (3.0 * SOURCE) * along
    flow = [scaled * speed[n] for n in range(3)]
    pull = [(3.0 * SOURCE) * force[n] for n in range(3)]
    linear = [3.0 * flow[n] + pull[n] for n in range(3)]
    square = [4.5 * flow[n] + 3.0 * pull[n] for n in range(3)]
    posts = [(1.0 - OMEGA) * f[0] + WEIGHTS[0] * base]
    for member in range(1, 19, 2):
        vector = LATTICE[member]
        even = WEIGHTS[member] * (base + dot_c(vector, speed) * dot_c(vector, square))
        odd = WEIGHTS[member] * dot_c(vector, linear)
        posts.append((1.0 - OMEGA) * f[member] + (even + odd))
        posts.append((1.0 - OMEGA) * f[member + 1] + (even - odd))
    return posts


def columns(source, out, at):
    planes, width_x = source.shape[1], source.shape[2]
    lane = iota((width_x, LANES), 1)
    lines = out.shape[1] // LANES
    totals = [jnp.zeros((width_x, LANES), F32) for _ in range(lines)]
    for plane in range(19 * planes):
        line, target = divmod(2 * plane, LANES)
        block = source[plane // planes, plane % planes]
        shift = (target - at) % LANES
        if shift:
            block = pltpu.roll(block, shift, 1)
        totals[line] = jnp.where((lane == target) | (lane == target + 1), block, totals[line])
    for line in range(lines):
        out[:, line * LANES : (line + 1) * LANES] = totals[line]


def corner_kernel(up, down, x_low, x_high, after_0, after_1, out_up, out_down):
    width_x, width_y = up.shape[0], x_low.shape[1]
    count = x_low.shape[0]
    pad = jnp.zeros((LANES - count, LANES), F32)
    for source, out, start, at in ((up, out_up, width_y - LANES, LANES - 2), (down, out_down, 0, 0)):
        out[0:width_x, :] = source[...]
        out[width_x:, :] = jnp.zeros((out.shape[0] - width_x, out.shape[1]), F32)
        for number, halo in enumerate((x_low, x_high)):
            turned = jnp.transpose(jnp.concatenate([halo[:, start : start + LANES], pad], axis=0))
            row = width_x + 2 * number
            out[row : row + 2, 0:LANES] = turned[at : at + 2]


def ring_rows(x_low, x_high, f_ref, ring_ref):
    planes, tall = f_ref.shape[1], f_ref.shape[2]
    for halo, members, row, inner in ((x_low, X_UP, RING - 1, RING - 2), (x_high, X_DOWN, 0, 1)):
        _, second, third = face_rows(members, planes)
        for z in range(planes):
            for member in range(19):
                places = [(row, member * planes + z)]
                if member in second:
                    places.append((inner, second[member] + z))
                for line, at in places:
                    line += tall - RING
                    f_ref[member, z, line : line + 1, :] = halo[at : at + 1, :]
            for number in range(4):
                at = third + number * planes + z
                ring_ref[number, z, inner : inner + 1, :] = halo[at : at + 1, :]


def side_cells(y_low, y_high, f_ref, ring_ref):
    planes, tall = f_ref.shape[1], f_ref.shape[2]
    width_x = tall - RING
    lane = iota((width_x, LANES), 1)
    wide_lane = iota((LANES, LANES), 1)
    pad = jnp.zeros((LANES - 8, LANES), F32)
    low = jnp.transpose(jnp.concatenate([y_low[width_x:, 0:LANES], pad], axis=0))
    high = jnp.transpose(jnp.concatenate([y_high[width_x:, 0:LANES], pad], axis=0))
    near = wide_lane >= LANES - 2
    ring_rows(
        jnp.where(near, pltpu.roll(low, LANES - 2, 1), high),
        jnp.where(near, pltpu.roll(low, LANES - 4, 1), pltpu.roll(high, LANES - 2, 1)),
        f_ref,
        ring_ref,
    )
    for plane in range(19 * planes):
        line, here = divmod(2 * plane, LANES)
        below = y_low[0:width_x, line * LANES : (line + 1) * LANES]
        above = y_high[0:width_x, line * LANES : (line + 1) * LANES]
        if (LANES - 2 - here) % LANES:
            below = pltpu.roll(below, (LANES - 2 - here) % LANES, 1)
        if here:
            above = pltpu.roll(above, LANES - here, 1)
        f_ref[plane // planes, plane % planes, 0:width_x, :] = jnp.where(lane >= LANES - 2, below, above)


def shifted(block, member):
    along_x, along_y, _ = LATTICE[member]
    if along_x:
        block = pltpu.roll(block, along_x % block.shape[0], 0)
    if along_y:
        block = pltpu.roll(block, along_y % block.shape[1], 1)
    return block


X_UP = [i for i in range(19) if LATTICE[i][0] == 1]
X_DOWN = [i for i in range(19) if LATTICE[i][0] == -1]
RUNS = [(0, 1, 0, 0), (1, 2, 1, 0), (3, 2, 0, 1), (5, 2, 0, 0), (7, 4, 1, 1), (11, 4, 1, 0), (15, 4, 0, 1)]
MOVED = [i for i in range(19) if LATTICE[i][0] or LATTICE[i][1]]


def force_at(ref, planes, tall, z, row, lanes):
    return [ref[pl.ds(pl.multiple_of((n * planes + z) * tall + row, 8), 8), lanes] for n in range(3)]


def for_rows(planes, width_x, body):
    @pl.loop(0, planes * (width_x // 8))
    def _(index):
        row = pl.multiple_of((index % (width_x // 8)) * 8, 8)
        body(index // (width_x // 8), row, pl.multiple_of(index * 8, 8))


def collide_block(f_ref, ring_ref, force_ref, z, row, lanes, force_lanes):
    planes, tall = f_ref.shape[1], f_ref.shape[2]
    at = pl.ds(row, 8)
    f = [f_ref[member, z, at, lanes] for member in range(19)]
    density, momenta = moments(f)
    if ring_ref is not None:
        outer = (iota((8, LANES), 0) == 1) | (iota((8, LANES), 0) == RING - 2)
        density = jnp.where(outer, ring_ref[0, z, :, lanes], density)
        momenta = [jnp.where(outer, ring_ref[n + 1, z, :, lanes], momenta[n]) for n in range(3)]
    force = force_at(force_ref, planes, tall, z, row, force_lanes)
    for member, value in enumerate(collide(f, density, momenta, force)):
        f_ref[member, z, at, lanes] = value


def first_kernel(f_in, x_low, x_high, force_ref, f_ref, ring_ref, sems):
    planes, width_x, width_y = f_in.shape[1], f_in.shape[2], f_in.shape[3]
    copies = fetch([(f_in.at[:, z], f_ref.at[:, z, pl.ds(0, width_x), :]) for z in range(planes)], sems)
    ring_rows(x_low, x_high, f_ref, ring_ref)

    @pl.loop(0, planes)
    def _(z):
        for start in range(0, width_y, LANES):
            lanes = pl.ds(start, LANES)
            collide_block(f_ref, ring_ref, force_ref, z, width_x, lanes, lanes)

    for z in range(planes):
        copies[z].wait()

        @pl.loop(0, width_x // 8)
        def _(index):
            row = pl.multiple_of(index * 8, 8)
            for start in range(0, width_y, LANES):
                lanes = pl.ds(start, LANES)
                collide_block(f_ref, None, force_ref, z, row, lanes, lanes)


def main_kernel(
    cap, steps, before, y_low, y_high, force_0, force_1, own_0, own_1, after_hbm, back_ref,
    side, after, ring_ref, probe_0, probe_1, rows, sems,
):
    planes, tall, width_y = before.shape[1], before.shape[2], before.shape[3]
    width_x, wide = tall - RING, after.shape[3]
    side_cells(y_low, y_high, side, ring_ref)
    far, all_lanes = pl.ds(width_y, LANES), pl.ds(0, LANES)

    def side_body(z, row, flat):
        collide_block(side, None, force_0, z, row, all_lanes, far)

    for_rows(planes, width_x, side_body)

    @pl.loop(0, planes)
    def _(z):
        collide_block(side, ring_ref, force_0, z, width_x, all_lanes, far)

    for member in MOVED:
        for z in range(planes):
            block = jnp.concatenate([before[member, z], side[member, z]], axis=1)
            after[member, (z + LATTICE[member][2]) % planes] = shifted(block, member)

    def second_block(z, row, start, flat=None, kept=range(19)):
        at, lanes = pl.ds(row, 8), pl.ds(start, LANES)
        f = []
        for member in range(19):
            if member in MOVED:
                f.append(after[member, z, at, lanes])
                continue
            other = (z - LATTICE[member][2]) % planes
            f.append(before[member, other, at, lanes] if start < width_y else side[member, other, at, all_lanes])
        density, momenta = moments(f)
        if flat is not None:
            inverse = 1.0 / density
            for number, force in enumerate(force_at(force_0, planes, tall, z, row, lanes)):
                probe_0[pl.ds(pl.multiple_of(number * planes * width_x + flat, 8), 8), lanes] = (
                    momenta[number] + 0.5 * force
                ) * inverse
        values = collide(f, density, momenta, force_at(force_1, planes, tall, z, row, lanes))
        for member in kept:
            after[member, z, at, lanes] = values[member]

    copies = []
    for z in range(planes):

        @pl.loop(0, width_x // 8)
        def _(index):
            row = pl.multiple_of(index * 8, 8)
            for start in range(0, width_y, LANES):
                second_block(z, row, start, pl.multiple_of(z * width_x + row, 8))
            second_block(z, row, width_y, kept=[i for i in range(19) if LATTICE[i][1]])

        for start in range(0, wide, LANES):
            second_block(z, width_x, start, kept=[i for i in range(19) if LATTICE[i][0]])
        for number, (first, count, along_x, along_y) in enumerate(RUNS):
            part = (pl.ds(first, count), z, pl.ds(0, tall if along_x else width_x), pl.ds(0, wide if along_y else width_y))
            copies.append(pltpu.make_async_copy(after.at[part], after_hbm.at[part], sems.at[len(RUNS) * z + number]))
            copies[-1].start()

    def sample_step(step, own_ref, probe_ref):
        for number, row in enumerate(sample(own_ref[...], planes, width_x, width_y, probe_ref)):
            rows[steps * number + step : steps * number + step + 1, :] = row

    sample_step(0, own_0, probe_0)
    for z in range(planes):

        def streamed(along_x, along_y, weight):
            total = None
            rows_used = tall if along_x else width_x
            lanes_used = wide if along_y else width_y
            for member in range(19):
                if LATTICE[member][:2] != (along_x, along_y) or weight(LATTICE[member][2]) == 0:
                    continue
                value = after[member, (z - LATTICE[member][2]) % planes, 0:rows_used, 0:lanes_used]
                value = value if weight(LATTICE[member][2]) > 0 else -value
                total = value if total is None else total + value
            if along_x:
                total = pltpu.roll(total, along_x % rows_used, 0)
            if along_y:
                total = pltpu.roll(total, along_y % lanes_used, 1)
            return total[0:width_x, 0:width_y]

        here = {(x, y): streamed(x, y, lambda cz: 1) for x in (-1, 0, 1) for y in (-1, 0, 1)}
        density = sum(here.values())
        momenta = [
            sum(here[1, y] - here[-1, y] for y in (-1, 0, 1)),
            sum(here[x, 1] - here[x, -1] for x in (-1, 0, 1)),
            sum(streamed(x, y, lambda cz: cz) for x, y in ((0, 0), (1, 0), (-1, 0), (0, 1), (0, -1))),
        ]
        inverse = 1.0 / density
        for number in range(3):
            at, to = (number * planes + z) * tall, (number * planes + z) * width_x
            probe_1[to : to + width_x, :] = (
                momenta[number] + 0.5 * force_1[at : at + width_x, 0:width_y]
            ) * inverse

    sample_step(1, own_1, probe_1)
    send_back(cap, rows, back_ref)
    for copy in copies:
        copy.wait()


def store_kernel(after_hbm, out_hbm, after, out_ref, sems, out_sems):
    planes, width_x, width_y = out_ref.shape[1], out_ref.shape[2], out_ref.shape[3]
    tall, wide = after.shape[2], after.shape[3]
    parts = [
        (pl.ds(first, count), slice(None), pl.ds(0, tall if along_x else width_x), pl.ds(0, wide if along_y else width_y))
        for first, count, along_x, along_y in RUNS
    ]
    arriving = fetch([(after_hbm.at[part], after.at[part]) for part in parts], sems)
    copies = []
    for copy, (first, count, along_x, along_y) in zip(arriving, RUNS):
        copy.wait()
        for member in range(first, first + count):
            for z in range(planes):
                block = after[member, z, 0 : tall if along_x else width_x, 0 : wide if along_y else width_y]
                out_ref[member, (z + LATTICE[member][2]) % planes] = shifted(block, member)[0:width_x, 0:width_y]
            copies.append(pltpu.make_async_copy(out_ref.at[member], out_hbm.at[member], out_sems.at[member]))
            copies[-1].start()
    for copy in copies:
        copy.wait()


def send_back(cap, rows, out_ref):
    devices, steps = out_ref.shape[0], out_ref.shape[1]
    per = LANES // cap
    group = iota((steps, LANES), 1) // cap
    for device in range(devices):
        line, place = device // per, device % per
        total = jnp.zeros((steps, LANES), F32)
        for number in range(3):
            piece = rows[number * steps : (number + 1) * steps, line * LANES : (line + 1) * LANES]
            shift = (number - place) * cap % LANES
            if shift:
                piece = pltpu.roll(piece, shift, 1)
            total = jnp.where(group == number, piece, total)
        out_ref[device] = total


def call(kernel, outs, scratch=(), flops=0, moved=0, limit=24, fetched=(False,), stored=None):
    shapes = [jax.ShapeDtypeStruct(shape, kind) for shape, kind in outs]
    out_specs = [pl.BlockSpec(memory_space=pltpu.SMEM if len(shape) == 1 else pltpu.VMEM) for shape, _ in outs]
    if stored:
        shapes = [pltpu.HBM(*out) if own else shape for out, shape, own in zip(outs, shapes, stored)]
        out_specs = [pl.BlockSpec(memory_space=pltpu.HBM if own else pltpu.VMEM) for own in stored]
    places = {True: pltpu.HBM, False: pltpu.VMEM, None: pltpu.SMEM}
    specs = [pl.BlockSpec(memory_space=places[own]) for own in fetched]
    made = pl.pallas_call(
        kernel,
        out_shape=shapes,
        out_specs=out_specs,
        scratch_shapes=list(scratch),
        **({"in_specs": specs} if fetched != (False,) else {}),
        cost_estimate=pl.CostEstimate(flops=flops, bytes_accessed=moved, transcendentals=0),
        compiler_params=pltpu.CompilerParams(vmem_limit_bytes=limit * 1024 * 1024),
    )
    if not any(fetched):
        return made
    return lambda *args: made(
        *[pltpu.with_memory_space_constraint(x, pltpu.HBM) if own else x for x, own in zip(args, fetched)]
    )


def pair(up, down, axis):
    count = lax.axis_size(axis)
    forward = [(i, (i + 1) % count) for i in range(count)]
    backward = [(target, source) for source, target in forward]
    return lax.ppermute(up, axis, forward), lax.ppermute(down, axis, backward)


def run(rounds, populations_in, marker_force, marker_frac, marker_cell, marker_tile):
    count_gx, count_gy = lax.axis_size("gx"), lax.axis_size("gy")
    devices = count_gx * count_gy
    steps, owned = marker_force.shape[0], marker_force.shape[2]
    cap = max(2, 2 * owned // devices)
    half, slots = cap // 2, devices * cap
    planes, width_x, width_y = populations_in.shape[1:]
    tall, wide = width_x + RING, width_y + SIDE
    grid = (count_gx, count_gy, width_x, width_y)
    by_comp = lambda x: jnp.transpose(x, (1, 0, 2))
    markers = (
        marker_tile.reshape(steps * owned // LANES, LANES),
        by_comp(marker_cell),
        by_comp(marker_frac),
        by_comp(marker_force),
    )
    message = ((devices, 8, LANES), F32)
    rows = pltpu.VMEM((16, owned), F32)

    def send(outgoing):
        return lax.all_to_all(outgoing, ("gx", "gy"), split_axis=0, concat_axis=0, tiled=True)

    def pack_markers(*refs):
        pack_kernel(grid, steps, cap, *refs)

    face = (((19 + len(X_UP) + 4) * planes, width_y), F32)
    packed = -(-2 * 19 * planes // LANES) * LANES
    outgoing, slot = call(
        pack_markers,
        [message, ((steps, owned), jnp.int32)],
        [
            rows,
            pltpu.VMEM((steps * owned // LANES, LANES), jnp.int32),
            pltpu.VMEM((3, steps, owned), jnp.int32),
            pltpu.VMEM((3, steps, owned), F32),
            pltpu.VMEM((3, steps, owned), F32),
            pltpu.SemaphoreType.DMA((4,)),
        ],
        fetched=(True,) * 4,
    )(*markers)
    x_up, x_down = call(
        strips_kernel,
        [face, face],
        [
            pltpu.VMEM((19, planes, 8, width_y), F32),
            pltpu.VMEM((19, planes, 8, width_y), F32),
            pltpu.SemaphoreType.DMA((2,)),
        ],
        fetched=(True, False),
    )(populations_in, slot)
    y_up, y_down = call(
        columns_kernel,
        [((width_x, packed), F32)] * 2,
        [
            pltpu.VMEM((19, planes, width_x, LANES), F32),
            pltpu.VMEM((19, planes, width_x, LANES), F32),
            pltpu.SemaphoreType.DMA((2,)),
        ],
        fetched=(True, False),
    )(populations_in, x_up)
    arrived = send(outgoing)

    x_low, x_high = pair(x_up, x_down, "gx")
    field = ((3 * planes * tall, wide), F32)

    def spread_markers(*refs):
        spread_kernel(cap, steps, planes, width_x, width_y, *refs)

    force_0, force_1, own_0, own_1, turns = call(
        spread_markers, [field] * steps + [((8, slots), F32)] * steps + [((1,), jnp.int32)]
    )(arrived)
    turns = turns.reshape(())

    y_up, y_down = call(corner_kernel, [((width_x + 8, packed), F32)] * 2)(y_up, y_down, x_low, x_high, own_0, own_1)
    y_low, y_high = pair(y_up, y_down, "gy")

    def again(state):
        return state[0] < turns

    def more(state):
        turn, *forces = state

        def turn_markers(*refs):
            turn_kernel(grid, steps, cap, *refs)

        def add_markers(*refs):
            more_kernel(cap, steps, planes, width_x, width_y, *refs)

        spec = [pl.BlockSpec(memory_space=pltpu.SMEM)] + [pl.BlockSpec(memory_space=pltpu.VMEM)] * 4
        (outgoing,) = pl.pallas_call(
            turn_markers,
            out_shape=[jax.ShapeDtypeStruct(*message)],
            in_specs=spec,
            scratch_shapes=[rows],
            compiler_params=pltpu.CompilerParams(vmem_limit_bytes=24 * 1024 * 1024),
        )(turn.reshape(1), *markers)
        return (turn + 1, *call(add_markers, [field] * steps)(send(outgoing), *forces))

    if rounds:
        _, force_0, force_1 = lax.while_loop(again, more, (jnp.int32(1), force_0, force_1))

    (before,) = call(
        first_kernel,
        [((19, planes, tall, width_y), F32)],
        [pltpu.VMEM((4, planes, RING, width_y), F32), pltpu.SemaphoreType.DMA((planes,))],
        fetched=(True,) + (False,) * 3,
    )(populations_in, x_low, x_high, force_0)

    def main(*refs):
        main_kernel(cap, steps, *refs)

    own_field = pltpu.VMEM((3 * planes * width_x, width_y), F32)
    after, back = call(
        main,
        [((19, planes, tall, wide), F32), ((devices, steps, LANES), F32)],
        [
            pltpu.VMEM((19, planes, tall, LANES), F32),
            pltpu.VMEM((19, planes, tall, wide), F32),
            pltpu.VMEM((4, planes, RING, LANES), F32),
            own_field,
            own_field,
            pltpu.VMEM((8, slots), F32),
            pltpu.SemaphoreType.DMA((len(RUNS) * planes,)),
        ],
        stored=(True, False),
    )(before, y_low, y_high, force_0, force_1, own_0, own_1)
    (fields,) = call(
        store_kernel,
        [(populations_in.shape, F32)],
        [
            pltpu.VMEM((19, planes, tall, wide), F32),
            pltpu.VMEM(populations_in.shape, F32),
            pltpu.SemaphoreType.DMA((len(RUNS),)),
            pltpu.SemaphoreType.DMA((19,)),
        ],
        fetched=(True,),
        stored=(True,),
    )(after)
    returned = send(back)

    def unpack(*refs):
        unpack_kernel(cap, steps, *refs)

    (velocity,) = call(unpack, [((3, steps, owned), F32)])(returned, slot)
    return fields, by_comp(velocity), turns


def local(*inputs):
    def again(state):
        return state[2] > 1

    def whole(state):
        fields, velocity, _ = run(True, *inputs)
        return fields, velocity, jnp.int32(0)

    fields, velocity, _ = lax.while_loop(again, whole, run(False, *inputs))
    return fields, velocity


def solution(mesh):
    return jax.shard_map(
        local,
        mesh=mesh,
        in_specs=(
            P(None, None, "gx", "gy"),
            P(None, None, ("gx", "gy")),
            P(None, None, ("gx", "gy")),
            P(None, None, ("gx", "gy")),
            P(None, ("gx", "gy"), None),
        ),
        out_specs=(P(None, None, "gx", "gy"), P(None, None, ("gx", "gy"))),
        check_vma=False,
    )
```

```python
import jax
import jax.numpy as jnp
from jax import lax
from jax.experimental import pallas as pl
from jax.experimental.pallas import tpu as pltpu
from jax.sharding import PartitionSpec as P

LATTICE = [
    (0, 0, 0),
    (1, 0, 0),
    (-1, 0, 0),
    (0, 1, 0),
    (0, -1, 0),
    (0, 0, 1),
    (0, 0, -1),
    (1, 1, 0),
    (-1, -1, 0),
    (1, -1, 0),
    (-1, 1, 0),
    (1, 0, 1),
    (-1, 0, -1),
    (1, 0, -1),
    (-1, 0, 1),
    (0, 1, 1),
    (0, -1, -1),
    (0, 1, -1),
    (0, -1, 1),
]
WEIGHTS = [1.0 / 3.0] + [1.0 / 18.0] * 6 + [1.0 / 36.0] * 12
relax_time = 0.8
OMEGA = 1.0 / relax_time
SOURCE = 1.0 - 0.5 / relax_time
LANES = 128

BF = jnp.bfloat16
F32 = jnp.float32


def split2(x):
    high = x.astype(BF)
    low = (x - high.astype(F32)).astype(BF)
    return high, low


def nt(a, b):
    return lax.dot_general(a, b, (((1,), (1,)), ((), ())), preferred_element_type=F32)


def nn(a, b):
    return lax.dot_general(a, b, (((1,), (0,)), ((), ())), preferred_element_type=F32)


def iota(shape, dim):
    return lax.broadcasted_iota(jnp.int32, shape, dim)


RING = 8
SIDE = LANES


def gather_lanes(rows, index):
    index = jnp.broadcast_to(index, (8, LANES))
    line, lane = index // LANES, index % LANES
    found = jnp.zeros((8, LANES), F32)
    for number in range(rows.shape[1] // LANES):
        piece = rows[:, number * LANES : (number + 1) * LANES]
        piece = jnp.take_along_axis(piece, lane, axis=1, mode="promise_in_bounds")
        found = jnp.where(line == number, piece, found)
    return found


def fetch(pairs, sems):
    copies = [pltpu.make_async_copy(source, target, sems.at[n]) for n, (source, target) in enumerate(pairs)]
    for copy in copies:
        copy.start()
    return copies


def ghosts(step, steps, count_gx, count_gy, width_x, width_y, tiles, cell_x, cell_y):
    reach = steps - step
    tiles = tiles.astype(F32)
    gx = jnp.floor((tiles + 0.5) * (1.0 / count_gy))
    along = []
    for cell, width, place, count in (
        (cell_x, width_x, gx, count_gx),
        (cell_y, width_y, tiles - gx * count_gy, count_gy),
    ):
        above, below = cell >= width - 1 - reach, cell <= reach - 1
        place_up = jnp.where(place == count - 1, 0.0, place + 1.0)
        place_down = jnp.where(place == 0, count - 1.0, place - 1.0)
        along.append((jnp.where(above | below, 1.0, 0.0), place, jnp.where(above, place_up, place_down)))
    (near_x, here_x, there_x), (near_y, here_y, there_y) = along
    return [
        jnp.where(near_x > 0, there_x * count_gy + here_y, -1.0),
        jnp.where(near_y > 0, here_x * count_gy + there_y, -1.0),
        jnp.where(near_x * near_y > 0, there_x * count_gy + there_y, -1.0),
    ]


def filled(rows, members, ranks, devices, width):
    owned = rows.shape[1]
    number = iota((1, owned), 1) + 1
    digits = [(number % 256).astype(F32), (number // 256).astype(F32)]
    left = jnp.concatenate([jnp.concatenate([m * digit for m in members], axis=1) for digit in digits], axis=0)
    place = (iota((LANES, owned), 0) % width).astype(F32)
    right = jnp.concatenate([jnp.where(place == rank, 1.0, 0.0) for rank in ranks], axis=1)
    found = nt(left.astype(BF), right.astype(BF))
    marker = (found[0:devices] + 256.0 * found[devices:]).astype(jnp.int32) - 1
    per = LANES // width
    group = iota((1, LANES), 1) // width
    halves = ([], [])
    for line in range(devices // per):
        index = marker[line * per : line * per + 1]
        for other in range(1, per):
            index = jnp.where(group == other, marker[line * per + other : line * per + other + 1], index)
        for half, source in zip(halves, (rows[0:8, :], rows[8:16, :])):
            half.append(gather_lanes(source, index))
    return [jnp.concatenate(half, axis=1) for half in halves]


def pack(grid, steps, cap, step_rows, out_ref, slot_ref, rows, turn=None):
    count_gx, count_gy, width_x, width_y = grid
    devices, half = count_gx * count_gy, cap // 2
    owned = rows.shape[1]
    spare = devices * half
    earlier = jnp.where(iota((owned, owned), 0) < iota((owned, owned), 1), 1.0, 0.0).astype(BF)
    column = iota((devices, owned), 0).astype(F32)
    octets, extras, most = [], [], []
    given = [step_rows(step) for step in range(steps)]
    asked = []
    for step, (tiles, values) in enumerate(given):
        asked.append([tiles.astype(F32)] + ghosts(step, steps, *grid, tiles, values[0], values[1]))
    member = [[jnp.where(column == tile, 1.0, 0.0) for tile in tiles] for tiles in asked]
    before = nn(jnp.concatenate(sum(member, []), axis=0).astype(BF), earlier)
    before = [before[n * devices : (n + 1) * devices] for n in range(4 * steps)]
    for step, (tiles, values) in enumerate(given):
        if turn is None:
            rank = jnp.sum(before[4 * step] * member[step][0], axis=0, keepdims=True)
            slot = tiles * cap + rank.astype(jnp.int32)
            slot_ref[step : step + 1, :] = slot
            rows[...] = jnp.zeros_like(rows)
            for number, value in enumerate(values):
                rows[number : number + 1, :] = value
            octets.append(filled(rows, [member[step][0]], [rank], devices, cap))
        taken = [jnp.zeros((devices, 1), F32)]
        ranks = []
        for number in range(1, 4):
            here = member[step][number]
            rank = jnp.sum((before[4 * step + number] + taken[-1]) * here, axis=0, keepdims=True)
            taken.append(taken[-1] + jnp.sum(here, axis=1, keepdims=True))
            ranks.append(rank if turn is None else rank - turn * half)
        rows[...] = jnp.zeros_like(rows)
        for place, value in zip((1, 2, 3, 4, 5, 6, 7, 9, 10), values):
            rows[place : place + 1, :] = value
        extra, more_extra = filled(rows, member[step][1:], ranks, devices, half)
        lanes, sender = iota((devices, spare), 1), iota((devices, spare), 0)
        ends = [
            jnp.sum(jnp.where(lanes // half == sender, end, 0.0), axis=0, keepdims=True) for end in (taken[1], taken[2])
        ]
        rank = (iota((1, spare), 1) % half).astype(F32)
        if turn is not None:
            rank = rank + turn * half
        in_x = (rank < ends[0]) | (rank >= ends[1])
        in_y = rank >= ends[0]
        first = []
        for cell, width, moved in ((extra[1:2], width_x, in_x), (extra[2:3], width_y, in_y)):
            first.append(cell + jnp.where(moved, jnp.where(cell * 2 < width, width * 1.0, -1.0 * width), 0.0))
        extras.append((jnp.concatenate([extra[0:1]] + first + [extra[3:8]], axis=0), more_extra))
        most.append(jnp.max(taken[3], axis=0, keepdims=True))
    lane, row = iota((8, LANES), 1), iota((8, LANES), 0)

    def placed(octet, device, width, offset):
        line, place = device * width // LANES, device * width % LANES
        piece = octet[:, line * LANES : (line + 1) * LANES]
        shift = (offset - place) % LANES
        if shift:
            piece = pltpu.roll(piece, shift, 1)
        return jnp.where((lane >= offset) & (lane < offset + width), piece, 0.0)

    heading = jnp.zeros((8, LANES), F32)
    for step in range(steps):
        start = (2 * step + 1) * cap + half
        heading = jnp.where((row == 3) & (lane >= start) & (lane < start + half), most[step], heading)
    for device in range(devices):
        block = heading
        for step in range(steps):
            start = 2 * step * cap
            if turn is None:
                block = block + placed(octets[step][0], device, cap, start)
                block = block + placed(octets[step][1], device, cap, start + cap)
            block = block + placed(extras[step][0], device, half, start + cap)
            block = block + placed(extras[step][1], device, half, start + cap + half)
        out_ref[device] = block


def marker_rows(tile_ref, cell_ref, frac_ref, force_ref):
    lines = cell_ref.shape[2] // LANES

    def step_rows(step):
        tiles = jnp.concatenate(
            [tile_ref[step * lines + r : step * lines + r + 1, :] for r in range(lines)], axis=1
        )
        values = [cell_ref[n, step : step + 1, :].astype(F32) for n in range(3)]
        values += [frac_ref[n, step : step + 1, :] for n in range(3)]
        values += [force_ref[n, step : step + 1, :] for n in range(3)]
        return tiles, values

    return step_rows


def pack_kernel(
    grid, steps, cap, tile_in, cell_in, frac_in, force_in, out_ref, slot_ref,
    rows, tile_ref, cell_ref, frac_ref, force_ref, sems,
):
    copies = fetch([(tile_in, tile_ref), (cell_in, cell_ref), (frac_in, frac_ref), (force_in, force_ref)], sems)
    for copy in copies:
        copy.wait()
    pack(grid, steps, cap, marker_rows(tile_ref, cell_ref, frac_ref, force_ref), out_ref, slot_ref, rows)


def columns_kernel(f_in, after_ref, up, down, far_ref, near_ref, sems):
    width_y = f_in.shape[3]
    copies = fetch(
        [
            (f_in.at[:, :, :, pl.ds(width_y - LANES, LANES)], far_ref),
            (f_in.at[:, :, :, pl.ds(0, LANES)], near_ref),
        ],
        sems,
    )
    for copy, out, source, at in ((copies[0], up, far_ref, LANES - 2), (copies[1], down, near_ref, 0)):
        copy.wait()
        columns(source, out, at)


def face_rows(members, planes):
    first = 19 * planes
    second = {member: first + n * planes for n, member in enumerate(members)}
    return first, second, first + len(members) * planes


def strips_kernel(f_in, after_ref, x_up, x_down, near_ref, far_ref, sems):
    planes, width_x = f_in.shape[1], f_in.shape[2]
    copies = fetch(
        [
            (f_in.at[:, :, pl.ds(width_x - 8, 8), :], far_ref),
            (f_in.at[:, :, pl.ds(0, 8), :], near_ref),
        ],
        sems,
    )
    for copy, out, source, members, row, inner in (
        (copies[0], x_up, far_ref, X_UP, 7, 6),
        (copies[1], x_down, near_ref, X_DOWN, 0, 1),
    ):
        copy.wait()
        _, second, third = face_rows(members, planes)
        for z in range(planes):
            for member in range(19):
                at = member * planes + z
                out[at : at + 1, :] = source[member, z, row : row + 1, :]
            for member, at in second.items():
                out[at + z : at + z + 1, :] = source[member, z, inner : inner + 1, :]
            density, momenta = moments([source[member, z] for member in range(19)])
            for number, value in enumerate([density] + momenta):
                at = third + number * planes + z
                out[at : at + 1, :] = value[inner : inner + 1]


def turn_kernel(grid, steps, cap, turn_ref, tile_ref, cell_ref, frac_ref, force_ref, out_ref, rows):
    step_rows = marker_rows(tile_ref, cell_ref, frac_ref, force_ref)
    pack(grid, steps, cap, step_rows, out_ref, None, rows, turn_ref[0].astype(F32))


def gather(recv_ref, offset, width):
    devices = recv_ref.shape[0]
    per = LANES // width
    group = iota((8, LANES), 1) // width
    pieces = []
    for line in range(devices // per):
        total = jnp.zeros((8, LANES), F32)
        for place in range(per):
            piece = recv_ref[line * per + place]
            shift = (place * width - offset) % LANES
            if shift:
                piece = pltpu.roll(piece, shift, 1)
            total = jnp.where(group == place, piece, total)
        pieces.append(total)
    return jnp.concatenate(pieces, axis=1)


def unpack_kernel(cap, steps, recv_ref, slot_ref, out_ref):
    devices = recv_ref.shape[0]
    per = LANES // cap
    group = iota((steps, LANES), 1) // cap
    comps = []
    for number in range(3):
        pieces = []
        for line in range(devices // per):
            total = jnp.zeros((steps, LANES), F32)
            for place in range(per):
                piece = recv_ref[line * per + place]
                shift = (place - number) * cap % LANES
                if shift:
                    piece = pltpu.roll(piece, shift, 1)
                total = jnp.where(group == place, piece, total)
            pieces.append(total)
        comps.append(jnp.concatenate(pieces, axis=1))
    for step in range(steps):
        rows = jnp.concatenate([comp[step : step + 1] for comp in comps] + [jnp.zeros((5, devices * cap), F32)], axis=0)
        for start in range(0, slot_ref.shape[1], LANES):
            found = gather_lanes(rows, slot_ref[step : step + 1, start : start + LANES])
            for number in range(3):
                out_ref[number, step : step + 1, start : start + LANES] = found[number : number + 1]


def line_weights(cell, frac, extent):
    grid = iota((extent, cell.shape[1]), 0).astype(F32)
    return jnp.where(grid == cell, 1.0 - frac, jnp.where(grid == cell + 1.0, frac, 0.0))


def y_table(cell, frac, extent):
    grid = iota((extent, cell.shape[1]), 0).astype(F32)
    lower, upper = grid == cell, grid == cell + 1.0
    tables = []
    for low, high in zip(split2(1.0 - frac), split2(frac)):
        low, high = low.astype(F32), high.astype(F32)
        tables.append(jnp.where(lower, low, jnp.where(upper, high, 0.0)).astype(BF))
    return tables


def plane_table(rows, planes, width_x):
    kernel_x = line_weights(rows[0:1], rows[3:4], width_x)
    kernel_z = line_weights(rows[2:3], rows[5:6], 8)
    return [kernel_z[z : z + 1] * kernel_x for z in range(planes)]


def product(table, along_y):
    high, low = split2(table)
    high_y, low_y = along_y
    return nt(
        jnp.concatenate([high, low, high], axis=1), jnp.concatenate([high_y, high_y, low_y], axis=1)
    )


def spread_own(first, second, planes, width_x, width_y, force_ref):
    tall = width_x + RING
    table = jnp.concatenate(plane_table(first, planes, width_x), axis=0)
    along_y = y_table(first[1:2], first[4:5], width_y)
    strengths = (first[6:7], first[7:8], second[0:1])
    found = product(jnp.concatenate([table * strength for strength in strengths], axis=0), along_y)
    for number in range(3 * planes):
        force_ref[number * tall : number * tall + width_x, 0:width_y] = found[number * width_x : (number + 1) * width_x]


def spread_ghosts(first, second, planes, width_x, width_y, force_ref, add):
    tall, wide = width_x + RING, width_y + SIDE
    cell_x = jnp.where(first[1:2] < 0, first[1:2] + tall, first[1:2])
    cell_y = jnp.where(first[2:3] < 0, first[2:3] + wide, first[2:3])
    kernel_x = line_weights(cell_x, first[4:5], tall)
    kernel_z = line_weights(first[3:4], first[6:7], 8)
    along_y = y_table(cell_y, first[5:6], wide)
    side_y = [table[width_y:] for table in along_y]
    ring = [kernel_z[z : z + 1] * kernel_x[width_x:] for z in range(planes)]
    side = [kernel_z[z : z + 1] * kernel_x[0:width_x] for z in range(planes)]
    ring, side = jnp.concatenate(ring, axis=0), jnp.concatenate(side, axis=0)
    strengths = (first[7:8], second[1:2], second[2:3])
    found_ring = product(jnp.concatenate([ring * strength for strength in strengths], axis=0), along_y)
    found_side = product(jnp.concatenate([side * strength for strength in strengths], axis=0), side_y)
    for number in range(3 * planes):
        at = number * tall
        part_ring = found_ring[number * RING : (number + 1) * RING]
        part_side = found_side[number * width_x : (number + 1) * width_x]
        if add:
            part_ring = part_ring + force_ref[at + width_x : at + tall, :]
            part_side = part_side + force_ref[at : at + width_x, width_y:]
        force_ref[at + width_x : at + tall, :] = part_ring
        force_ref[at : at + width_x, width_y:] = part_side


def spread_kernel(cap, steps, planes, width_x, width_y, recv_ref, *refs):
    forces, owns, turns_ref = refs[:steps], refs[steps : 2 * steps], refs[2 * steps]
    half = cap // 2
    most = jnp.zeros((1, recv_ref.shape[0] * half), F32)
    for step in range(steps):
        start = 2 * step * cap
        first = gather(recv_ref, start, cap)
        owns[step][...] = first
        second = gather(recv_ref, start + cap, cap)
        spread_own(first, second, planes, width_x, width_y, forces[step])
        first = gather(recv_ref, start + cap, half)
        second = gather(recv_ref, start + cap + half, half)
        spread_ghosts(first, second, planes, width_x, width_y, forces[step], False)
        most = jnp.maximum(most, second[3:4])
    turns_ref[0] = (jnp.max(most).astype(jnp.int32) + half - 1) // half


def more_kernel(cap, steps, planes, width_x, width_y, recv_ref, *refs):
    half = cap // 2
    for step in range(steps):
        start = (2 * step + 1) * cap
        force_ref = refs[steps + step]
        force_ref[...] = refs[step][...]
        first, second = gather(recv_ref, start, half), gather(recv_ref, start + half, half)
        spread_ghosts(first, second, planes, width_x, width_y, force_ref, True)


def sample(first, planes, width_x, width_y, probe_ref):
    table = jnp.concatenate(plane_table(first, planes, width_x), axis=0)
    along_y = y_table(first[1:2], first[4:5], width_y)
    size = planes * width_x
    high, low = split2(probe_ref[...])
    high_y, low_y = along_y
    found = nn(jnp.concatenate([high, low, high], axis=1), jnp.concatenate([high_y, high_y, low_y], axis=0))
    rows = [jnp.sum(found[n * size : (n + 1) * size] * table, axis=0, keepdims=True) for n in range(3)]
    return rows


def moments(f):
    density = f[0]
    diff = {}
    for member in range(1, 19, 2):
        density = density + (f[member] + f[member + 1])
        diff[member] = f[member] - f[member + 1]
    momenta = []
    for number in range(3):
        total = None
        for member in range(1, 19, 2):
            sign = LATTICE[member][number]
            if sign == 0:
                continue
            if total is None:
                total = diff[member] if sign == 1 else -diff[member]
            else:
                total = total + diff[member] if sign == 1 else total - diff[member]
        momenta.append(total)
    return density, momenta


def dot_c(vector, comps):
    total = None
    for number in range(3):
        if vector[number] == 0:
            continue
        if total is None:
            total = comps[number] if vector[number] == 1 else -comps[number]
        else:
            total = total + comps[number] if vector[number] == 1 else total - comps[number]
    return total


def collide(f, density, momenta, force):
    inverse = 1.0 / density
    speed = [(momenta[n] + 0.5 * force[n]) * inverse for n in range(3)]
    scaled = OMEGA * density
    speed_sq = speed[0] * speed[0] + speed[1] * speed[1] + speed[2] * speed[2]
    along = speed[0] * force[0] + speed[1] * force[1] + speed[2] * force[2]
    base = scaled * (1.0 - 1.5 * speed_sq) - (3.0 * SOURCE) * along
    flow = [scaled * speed[n] for n in range(3)]
    pull = [(3.0 * SOURCE) * force[n] for n in range(3)]
    linear = [3.0 * flow[n] + pull[n] for n in range(3)]
    square = [4.5 * flow[n] + 3.0 * pull[n] for n in range(3)]
    posts = [(1.0 - OMEGA) * f[0] + WEIGHTS[0] * base]
    for member in range(1, 19, 2):
        vector = LATTICE[member]
        even = WEIGHTS[member] * (base + dot_c(vector, speed) * dot_c(vector, square))
        odd = WEIGHTS[member] * dot_c(vector, linear)
        posts.append((1.0 - OMEGA) * f[member] + (even + odd))
        posts.append((1.0 - OMEGA) * f[member + 1] + (even - odd))
    return posts


def columns(source, out, at):
    planes, width_x = source.shape[1], source.shape[2]
    lane = iota((width_x, LANES), 1)
    lines = out.shape[1] // LANES
    totals = [jnp.zeros((width_x, LANES), F32) for _ in range(lines)]
    for plane in range(19 * planes):
        line, target = divmod(2 * plane, LANES)
        block = source[plane // planes, plane % planes]
        shift = (target - at) % LANES
        if shift:
            block = pltpu.roll(block, shift, 1)
        totals[line] = jnp.where((lane == target) | (lane == target + 1), block, totals[line])
    for line in range(lines):
        out[:, line * LANES : (line + 1) * LANES] = totals[line]


def corner_kernel(up, down, x_low, x_high, after_0, after_1, out_up, out_down):
    width_x, width_y = up.shape[0], x_low.shape[1]
    count = x_low.shape[0]
    pad = jnp.zeros((LANES - count, LANES), F32)
    for source, out, start, at in ((up, out_up, width_y - LANES, LANES - 2), (down, out_down, 0, 0)):
        out[0:width_x, :] = source[...]
        out[width_x:, :] = jnp.zeros((out.shape[0] - width_x, out.shape[1]), F32)
        for number, halo in enumerate((x_low, x_high)):
            turned = jnp.transpose(jnp.concatenate([halo[:, start : start + LANES], pad], axis=0))
            row = width_x + 2 * number
            out[row : row + 2, 0:LANES] = turned[at : at + 2]


def ring_rows(x_low, x_high, f_ref, ring_ref):
    planes, tall = f_ref.shape[1], f_ref.shape[2]
    for halo, members, row, inner in ((x_low, X_UP, RING - 1, RING - 2), (x_high, X_DOWN, 0, 1)):
        _, second, third = face_rows(members, planes)
        for z in range(planes):
            for member in range(19):
                places = [(row, member * planes + z)]
                if member in second:
                    places.append((inner, second[member] + z))
                for line, at in places:
                    line += tall - RING
                    f_ref[member, z, line : line + 1, :] = halo[at : at + 1, :]
            for number in range(4):
                at = third + number * planes + z
                ring_ref[number, z, inner : inner + 1, :] = halo[at : at + 1, :]


def side_cells(y_low, y_high, f_ref, ring_ref):
    planes, tall = f_ref.shape[1], f_ref.shape[2]
    width_x = tall - RING
    lane = iota((width_x, LANES), 1)
    wide_lane = iota((LANES, LANES), 1)
    pad = jnp.zeros((LANES - 8, LANES), F32)
    low = jnp.transpose(jnp.concatenate([y_low[width_x:, 0:LANES], pad], axis=0))
    high = jnp.transpose(jnp.concatenate([y_high[width_x:, 0:LANES], pad], axis=0))
    near = wide_lane >= LANES - 2
    ring_rows(
        jnp.where(near, pltpu.roll(low, LANES - 2, 1), high),
        jnp.where(near, pltpu.roll(low, LANES - 4, 1), pltpu.roll(high, LANES - 2, 1)),
        f_ref,
        ring_ref,
    )
    for plane in range(19 * planes):
        line, here = divmod(2 * plane, LANES)
        below = y_low[0:width_x, line * LANES : (line + 1) * LANES]
        above = y_high[0:width_x, line * LANES : (line + 1) * LANES]
        if (LANES - 2 - here) % LANES:
            below = pltpu.roll(below, (LANES - 2 - here) % LANES, 1)
        if here:
            above = pltpu.roll(above, LANES - here, 1)
        f_ref[plane // planes, plane % planes, 0:width_x, :] = jnp.where(lane >= LANES - 2, below, above)


def shifted(block, member):
    along_x, along_y, _ = LATTICE[member]
    if along_x:
        block = pltpu.roll(block, along_x % block.shape[0], 0)
    if along_y:
        block = pltpu.roll(block, along_y % block.shape[1], 1)
    return block


X_UP = [i for i in range(19) if LATTICE[i][0] == 1]
X_DOWN = [i for i in range(19) if LATTICE[i][0] == -1]
RUNS = [(0, 1, 0, 0), (1, 2, 1, 0), (3, 2, 0, 1), (5, 2, 0, 0), (7, 4, 1, 1), (11, 4, 1, 0), (15, 4, 0, 1)]
MOVED = [i for i in range(19) if LATTICE[i][0] or LATTICE[i][1]]


def force_at(ref, planes, tall, z, row, lanes):
    return [ref[pl.ds(pl.multiple_of((n * planes + z) * tall + row, 8), 8), lanes] for n in range(3)]


def for_rows(planes, width_x, body):
    @pl.loop(0, planes * (width_x // 8))
    def _(index):
        row = pl.multiple_of((index % (width_x // 8)) * 8, 8)
        body(index // (width_x // 8), row, pl.multiple_of(index * 8, 8))


def collide_block(f_ref, ring_ref, force_ref, z, row, lanes, force_lanes):
    planes, tall = f_ref.shape[1], f_ref.shape[2]
    at = pl.ds(row, 8)
    f = [f_ref[member, z, at, lanes] for member in range(19)]
    density, momenta = moments(f)
    if ring_ref is not None:
        outer = (iota((8, LANES), 0) == 1) | (iota((8, LANES), 0) == RING - 2)
        density = jnp.where(outer, ring_ref[0, z, :, lanes], density)
        momenta = [jnp.where(outer, ring_ref[n + 1, z, :, lanes], momenta[n]) for n in range(3)]
    force = force_at(force_ref, planes, tall, z, row, force_lanes)
    for member, value in enumerate(collide(f, density, momenta, force)):
        f_ref[member, z, at, lanes] = value


def first_kernel(f_in, x_low, x_high, force_ref, f_ref, ring_ref, sems):
    planes, width_x, width_y = f_in.shape[1], f_in.shape[2], f_in.shape[3]
    copies = fetch([(f_in.at[:, z], f_ref.at[:, z, pl.ds(0, width_x), :]) for z in range(planes)], sems)
    ring_rows(x_low, x_high, f_ref, ring_ref)

    @pl.loop(0, planes)
    def _(z):
        for start in range(0, width_y, LANES):
            lanes = pl.ds(start, LANES)
            collide_block(f_ref, ring_ref, force_ref, z, width_x, lanes, lanes)

    for z in range(planes):
        copies[z].wait()

        @pl.loop(0, width_x // 8)
        def _(index):
            row = pl.multiple_of(index * 8, 8)
            for start in range(0, width_y, LANES):
                lanes = pl.ds(start, LANES)
                collide_block(f_ref, None, force_ref, z, row, lanes, lanes)


def main_kernel(
    cap, steps, before, y_low, y_high, force_0, force_1, own_0, own_1, after_hbm, back_ref,
    side, after, ring_ref, probe_0, probe_1, rows, sems,
):
    planes, tall, width_y = before.shape[1], before.shape[2], before.shape[3]
    width_x, wide = tall - RING, after.shape[3]
    side_cells(y_low, y_high, side, ring_ref)
    far, all_lanes = pl.ds(width_y, LANES), pl.ds(0, LANES)

    @pl.loop(0, planes)
    def _(z):
        for row in range(0, width_x, 8):
            collide_block(side, None, force_0, z, row, all_lanes, far)
        collide_block(side, ring_ref, force_0, z, width_x, all_lanes, far)

    for member in MOVED:
        for z in range(planes):
            block = jnp.concatenate([before[member, z], side[member, z]], axis=1)
            after[member, (z + LATTICE[member][2]) % planes] = shifted(block, member)

    def second_block(z, row, start, flat=None, kept=range(19)):
        at, lanes = pl.ds(row, 8), pl.ds(start, LANES)
        f = []
        for member in range(19):
            if member in MOVED:
                f.append(after[member, z, at, lanes])
                continue
            other = (z - LATTICE[member][2]) % planes
            f.append(before[member, other, at, lanes] if start < width_y else side[member, other, at, all_lanes])
        density, momenta = moments(f)
        if flat is not None:
            inverse = 1.0 / density
            for number, force in enumerate(force_at(force_0, planes, tall, z, row, lanes)):
                probe_0[pl.ds(pl.multiple_of(number * planes * width_x + flat, 8), 8), lanes] = (
                    momenta[number] + 0.5 * force
                ) * inverse
        values = collide(f, density, momenta, force_at(force_1, planes, tall, z, row, lanes))
        for member in kept:
            after[member, z, at, lanes] = values[member]

    copies = []
    for z in range(planes):

        @pl.loop(0, width_x // 8)
        def _(index):
            row = pl.multiple_of(index * 8, 8)
            for start in range(0, width_y, LANES):
                second_block(z, row, start, pl.multiple_of(z * width_x + row, 8))
            second_block(z, row, width_y, kept=[i for i in range(19) if LATTICE[i][1]])

        for start in range(0, wide, LANES):
            second_block(z, width_x, start, kept=[i for i in range(19) if LATTICE[i][0]])
        for number, (first, count, along_x, along_y) in enumerate(RUNS):
            part = (pl.ds(first, count), z, pl.ds(0, tall if along_x else width_x), pl.ds(0, wide if along_y else width_y))
            copies.append(pltpu.make_async_copy(after.at[part], after_hbm.at[part], sems.at[len(RUNS) * z + number]))
            copies[-1].start()

    def sample_step(step, own_ref, probe_ref):
        for number, row in enumerate(sample(own_ref[...], planes, width_x, width_y, probe_ref)):
            rows[steps * number + step : steps * number + step + 1, :] = row

    sample_step(0, own_0, probe_0)
    for z in range(planes):

        def streamed(along_x, along_y, weight):
            total = None
            rows_used = tall if along_x else width_x
            lanes_used = wide if along_y else width_y
            for member in range(19):
                if LATTICE[member][:2] != (along_x, along_y) or weight(LATTICE[member][2]) == 0:
                    continue
                value = after[member, (z - LATTICE[member][2]) % planes, 0:rows_used, 0:lanes_used]
                value = value if weight(LATTICE[member][2]) > 0 else -value
                total = value if total is None else total + value
            if along_x:
                total = pltpu.roll(total, along_x % rows_used, 0)
            if along_y:
                total = pltpu.roll(total, along_y % lanes_used, 1)
            return total[0:width_x, 0:width_y]

        here = {(x, y): streamed(x, y, lambda cz: 1) for x in (-1, 0, 1) for y in (-1, 0, 1)}
        density = sum(here.values())
        momenta = [
            sum(here[1, y] - here[-1, y] for y in (-1, 0, 1)),
            sum(here[x, 1] - here[x, -1] for x in (-1, 0, 1)),
            sum(streamed(x, y, lambda cz: cz) for x, y in ((0, 0), (1, 0), (-1, 0), (0, 1), (0, -1))),
        ]
        inverse = 1.0 / density
        for number in range(3):
            at, to = (number * planes + z) * tall, (number * planes + z) * width_x
            probe_1[to : to + width_x, :] = (
                momenta[number] + 0.5 * force_1[at : at + width_x, 0:width_y]
            ) * inverse

    sample_step(1, own_1, probe_1)
    send_back(cap, rows, back_ref)
    for copy in copies:
        copy.wait()


def store_kernel(after_hbm, out_hbm, after, out_ref, sems, out_sems):
    planes, width_x, width_y = out_ref.shape[1], out_ref.shape[2], out_ref.shape[3]
    tall, wide = after.shape[2], after.shape[3]
    parts = [
        (pl.ds(first, count), slice(None), pl.ds(0, tall if along_x else width_x), pl.ds(0, wide if along_y else width_y))
        for first, count, along_x, along_y in RUNS
    ]
    arriving = fetch([(after_hbm.at[part], after.at[part]) for part in parts], sems)
    copies = []
    for copy, (first, count, along_x, along_y) in zip(arriving, RUNS):
        copy.wait()
        for member in range(first, first + count):
            for z in range(planes):
                block = after[member, z, 0 : tall if along_x else width_x, 0 : wide if along_y else width_y]
                out_ref[member, (z + LATTICE[member][2]) % planes] = shifted(block, member)[0:width_x, 0:width_y]
            copies.append(pltpu.make_async_copy(out_ref.at[member], out_hbm.at[member], out_sems.at[member]))
            copies[-1].start()
    for copy in copies:
        copy.wait()


def send_back(cap, rows, out_ref):
    devices, steps = out_ref.shape[0], out_ref.shape[1]
    per = LANES // cap
    group = iota((steps, LANES), 1) // cap
    for device in range(devices):
        line, place = device // per, device % per
        total = jnp.zeros((steps, LANES), F32)
        for number in range(3):
            piece = rows[number * steps : (number + 1) * steps, line * LANES : (line + 1) * LANES]
            shift = (number - place) * cap % LANES
            if shift:
                piece = pltpu.roll(piece, shift, 1)
            total = jnp.where(group == number, piece, total)
        out_ref[device] = total


def call(kernel, outs, scratch=(), flops=0, moved=0, limit=24, fetched=(False,), stored=None):
    shapes = [jax.ShapeDtypeStruct(shape, kind) for shape, kind in outs]
    out_specs = [pl.BlockSpec(memory_space=pltpu.SMEM if len(shape) == 1 else pltpu.VMEM) for shape, _ in outs]
    if stored:
        shapes = [pltpu.HBM(*out) if own else shape for out, shape, own in zip(outs, shapes, stored)]
        out_specs = [pl.BlockSpec(memory_space=pltpu.HBM if own else pltpu.VMEM) for own in stored]
    places = {True: pltpu.HBM, False: pltpu.VMEM, None: pltpu.SMEM}
    specs = [pl.BlockSpec(memory_space=places[own]) for own in fetched]
    made = pl.pallas_call(
        kernel,
        out_shape=shapes,
        out_specs=out_specs,
        scratch_shapes=list(scratch),
        **({"in_specs": specs} if fetched != (False,) else {}),
        cost_estimate=pl.CostEstimate(flops=flops, bytes_accessed=moved, transcendentals=0),
        compiler_params=pltpu.CompilerParams(vmem_limit_bytes=limit * 1024 * 1024),
    )
    if not any(fetched):
        return made
    return lambda *args: made(
        *[pltpu.with_memory_space_constraint(x, pltpu.HBM) if own else x for x, own in zip(args, fetched)]
    )


def pair(up, down, axis):
    count = lax.axis_size(axis)
    forward = [(i, (i + 1) % count) for i in range(count)]
    backward = [(target, source) for source, target in forward]
    return lax.ppermute(up, axis, forward), lax.ppermute(down, axis, backward)


def run(rounds, populations_in, marker_force, marker_frac, marker_cell, marker_tile):
    count_gx, count_gy = lax.axis_size("gx"), lax.axis_size("gy")
    devices = count_gx * count_gy
    steps, owned = marker_force.shape[0], marker_force.shape[2]
    cap = max(2, 2 * owned // devices)
    half, slots = cap // 2, devices * cap
    planes, width_x, width_y = populations_in.shape[1:]
    tall, wide = width_x + RING, width_y + SIDE
    grid = (count_gx, count_gy, width_x, width_y)
    by_comp = lambda x: jnp.transpose(x, (1, 0, 2))
    markers = (
        marker_tile.reshape(steps * owned // LANES, LANES),
        by_comp(marker_cell),
        by_comp(marker_frac),
        by_comp(marker_force),
    )
    message = ((devices, 8, LANES), F32)
    rows = pltpu.VMEM((16, owned), F32)

    def send(outgoing):
        return lax.all_to_all(outgoing, ("gx", "gy"), split_axis=0, concat_axis=0, tiled=True)

    def pack_markers(*refs):
        pack_kernel(grid, steps, cap, *refs)

    face = (((19 + len(X_UP) + 4) * planes, width_y), F32)
    packed = -(-2 * 19 * planes // LANES) * LANES
    outgoing, slot = call(
        pack_markers,
        [message, ((steps, owned), jnp.int32)],
        [
            rows,
            pltpu.VMEM((steps * owned // LANES, LANES), jnp.int32),
            pltpu.VMEM((3, steps, owned), jnp.int32),
            pltpu.VMEM((3, steps, owned), F32),
            pltpu.VMEM((3, steps, owned), F32),
            pltpu.SemaphoreType.DMA((4,)),
        ],
        fetched=(True,) * 4,
    )(*markers)
    x_up, x_down = call(
        strips_kernel,
        [face, face],
        [
            pltpu.VMEM((19, planes, 8, width_y), F32),
            pltpu.VMEM((19, planes, 8, width_y), F32),
            pltpu.SemaphoreType.DMA((2,)),
        ],
        fetched=(True, False),
    )(populations_in, slot)
    y_up, y_down = call(
        columns_kernel,
        [((width_x, packed), F32)] * 2,
        [
            pltpu.VMEM((19, planes, width_x, LANES), F32),
            pltpu.VMEM((19, planes, width_x, LANES), F32),
            pltpu.SemaphoreType.DMA((2,)),
        ],
        fetched=(True, False),
    )(populations_in, x_up)
    arrived = send(outgoing)

    x_low, x_high = pair(x_up, x_down, "gx")
    field = ((3 * planes * tall, wide), F32)

    def spread_markers(*refs):
        spread_kernel(cap, steps, planes, width_x, width_y, *refs)

    force_0, force_1, own_0, own_1, turns = call(
        spread_markers, [field] * steps + [((8, slots), F32)] * steps + [((1,), jnp.int32)]
    )(arrived)
    turns = turns.reshape(())

    y_up, y_down = call(corner_kernel, [((width_x + 8, packed), F32)] * 2)(y_up, y_down, x_low, x_high, own_0, own_1)
    y_low, y_high = pair(y_up, y_down, "gy")

    def again(state):
        return state[0] < turns

    def more(state):
        turn, *forces = state

        def turn_markers(*refs):
            turn_kernel(grid, steps, cap, *refs)

        def add_markers(*refs):
            more_kernel(cap, steps, planes, width_x, width_y, *refs)

        spec = [pl.BlockSpec(memory_space=pltpu.SMEM)] + [pl.BlockSpec(memory_space=pltpu.VMEM)] * 4
        (outgoing,) = pl.pallas_call(
            turn_markers,
            out_shape=[jax.ShapeDtypeStruct(*message)],
            in_specs=spec,
            scratch_shapes=[rows],
            compiler_params=pltpu.CompilerParams(vmem_limit_bytes=24 * 1024 * 1024),
        )(turn.reshape(1), *markers)
        return (turn + 1, *call(add_markers, [field] * steps)(send(outgoing), *forces))

    if rounds:
        _, force_0, force_1 = lax.while_loop(again, more, (jnp.int32(1), force_0, force_1))

    (before,) = call(
        first_kernel,
        [((19, planes, tall, width_y), F32)],
        [pltpu.VMEM((4, planes, RING, width_y), F32), pltpu.SemaphoreType.DMA((planes,))],
        fetched=(True,) + (False,) * 3,
    )(populations_in, x_low, x_high, force_0)

    def main(*refs):
        main_kernel(cap, steps, *refs)

    own_field = pltpu.VMEM((3 * planes * width_x, width_y), F32)
    after, back = call(
        main,
        [((19, planes, tall, wide), F32), ((devices, steps, LANES), F32)],
        [
            pltpu.VMEM((19, planes, tall, LANES), F32),
            pltpu.VMEM((19, planes, tall, wide), F32),
            pltpu.VMEM((4, planes, RING, LANES), F32),
            own_field,
            own_field,
            pltpu.VMEM((8, slots), F32),
            pltpu.SemaphoreType.DMA((len(RUNS) * planes,)),
        ],
        stored=(True, False),
    )(before, y_low, y_high, force_0, force_1, own_0, own_1)
    (fields,) = call(
        store_kernel,
        [(populations_in.shape, F32)],
        [
            pltpu.VMEM((19, planes, tall, wide), F32),
            pltpu.VMEM(populations_in.shape, F32),
            pltpu.SemaphoreType.DMA((len(RUNS),)),
            pltpu.SemaphoreType.DMA((19,)),
        ],
        fetched=(True,),
        stored=(True,),
    )(after)
    returned = send(back)

    def unpack(*refs):
        unpack_kernel(cap, steps, *refs)

    (velocity,) = call(unpack, [((3, steps, owned), F32)])(returned, slot)
    return fields, by_comp(velocity), turns


def local(*inputs):
    def again(state):
        return state[2] > 1

    def whole(state):
        fields, velocity, _ = run(True, *inputs)
        return fields, velocity, jnp.int32(0)

    fields, velocity, _ = lax.while_loop(again, whole, run(False, *inputs))
    return fields, velocity


def solution(mesh):
    return jax.shard_map(
        local,
        mesh=mesh,
        in_specs=(
            P(None, None, "gx", "gy"),
            P(None, None, ("gx", "gy")),
            P(None, None, ("gx", "gy")),
            P(None, None, ("gx", "gy")),
            P(None, ("gx", "gy"), None),
        ),
        out_specs=(P(None, None, "gx", "gy"), P(None, None, ("gx", "gy"))),
        check_vma=False,
    )
```
